32 devices in a mesh: row: 8 (over y, x, core), col: 4 (over z).
Axes of the slice: x: 2, y: 2, z: 4, core: 2. Of those that a mesh axis runs over, the one named last changes fastest.
Arguments:
- kernel: bfloat16 [16, 8, 16, 4, 8192], P(None, 'row', None, 'col'), as said below
Outputs:
- factor: float32 [16, 8, 16, 4, 8192], P(None, 'row', None, 'col')
Inputs may be any that keep to these rules, and one draw needn't show every extreme that they name: kernel holds a symmetric positive definite matrix.
All inputs are finite; a program needn't handle non-finite values.
Results may differ from the reference program's by a relative error of at most 0.0046.
Values may be sent and summed in bfloat16 or wider, within the bound.
No kernel may reach another device: no remote copies, remote signals or barrier semaphores. Data moves between devices by JAX's collectives and lax.ppermute only.
A program may use at most 64 MiB of HBM per device.

```python
import math
import jax
import jax.numpy as jnp
from jax import lax

P_SIZE = 512
NT = 16
BR = 64
BC = 128
TILE = 8192
M = 8192
N_ROW = 8
N_COL = 4


SQRT_FIVE = 2.2360679775


def draw_kernel(key, part):
    matrix_order = NT * P_SIZE
    coord_key, weight_key, nugget_key = jax.random.split(key, 3)
    weights = jax.random.randint(weight_key, (8,), 1, 5).astype(jnp.float32)
    coords = jax.random.randint(coord_key, (matrix_order, 8), 0, 16).astype(jnp.float32)
    length = 16.0
    nugget_low = 0.05
    nugget_high = 0.2
    fraction = jax.random.uniform(nugget_key, (matrix_order,), jnp.float32, 0.0, 1.0)
    nugget = nugget_low * jnp.exp(fraction * math.log(nugget_high / nugget_low))
    diagonal_values = 1.0 + nugget
    positions = jnp.arange(matrix_order)

    def one_block(start_at):
        block_coords = lax.dynamic_slice_in_dim(coords, start_at, P_SIZE, 0)
        squared = jnp.zeros((P_SIZE, matrix_order), jnp.float32)
        for dim_at in range(8):
            gap_value = block_coords[:, dim_at][:, None] - coords[:, dim_at][None, :]
            squared = squared + weights[dim_at] * gap_value * gap_value
        scaled = jnp.sqrt(squared) * (SQRT_FIVE / length)
        values = (1.0 + scaled + scaled * scaled / 3.0) * jnp.exp(-scaled)
        on_diagonal = (start_at + jnp.arange(P_SIZE))[:, None] == positions[None, :]
        return jnp.where(on_diagonal, diagonal_values[None, :], values)
    blocks = lax.map(one_block, jnp.arange(NT) * P_SIZE)
    symmetric = blocks.reshape(matrix_order, matrix_order)
    tiled = symmetric.reshape(NT, N_ROW, BR, NT, N_COL, BC)
    return tiled.transpose(0, 1, 3, 4, 2, 5).reshape(NT, N_ROW, NT, N_COL, TILE).astype(jnp.bfloat16)


def setup_inputs(seed: int = 0) -> dict:
    key_list = jax.random.split(jax.random.key(seed), 2)
    kernel = draw_kernel(jax.random.fold_in(key_list[1], 71), 0)
    return dict(kernel=kernel)


def to_matrix(kernel):
    tiled = kernel.reshape(NT, N_ROW, NT, N_COL, BR, BC)
    return tiled.transpose(0, 1, 4, 2, 3, 5).reshape(M, M)

def to_tiles(matrix):
    tiled = matrix.reshape(NT, N_ROW, BR, NT, N_COL, BC)
    return tiled.transpose(0, 1, 3, 4, 2, 5).reshape(NT, N_ROW, NT, N_COL, TILE)

def reference(kernel):
    updated = to_matrix(kernel).astype(jnp.float32)
    result = jnp.zeros((M, M), jnp.float32)
    for panel_at in range(2):
        begin_at = panel_at * P_SIZE
        end_at = begin_at + P_SIZE
        corner_block = updated[begin_at:end_at, begin_at:end_at]
        corner_factor = jnp.linalg.cholesky(0.5 * (corner_block + corner_block.T))
        below_rows = updated[end_at:, begin_at:end_at]
        solved = jax.scipy.linalg.solve_triangular(corner_factor, below_rows.T, lower=True).T
        rounded = solved.astype(jnp.bfloat16)
        update_term = jnp.dot(rounded.astype(jnp.float32), rounded.T.astype(jnp.float32), preferred_element_type=jnp.float32)
        updated = updated.at[end_at:, end_at:].add(-update_term)
        result = result.at[begin_at:end_at, begin_at:end_at].set(corner_factor)
        result = result.at[end_at:, begin_at:end_at].set(solved)
    result = result.at[2 * P_SIZE:, 2 * P_SIZE:].set(updated[2 * P_SIZE:, 2 * P_SIZE:])
    return to_tiles(result)
```

```python
import jax
import jax.numpy as jnp
from jax import lax
from jax.experimental import pallas as pl
from jax.experimental.pallas import tpu as pltpu
from jax.sharding import PartitionSpec as P

P_SIZE = 512
NT = 16
STEP = 16
BLOCK = 128
EXACT = lax.Precision.HIGHEST


def exact_dot(left_side, right_side, contract=((1,), (0,))):
    return lax.dot_general(
        left_side,
        right_side,
        (contract, ((), ())),
        preferred_element_type=jnp.float32,
        precision=EXACT,
    )


def fast_dot(left_side, right_side, contract=((1,), (0,))):
    return lax.dot_general(
        left_side, right_side, (contract, ((), ())), preferred_element_type=jnp.float32
    )


def factor_block(work, done):
    row_id = lax.broadcasted_iota(jnp.int32, (STEP, BLOCK), 0)
    for start in range(0, BLOCK, STEP):
        here = slice(start, start + STEP)
        halves = [work[here, 0:BLOCK], work[here, BLOCK : 2 * BLOCK]]
        columns = [
            jnp.broadcast_to(halves[0][:, start + j : start + j + 1], (STEP, BLOCK))
            for j in range(STEP)
        ]
        raw = work[start + STEP :, here] if start + STEP < BLOCK else None
        kept = [jnp.zeros((STEP, BLOCK), jnp.float32)] * 2
        pivots = jnp.ones((STEP, BLOCK), jnp.float32)
        for k in range(STEP):
            pivot = jnp.broadcast_to(columns[k][k : k + 1, :], (STEP, BLOCK))
            factors = jnp.where(row_id == k, 0.0, columns[k] * (1.0 / pivot))
            for j in range(k + 1, STEP):
                top = jnp.broadcast_to(columns[j][k : k + 1, :], (STEP, BLOCK))
                columns[j] = columns[j] - factors * top
            pivots = jnp.where(row_id == k, pivot, pivots)
            for h in range(2):
                top = jnp.broadcast_to(halves[h][k : k + 1, :], (STEP, BLOCK))
                kept[h] = jnp.where(row_id == k, top, kept[h])
                halves[h] = halves[h] - factors * top
        scale = lax.rsqrt(pivots)
        inverse = 1.0 / pivots
        for h in range(2):
            done[here, h * BLOCK : (h + 1) * BLOCK] = kept[h] * scale
        if raw is not None:
            solved = jnp.concatenate([halves[0] * inverse, halves[1] * inverse], axis=1)
            work[start + STEP :, :] = work[start + STEP :, :] - exact_dot(raw, solved)


def factor_kernel(given, factor, inverse, rest, work, done):
    order = given.shape[0]
    rest[...] = given[...]
    inverse[...] = jnp.zeros_like(inverse)
    factor[...] = jnp.zeros_like(factor)
    row_id = lax.broadcasted_iota(jnp.int32, (BLOCK, BLOCK), 0)
    column_id = lax.broadcasted_iota(jnp.int32, (BLOCK, BLOCK), 1)
    for start in range(0, order, BLOCK):
        here = slice(start, start + BLOCK)
        work[:, 0:BLOCK] = rest[here, here]
        work[:, BLOCK:] = (row_id == column_id).astype(jnp.float32)
        factor_block(work, done)
        factor[here, here] = jnp.where(column_id >= row_id, done[:, 0:BLOCK], 0.0).T
        block_inverse = done[:, BLOCK:]
        if start:
            inverse[here, 0:start] = exact_dot(block_inverse, inverse[here, 0:start])
        inverse[here, here] = block_inverse
        if start + BLOCK < order:
            after = slice(start + BLOCK, order)
            upper = exact_dot(block_inverse, rest[here, after])
            lower = upper.T
            factor[after, here] = lower
            rest[after, after] = rest[after, after] - exact_dot(lower, upper)
            so_far = slice(0, start + BLOCK)
            inverse[after, so_far] = inverse[after, so_far] - exact_dot(
                lower, inverse[here, so_far]
            )


def factor_corner(corner):
    order = corner.shape[0]
    square = jax.ShapeDtypeStruct((order, order), jnp.float32)
    return pl.pallas_call(
        factor_kernel,
        out_shape=[square, square],
        scratch_shapes=[
            pltpu.VMEM((order, order), jnp.float32),
            pltpu.VMEM((BLOCK, 2 * BLOCK), jnp.float32),
            pltpu.VMEM((BLOCK, 2 * BLOCK), jnp.float32),
        ],
        compiler_params=pltpu.CompilerParams(vmem_limit_bytes=32 * 2**20),
    )(corner)


def spread(value, axis, offsets):
    count = lax.axis_size(axis)
    parts = [value]
    for offset in offsets[1:]:
        parts.append(lax.ppermute(value, axis, [(i, i ^ offset) for i in range(count)]))
    return jnp.stack(parts)


def gather_corner(mine):
    row_count = lax.axis_size("row")
    col_count = lax.axis_size("col")
    row_index = lax.axis_index("row")
    column_index = lax.axis_index("col")
    over_cols = spread(mine, "col", list(range(col_count)))
    over_chips = spread(over_cols, "row", list(range(0, row_count, 2)))
    slots = spread(over_chips, "row", [0, 1])
    slots = slots.transpose(1, 0, 2, 3, 4, 5).reshape(row_count, col_count, *mine.shape)
    slots = jnp.take(slots, jnp.arange(row_count) ^ row_index, axis=0, mode="clip")
    slots = jnp.take(slots, jnp.arange(col_count) ^ column_index, axis=1, mode="clip")
    return slots.transpose(2, 0, 3, 1, 4).reshape(3, P_SIZE, P_SIZE)


def per_device(kernel):
    row_count = lax.axis_size("row")
    col_count = lax.axis_size("col")
    tile_rows = P_SIZE // row_count
    tile_cols = P_SIZE // col_count
    row_index = lax.axis_index("row")
    column_index = lax.axis_index("col")
    tiles = kernel.reshape(NT, NT, tile_rows, tile_cols)
    corner = gather_corner(jnp.stack([tiles[0, 0], tiles[1, 0], tiles[1, 1]]))
    own_rows = tiles[:, 0:2].transpose(0, 2, 1, 3).reshape(NT * tile_rows, 2 * tile_cols)
    own_rows = lax.all_gather(own_rows, "col", axis=0, tiled=False)
    own_rows = own_rows.reshape(col_count, NT * tile_rows, 2, tile_cols).transpose(1, 2, 0, 3)
    own_rows = own_rows.reshape(NT * tile_rows, 2, P_SIZE)
    own_cols = tiles[0:2].transpose(0, 2, 1, 3).reshape(2 * tile_rows, NT * tile_cols)
    own_cols = lax.all_gather(own_cols, "row", axis=0, tiled=False)
    own_cols = own_cols.reshape(row_count, 2, tile_rows, NT * tile_cols).transpose(1, 0, 2, 3)
    own_cols = own_cols.reshape(2, P_SIZE, NT * tile_cols)

    first_corner, cross_corner, second_corner = (corner[i].astype(jnp.float32) for i in range(3))
    first_factor, first_inverse = factor_corner(0.5 * (first_corner + first_corner.T))
    cross = exact_dot(cross_corner, first_inverse, ((1,), (1,))).astype(jnp.bfloat16)
    updated_corner = second_corner - fast_dot(cross, cross, ((1,), (1,)))
    second_factor, second_inverse = factor_corner(0.5 * (updated_corner + updated_corner.T))

    first_rows = exact_dot(
        own_rows[tile_rows:, 0].astype(jnp.float32), first_inverse, ((1,), (1,))
    )
    first_cols = exact_dot(first_inverse, own_cols[0, :, tile_cols:].astype(jnp.float32))
    first_rows_rounded = first_rows.astype(jnp.bfloat16)
    first_cols_rounded = first_cols.astype(jnp.bfloat16)
    second_rows = own_rows[2 * tile_rows :, 1].astype(jnp.float32) - fast_dot(
        first_rows_rounded[tile_rows:], cross, ((1,), (1,))
    )
    second_cols = own_cols[1, :, 2 * tile_cols :].astype(jnp.float32) - fast_dot(
        cross, first_cols_rounded[:, tile_cols:]
    )
    second_rows = exact_dot(second_rows, second_inverse, ((1,), (1,)))
    second_cols = exact_dot(second_inverse, second_cols)
    left_side = jnp.concatenate(
        [first_rows_rounded[tile_rows:], second_rows.astype(jnp.bfloat16)], axis=1
    )
    right_side = jnp.concatenate(
        [first_cols_rounded[:, tile_cols:], second_cols.astype(jnp.bfloat16)], axis=0
    )
    inner = NT - 2
    product = fast_dot(left_side, right_side).reshape(inner, tile_rows, inner, tile_cols)
    trailing = tiles[2:, 2:].astype(jnp.float32) - product.transpose(0, 2, 1, 3)
    own = (row_index * tile_rows, column_index * tile_cols)
    first_own = lax.dynamic_slice_in_dim(first_rows, own[1], tile_cols, 1)
    second_own = lax.dynamic_slice_in_dim(second_rows, own[1], tile_cols, 1)
    first_tile = lax.dynamic_slice(first_factor, own, (tile_rows, tile_cols))
    second_tile = lax.dynamic_slice(second_factor, own, (tile_rows, tile_cols))
    result = jnp.zeros(tiles.shape, jnp.float32)
    result = result.at[2:, 2:].set(trailing)
    result = result.at[0, 0].set(first_tile)
    result = result.at[1:, 0].set(first_own.reshape(NT - 1, tile_rows, tile_cols))
    result = result.at[1, 1].set(second_tile)
    result = result.at[2:, 1].set(second_own.reshape(NT - 2, tile_rows, tile_cols))
    return result.reshape(kernel.shape)


def solution(mesh):
    placed = P(None, "row", None, "col", None)
    return jax.shard_map(
        per_device, mesh=mesh, in_specs=(placed,), out_specs=placed, check_vma=False
    )
```

```python
import functools

import jax
import jax.numpy as jnp
from jax import lax
from jax.experimental import pallas as pl
from jax.experimental.pallas import tpu as pltpu
from jax.sharding import PartitionSpec as P

P_SIZE = 512
NT = 16
STEP = 16
BLOCK = 128
EXACT = lax.Precision.HIGHEST


def exact_dot(left_side, right_side, contract=((1,), (0,))):
    return lax.dot_general(
        left_side,
        right_side,
        (contract, ((), ())),
        preferred_element_type=jnp.float32,
        precision=EXACT,
    )


def fast_dot(left_side, right_side, contract=((1,), (0,))):
    return lax.dot_general(
        left_side, right_side, (contract, ((), ())), preferred_element_type=jnp.float32
    )


def factor_block(work, done):
    row_id = lax.broadcasted_iota(jnp.int32, (STEP, BLOCK), 0)
    for start in range(0, BLOCK, STEP):
        here = slice(start, start + STEP)
        halves = [work[here, 0:BLOCK], work[here, BLOCK : 2 * BLOCK]]
        columns = [
            jnp.broadcast_to(halves[0][:, start + j : start + j + 1], (STEP, BLOCK))
            for j in range(STEP)
        ]
        raw = work[start + STEP :, here] if start + STEP < BLOCK else None
        kept = [jnp.zeros((STEP, BLOCK), jnp.float32)] * 2
        pivots = jnp.ones((STEP, BLOCK), jnp.float32)
        for k in range(STEP):
            pivot = jnp.broadcast_to(columns[k][k : k + 1, :], (STEP, BLOCK))
            factors = jnp.where(row_id == k, 0.0, columns[k] * (1.0 / pivot))
            for j in range(k + 1, STEP):
                top = jnp.broadcast_to(columns[j][k : k + 1, :], (STEP, BLOCK))
                columns[j] = columns[j] - factors * top
            pivots = jnp.where(row_id == k, pivot, pivots)
            for h in range(2):
                top = jnp.broadcast_to(halves[h][k : k + 1, :], (STEP, BLOCK))
                kept[h] = jnp.where(row_id == k, top, kept[h])
                halves[h] = halves[h] - factors * top
        scale = lax.rsqrt(pivots)
        inverse = 1.0 / pivots
        for h in range(2):
            done[here, h * BLOCK : (h + 1) * BLOCK] = kept[h] * scale
        if raw is not None:
            solved = jnp.concatenate([halves[0] * inverse, halves[1] * inverse], axis=1)
            work[start + STEP :, :] = work[start + STEP :, :] - exact_dot(raw, solved)


def factor_kernel(given, factor, inverse, rest, work, done):
    rest[...] = given[...]
    factor_rest(rest, factor, inverse, work, done)


def factor_rest(rest, factor, inverse, work, done):
    order = rest.shape[0]
    inverse[...] = jnp.zeros_like(inverse)
    factor[...] = jnp.zeros_like(factor)
    row_id = lax.broadcasted_iota(jnp.int32, (BLOCK, BLOCK), 0)
    column_id = lax.broadcasted_iota(jnp.int32, (BLOCK, BLOCK), 1)
    for start in range(0, order, BLOCK):
        here = slice(start, start + BLOCK)
        work[:, 0:BLOCK] = rest[here, here]
        work[:, BLOCK:] = (row_id == column_id).astype(jnp.float32)
        factor_block(work, done)
        factor[here, here] = jnp.where(column_id >= row_id, done[:, 0:BLOCK], 0.0).T
        block_inverse = done[:, BLOCK:]
        if start:
            inverse[here, 0:start] = exact_dot(block_inverse, inverse[here, 0:start])
        inverse[here, here] = block_inverse
        if start + BLOCK < order:
            after = slice(start + BLOCK, order)
            upper = exact_dot(block_inverse, rest[here, after])
            lower = upper.T
            factor[after, here] = lower
            rest[after, after] = rest[after, after] - exact_dot(lower, upper)
            so_far = slice(0, start + BLOCK)
            inverse[after, so_far] = inverse[after, so_far] - exact_dot(
                lower, inverse[here, so_far]
            )


def factor_scratch():
    return [
        pltpu.VMEM((P_SIZE, P_SIZE), jnp.float32),
        pltpu.VMEM((BLOCK, 2 * BLOCK), jnp.float32),
        pltpu.VMEM((BLOCK, 2 * BLOCK), jnp.float32),
    ]


def factor_corner(corner):
    order = corner.shape[0]
    square = jax.ShapeDtypeStruct((order, order), jnp.float32)
    return pl.pallas_call(
        factor_kernel,
        out_shape=[square, square],
        scratch_shapes=factor_scratch(),
        compiler_params=pltpu.CompilerParams(vmem_limit_bytes=32 * 2**20),
    )(corner)


def spread(value, axis, offsets):
    count = lax.axis_size(axis)
    parts = [value]
    for offset in offsets[1:]:
        parts.append(lax.ppermute(value, axis, [(i, i ^ offset) for i in range(count)]))
    return jnp.stack(parts)


def gather_corner(mine):
    row_count = lax.axis_size("row")
    col_count = lax.axis_size("col")
    row_index = lax.axis_index("row")
    column_index = lax.axis_index("col")
    over_cols = spread(mine, "col", list(range(col_count)))
    over_chips = spread(over_cols, "row", list(range(0, row_count, 2)))
    slots = spread(over_chips, "row", [0, 1])
    slots = slots.transpose(1, 0, 2, 3, 4, 5).reshape(row_count, col_count, *mine.shape)
    slots = jnp.take(slots, jnp.arange(row_count) ^ row_index, axis=0, mode="clip")
    slots = jnp.take(slots, jnp.arange(col_count) ^ column_index, axis=1, mode="clip")
    return slots.transpose(2, 0, 3, 1, 4).reshape(3, P_SIZE, P_SIZE)


def per_device_general(kernel):
    row_count = lax.axis_size("row")
    col_count = lax.axis_size("col")
    tile_rows = P_SIZE // row_count
    tile_cols = P_SIZE // col_count
    row_index = lax.axis_index("row")
    column_index = lax.axis_index("col")
    tiles = kernel.reshape(NT, NT, tile_rows, tile_cols)
    corner = gather_corner(jnp.stack([tiles[0, 0], tiles[1, 0], tiles[1, 1]]))
    own_rows = tiles[:, 0:2].transpose(0, 2, 1, 3).reshape(NT * tile_rows, 2 * tile_cols)
    own_rows = lax.all_gather(own_rows, "col", axis=0, tiled=False)
    own_rows = own_rows.reshape(col_count, NT * tile_rows, 2, tile_cols).transpose(1, 2, 0, 3)
    own_rows = own_rows.reshape(NT * tile_rows, 2, P_SIZE)
    own_cols = tiles[0:2].transpose(0, 2, 1, 3).reshape(2 * tile_rows, NT * tile_cols)
    own_cols = lax.all_gather(own_cols, "row", axis=0, tiled=False)
    own_cols = own_cols.reshape(row_count, 2, tile_rows, NT * tile_cols).transpose(1, 0, 2, 3)
    own_cols = own_cols.reshape(2, P_SIZE, NT * tile_cols)

    first_corner, cross_corner, second_corner = (corner[i].astype(jnp.float32) for i in range(3))
    first_factor, first_inverse = factor_corner(0.5 * (first_corner + first_corner.T))
    cross = exact_dot(cross_corner, first_inverse, ((1,), (1,))).astype(jnp.bfloat16)
    updated_corner = second_corner - fast_dot(cross, cross, ((1,), (1,)))
    second_factor, second_inverse = factor_corner(0.5 * (updated_corner + updated_corner.T))

    first_rows = exact_dot(
        own_rows[tile_rows:, 0].astype(jnp.float32), first_inverse, ((1,), (1,))
    )
    first_cols = exact_dot(first_inverse, own_cols[0, :, tile_cols:].astype(jnp.float32))
    first_rows_rounded = first_rows.astype(jnp.bfloat16)
    first_cols_rounded = first_cols.astype(jnp.bfloat16)
    second_rows = own_rows[2 * tile_rows :, 1].astype(jnp.float32) - fast_dot(
        first_rows_rounded[tile_rows:], cross, ((1,), (1,))
    )
    second_cols = own_cols[1, :, 2 * tile_cols :].astype(jnp.float32) - fast_dot(
        cross, first_cols_rounded[:, tile_cols:]
    )
    second_rows = exact_dot(second_rows, second_inverse, ((1,), (1,)))
    second_cols = exact_dot(second_inverse, second_cols)
    left_side = jnp.concatenate(
        [first_rows_rounded[tile_rows:], second_rows.astype(jnp.bfloat16)], axis=1
    )
    right_side = jnp.concatenate(
        [first_cols_rounded[:, tile_cols:], second_cols.astype(jnp.bfloat16)], axis=0
    )
    inner = NT - 2
    product = fast_dot(left_side, right_side).reshape(inner, tile_rows, inner, tile_cols)
    trailing = tiles[2:, 2:].astype(jnp.float32) - product.transpose(0, 2, 1, 3)
    own = (row_index * tile_rows, column_index * tile_cols)
    first_own = lax.dynamic_slice_in_dim(first_rows, own[1], tile_cols, 1)
    second_own = lax.dynamic_slice_in_dim(second_rows, own[1], tile_cols, 1)
    first_tile = lax.dynamic_slice(first_factor, own, (tile_rows, tile_cols))
    second_tile = lax.dynamic_slice(second_factor, own, (tile_rows, tile_cols))
    result = jnp.zeros(tiles.shape, jnp.float32)
    result = result.at[2:, 2:].set(trailing)
    result = result.at[0, 0].set(first_tile)
    result = result.at[1:, 0].set(first_own.reshape(NT - 1, tile_rows, tile_cols))
    result = result.at[1, 1].set(second_tile)
    result = result.at[2:, 1].set(second_own.reshape(NT - 2, tile_rows, tile_cols))
    return result.reshape(kernel.shape)


def whole(shape):
    return pl.BlockSpec(shape, lambda *_: (0,) * len(shape))


def natural_tile(tiles, spread_rows, tile_rows):
    for r in range(tile_rows):
        spread_rows[r * NT : (r + 1) * NT, :] = tiles[:, r * BLOCK : (r + 1) * BLOCK].astype(
            jnp.float32
        )


def top_kernel(tiles, corner, top, spread_rows):
    tile_rows = corner.shape[1]
    for t in range(2):
        natural_tile(tiles[t], spread_rows, tile_rows)
        for s in range(NT):
            tile = spread_rows[pl.ds(s, tile_rows, stride=NT), :].astype(jnp.bfloat16)
            top[t * tile_rows : (t + 1) * tile_rows, s * BLOCK : (s + 1) * BLOCK] = tile
            if s <= t:
                corner[t + s] = tile


def natural_kernel(tiles, natural, left, spread_rows):
    tile_rows = natural.shape[0]
    natural_tile(tiles[0], spread_rows, tile_rows)
    for s in range(NT):
        tile = spread_rows[pl.ds(s, tile_rows, stride=NT), :].astype(jnp.bfloat16)
        natural[:, s * BLOCK : (s + 1) * BLOCK] = tile
        if s < 2:
            left[:, s * BLOCK : (s + 1) * BLOCK] = tile


def take_top(tiles, tile_rows):
    return pl.pallas_call(
        top_kernel,
        grid=(1,),
        in_specs=[pl.BlockSpec((2, NT, tile_rows * BLOCK), lambda i: (0, 0, 0))],
        out_specs=[whole((3, tile_rows, BLOCK)), whole((2 * tile_rows, NT * BLOCK))],
        out_shape=[
            jax.ShapeDtypeStruct((3, tile_rows, BLOCK), jnp.bfloat16),
            jax.ShapeDtypeStruct((2 * tile_rows, NT * BLOCK), jnp.bfloat16),
        ],
        scratch_shapes=[pltpu.VMEM((tile_rows * NT, BLOCK), jnp.float32)],
        compiler_params=pltpu.CompilerParams(vmem_limit_bytes=16 * 2**20),
    )(tiles)


def take_natural(tiles, tile_rows):
    return pl.pallas_call(
        natural_kernel,
        grid=(NT,),
        in_specs=[pl.BlockSpec((1, NT, tile_rows * BLOCK), lambda t: (t, 0, 0))],
        out_specs=[
            pl.BlockSpec((tile_rows, NT * BLOCK), lambda t: (t, 0)),
            pl.BlockSpec((tile_rows, 2 * BLOCK), lambda t: (t, 0)),
        ],
        out_shape=[
            jax.ShapeDtypeStruct((NT * tile_rows, NT * BLOCK), jnp.bfloat16),
            jax.ShapeDtypeStruct((NT * tile_rows, 2 * BLOCK), jnp.bfloat16),
        ],
        scratch_shapes=[pltpu.VMEM((tile_rows * NT, BLOCK), jnp.float32)],
        compiler_params=pltpu.CompilerParams(vmem_limit_bytes=16 * 2**20),
        cost_estimate=pl.CostEstimate(
            flops=0, bytes_accessed=16 * NT * tile_rows * NT * BLOCK, transcendentals=0
        ),
    )(tiles)


def place_corner(place, slots, which, corner):
    row_index, column_index = place[0], place[1]
    chips, col_count, _, tile_rows, _ = slots[0].shape
    for core, held in enumerate(slots):
        for chip in range(chips):
            first_row = pl.multiple_of((row_index ^ (2 * chip + core)) * tile_rows, tile_rows)
            for col in range(col_count):
                first_col = pl.multiple_of((column_index ^ col) * BLOCK, BLOCK)
                corner[pl.ds(first_row, tile_rows), pl.ds(first_col, BLOCK)] = held[
                    chip, col, which
                ].astype(jnp.float32)


def first_kernel(place, near, far, factor, inverse, rest, work, done):
    place_corner(place, (near, far), 0, rest)
    factor_rest(rest, factor, inverse, work, done)


def second_kernel(
    place, near, far, first_inverse, factor, inverse, cross, rest, work, done
):
    place_corner(place, (near, far), 1, rest)
    solved = exact_dot(rest[...], first_inverse[...], ((1,), (1,))).astype(jnp.bfloat16)
    cross[...] = solved
    place_corner(place, (near, far), 2, rest)
    rest[...] = rest[...] - fast_dot(solved, solved, ((1,), (1,)))
    factor_rest(rest, factor, inverse, work, done)


def factor_call(body, place, slots, extra, extra_out):
    square = jax.ShapeDtypeStruct((P_SIZE, P_SIZE), jnp.float32)
    on_vmem = pl.BlockSpec(memory_space=pltpu.VMEM)
    return pl.pallas_call(
        body,
        in_specs=[pl.BlockSpec(memory_space=pltpu.SMEM)] + [on_vmem] * (2 + len(extra)),
        out_shape=[square, square] + extra_out,
        scratch_shapes=factor_scratch(),
        compiler_params=pltpu.CompilerParams(vmem_limit_bytes=32 * 2**20),
        cost_estimate=pl.CostEstimate(
            flops=20 * 10**9, bytes_accessed=4 * 2**20, transcendentals=0
        ),
    )(place, *slots, *extra)


def split(value):
    high = value.astype(jnp.bfloat16)
    return high, (value - high.astype(jnp.float32)).astype(jnp.bfloat16)


def tail_kernel(pieces, group, *refs):
    place, natural = refs[0], refs[1]
    lefts = refs[2 : 2 + pieces[0]]
    tops = refs[2 + pieces[0] : 2 + pieces[0] + pieces[1]]
    first_factor, first_inverse, second_factor, second_inverse, cross, result = refs[
        2 + sum(pieces) : 8 + sum(pieces)
    ]
    (
        given_cols,
        solved_cols,
        first_high,
        first_low,
        second_high,
        second_low,
        cross_mixed,
        solved_rows,
        copied,
    ) = refs[8 + sum(pieces) :]
    row_index, column_index = place[0], place[1]
    tile_rows = tops[0].shape[0] // 2
    own_row = pl.multiple_of(row_index * tile_rows, tile_rows)
    own_col = pl.multiple_of(column_index * BLOCK, BLOCK)
    order = P_SIZE
    at_group = pl.program_id(0)

    @pl.when(at_group == 0)
    def _():
        copies = []
        for offset, piece in enumerate(tops):
            first_row = pl.multiple_of((row_index ^ offset) * tile_rows, tile_rows)
            for t in range(2):
                copies.append(
                    pltpu.make_async_copy(
                        piece.at[pl.ds(t * tile_rows, tile_rows), :],
                        given_cols.at[pl.ds(t * order + first_row, tile_rows), :],
                        copied.at[2 * offset + t],
                    )
                )
                copies[-1].start()
        first_plain = split(first_inverse[...])
        second_plain = split(second_inverse[...])
        for offset in range(len(lefts)):
            first_col = pl.multiple_of((column_index ^ offset) * BLOCK, BLOCK)
            here = slice(offset * BLOCK, (offset + 1) * BLOCK)
            first_high[:, here], first_low[:, here] = split(
                first_inverse[:, pl.ds(first_col, BLOCK)]
            )
            second_high[:, here], second_low[:, here] = split(
                second_inverse[:, pl.ds(first_col, BLOCK)]
            )
            cross_mixed[here, :] = cross[pl.ds(first_col, BLOCK), :]
        for copy in copies:
            copy.wait()
        for begin in range(2 * BLOCK, NT * BLOCK, 2 * BLOCK):
            here = slice(begin, begin + 2 * BLOCK)
            given = given_cols[0:order, here]
            solved = fast_dot(first_plain[0], given) + fast_dot(first_plain[1], given)
            rounded = solved.astype(jnp.bfloat16)
            solved_cols[0:order, here] = rounded
            left_over = given_cols[order:, here].astype(jnp.float32) - fast_dot(
                cross[...], rounded
            )
            high, low = split(left_over)
            solved = (
                fast_dot(second_plain[0], high)
                + fast_dot(second_plain[0], low)
                + fast_dot(second_plain[1], high)
            )
            solved_cols[order:, here] = solved.astype(jnp.bfloat16)

    across = ((1,), (1,))
    given = jnp.concatenate([left[:, 0:BLOCK] for left in lefts], axis=1)
    solved = fast_dot(given, first_high[...], across) + fast_dot(given, first_low[...], across)
    solved_rows[:, 0:order] = solved
    rounded_first = solved.astype(jnp.bfloat16)
    given = jnp.concatenate([left[:, BLOCK : 2 * BLOCK] for left in lefts], axis=1)
    left_over = given.astype(jnp.float32) - fast_dot(rounded_first, cross_mixed[...], across)
    high, low = split(left_over)
    solved = (
        fast_dot(high, second_high[...], across)
        + fast_dot(low, second_high[...], across)
        + fast_dot(high, second_low[...], across)
    )
    solved_rows[:, order:] = solved
    rounded = jnp.concatenate([rounded_first, solved.astype(jnp.bfloat16)], axis=1)
    for begin in range(2 * BLOCK, NT * BLOCK, 2 * BLOCK):
        here = slice(begin, begin + 2 * BLOCK)
        kept = natural[:, here].astype(jnp.float32) - fast_dot(rounded, solved_cols[:, here])
        for s in (begin // BLOCK, begin // BLOCK + 1):
            for t in range(group):
                result[t, s] = kept[
                    t * tile_rows : (t + 1) * tile_rows,
                    s * BLOCK - begin : (s + 1) * BLOCK - begin,
                ]
    for t in range(group):
        rows = slice(t * tile_rows, (t + 1) * tile_rows)
        result[t, 0] = solved_rows[rows, pl.ds(own_col, BLOCK)]
        result[t, 1] = solved_rows[rows, pl.ds(order + own_col, BLOCK)]

    @pl.when(at_group == 0)
    def _():
        result[0, 0] = first_factor[pl.ds(own_row, tile_rows), pl.ds(own_col, BLOCK)]
        result[1, 1] = second_factor[pl.ds(own_row, tile_rows), pl.ds(own_col, BLOCK)]
        result[0, 1] = jnp.zeros((tile_rows, BLOCK), jnp.float32)
        for t in range(2):
            for s in range(2, NT):
                result[t, s] = jnp.zeros((tile_rows, BLOCK), jnp.float32)


def tail(place, natural, lefts, tops, factors, tile_rows):
    group = 4
    rows = group * tile_rows
    square = whole((P_SIZE, P_SIZE))
    half = pltpu.VMEM((P_SIZE, P_SIZE), jnp.bfloat16)
    return pl.pallas_call(
        functools.partial(tail_kernel, (len(lefts), len(tops)), group),
        grid=(NT // group,),
        in_specs=[
            pl.BlockSpec(memory_space=pltpu.SMEM),
            pl.BlockSpec((rows, NT * BLOCK), lambda i: (i, 0)),
            *[pl.BlockSpec((rows, 2 * BLOCK), lambda i: (i, 0)) for _ in lefts],
            *[pl.BlockSpec(memory_space=pl.ANY) for _ in tops],
            *[square] * 5,
        ],
        out_specs=pl.BlockSpec((group, NT, tile_rows, BLOCK), lambda i: (i, 0, 0, 0)),
        out_shape=jax.ShapeDtypeStruct((NT, NT, tile_rows, BLOCK), jnp.float32),
        scratch_shapes=[
            pltpu.VMEM((2 * P_SIZE, NT * BLOCK), jnp.bfloat16),
            pltpu.VMEM((2 * P_SIZE, NT * BLOCK), jnp.bfloat16),
            *[half] * 5,
            pltpu.VMEM((rows, 2 * P_SIZE), jnp.float32),
            pltpu.SemaphoreType.DMA((2 * len(tops),)),
        ],
        compiler_params=pltpu.CompilerParams(vmem_limit_bytes=56 * 2**20),
    )(place, natural, *lefts, *tops, *factors)


def swap(value, axis, offset):
    count = lax.axis_size(axis)
    return lax.ppermute(value, axis, [(i, i ^ offset) for i in range(count)])


def per_device(kernel):
    row_count = lax.axis_size("row")
    col_count = lax.axis_size("col")
    tile_rows = P_SIZE // row_count
    if P_SIZE != col_count * BLOCK or tile_rows % STEP:
        return per_device_general(kernel)
    place = jnp.stack([lax.axis_index("row"), lax.axis_index("col")]).astype(jnp.int32)
    tiles = kernel.reshape(NT, NT, tile_rows * BLOCK)
    corner, top = take_top(tiles, tile_rows)
    natural, left = take_natural(tiles, tile_rows)
    chips = range(2, row_count, 2)
    over_cols = jnp.stack([corner] + [swap(corner, "col", d) for d in range(1, col_count)])
    near = jnp.stack([over_cols] + [swap(over_cols, "row", d) for d in chips])
    far = swap(near, "row", 1)
    lefts = [left] + [swap(left, "col", d) for d in range(1, col_count)]
    even = [top] + [swap(top, "row", d) for d in chips]
    first_factor, first_inverse = factor_call(first_kernel, place, (near, far), (), [])
    odd = [swap(value, "row", 1) for value in even]
    half = jax.ShapeDtypeStruct((P_SIZE, P_SIZE), jnp.bfloat16)
    second_factor, second_inverse, cross = factor_call(
        second_kernel, place, (near, far), (first_inverse,), [half]
    )
    tops = [value for pair in zip(even, odd) for value in pair]
    factors = (first_factor, first_inverse, second_factor, second_inverse, cross)
    result = tail(place, natural, lefts, tops, factors, tile_rows)
    return result.reshape(kernel.shape)


def solution(mesh):
    placed = P(None, "row", None, "col", None)
    return jax.shard_map(
        per_device, mesh=mesh, in_specs=(placed,), out_specs=placed, check_vma=False
    )
```

```python
import functools

import jax
import jax.numpy as jnp
from jax import lax
from jax.experimental import pallas as pl
from jax.experimental.pallas import tpu as pltpu
from jax.sharding import PartitionSpec as P

P_SIZE = 512
NT = 16
STEP = 16
BLOCK = 128
EXACT = lax.Precision.HIGHEST


def exact_dot(left_side, right_side, contract=((1,), (0,))):
    return lax.dot_general(
        left_side,
        right_side,
        (contract, ((), ())),
        preferred_element_type=jnp.float32,
        precision=EXACT,
    )


def split(value):
    high = value.astype(jnp.bfloat16)
    return high, (value - high.astype(jnp.float32)).astype(jnp.bfloat16)


def split_three(value):
    high = value.astype(jnp.bfloat16)
    value = value - high.astype(jnp.float32)
    return high, *split(value)


def fast_dot(left_side, right_side, contract=((1,), (0,))):
    return lax.dot_general(
        left_side, right_side, (contract, ((), ())), preferred_element_type=jnp.float32
    )


def repeat_columns(rows, start):
    slot = lax.broadcasted_iota(jnp.int32, rows.shape, 1) // STEP
    spread_out = rows if start == 0 else pltpu.roll(rows, BLOCK - start, 1)
    at_start = spread_out
    for place in range(1, 6):
        spread_out = jnp.where(slot == place, pltpu.roll(at_start, place * STEP, 1), spread_out)
    high, middle, low = (part.astype(jnp.float32) for part in split_three(spread_out))
    parts = jnp.where(slot < 3, high, jnp.where(slot < 5, middle, low))
    return jnp.where(slot < 6, parts, 0.0).astype(jnp.bfloat16)


def factor_block(work, done):
    row_id = lax.broadcasted_iota(jnp.int32, (STEP, BLOCK), 0)
    for start in range(0, BLOCK, STEP):
        here = slice(start, start + STEP)
        halves = [work[here, 0:BLOCK], work[here, BLOCK : 2 * BLOCK]]
        columns = [
            jnp.broadcast_to(halves[0][:, start + j : start + j + 1], (STEP, BLOCK))
            for j in range(STEP)
        ]
        if start + STEP < BLOCK:
            raw = repeat_columns(work[start + STEP :, 0:BLOCK], start)
        kept = [jnp.zeros((STEP, BLOCK), jnp.float32)] * 2
        pivots = jnp.ones((STEP, BLOCK), jnp.float32)
        for k in range(STEP):
            pivot = jnp.broadcast_to(columns[k][k : k + 1, :], (STEP, BLOCK))
            factors = jnp.where(row_id == k, 0.0, columns[k] * (1.0 / pivot))
            for j in range(k + 1, STEP):
                top = jnp.broadcast_to(columns[j][k : k + 1, :], (STEP, BLOCK))
                columns[j] = columns[j] - factors * top
            pivots = jnp.where(row_id == k, pivot, pivots)
            for h in range(2):
                top = jnp.broadcast_to(halves[h][k : k + 1, :], (STEP, BLOCK))
                kept[h] = jnp.where(row_id == k, top, kept[h])
                halves[h] = halves[h] - factors * top
        scale = lax.rsqrt(pivots)
        inverse = 1.0 / pivots
        for h in range(2):
            done[here, h * BLOCK : (h + 1) * BLOCK] = kept[h] * scale
        if start + STEP < BLOCK:
            solved = jnp.concatenate([halves[0] * inverse, halves[1] * inverse], axis=1)
            high, middle, low = split_three(solved)
            parts = jnp.concatenate(
                [high, middle, low, high, middle, high, jnp.zeros_like(high), jnp.zeros_like(high)]
            )
            work[start + STEP :, :] = work[start + STEP :, :] - fast_dot(raw, parts)


def factor_kernel(given, factor, inverse, rest, work, done):
    rest[...] = given[...]
    factor_rest(rest, factor, inverse, work, done)


def factor_rest(rest, factor, inverse, work, done):
    order = rest.shape[0]
    inverse[...] = jnp.zeros_like(inverse)
    factor[...] = jnp.zeros_like(factor)
    row_id = lax.broadcasted_iota(jnp.int32, (BLOCK, BLOCK), 0)
    column_id = lax.broadcasted_iota(jnp.int32, (BLOCK, BLOCK), 1)
    for start in range(0, order, BLOCK):
        here = slice(start, start + BLOCK)
        work[:, 0:BLOCK] = rest[here, here]
        work[:, BLOCK:] = (row_id == column_id).astype(jnp.float32)
        factor_block(work, done)
        factor[here, here] = jnp.where(column_id >= row_id, done[:, 0:BLOCK], 0.0).T
        block_inverse = done[:, BLOCK:]
        if start:
            inverse[here, 0:start] = exact_dot(block_inverse, inverse[here, 0:start])
        inverse[here, here] = block_inverse
        if start + BLOCK < order:
            after = slice(start + BLOCK, order)
            upper = exact_dot(block_inverse, rest[here, after])
            lower = upper.T
            factor[after, here] = lower
            rest[after, after] = rest[after, after] - exact_dot(lower, upper)
            so_far = slice(0, start + BLOCK)
            inverse[after, so_far] = inverse[after, so_far] - exact_dot(
                lower, inverse[here, so_far]
            )


def factor_scratch():
    return [
        pltpu.VMEM((P_SIZE, P_SIZE), jnp.float32),
        pltpu.VMEM((BLOCK, 2 * BLOCK), jnp.float32),
        pltpu.VMEM((BLOCK, 2 * BLOCK), jnp.float32),
    ]


def factor_corner(corner):
    order = corner.shape[0]
    square = jax.ShapeDtypeStruct((order, order), jnp.float32)
    return pl.pallas_call(
        factor_kernel,
        out_shape=[square, square],
        scratch_shapes=factor_scratch(),
        compiler_params=pltpu.CompilerParams(vmem_limit_bytes=32 * 2**20),
    )(corner)


def spread(value, axis, offsets):
    count = lax.axis_size(axis)
    parts = [value]
    for offset in offsets[1:]:
        parts.append(lax.ppermute(value, axis, [(i, i ^ offset) for i in range(count)]))
    return jnp.stack(parts)


def gather_corner(mine):
    row_count = lax.axis_size("row")
    col_count = lax.axis_size("col")
    row_index = lax.axis_index("row")
    column_index = lax.axis_index("col")
    over_cols = spread(mine, "col", list(range(col_count)))
    over_chips = spread(over_cols, "row", list(range(0, row_count, 2)))
    slots = spread(over_chips, "row", [0, 1])
    slots = slots.transpose(1, 0, 2, 3, 4, 5).reshape(row_count, col_count, *mine.shape)
    slots = jnp.take(slots, jnp.arange(row_count) ^ row_index, axis=0, mode="clip")
    slots = jnp.take(slots, jnp.arange(col_count) ^ column_index, axis=1, mode="clip")
    return slots.transpose(2, 0, 3, 1, 4).reshape(3, P_SIZE, P_SIZE)


def per_device_general(kernel):
    row_count = lax.axis_size("row")
    col_count = lax.axis_size("col")
    tile_rows = P_SIZE // row_count
    tile_cols = P_SIZE // col_count
    row_index = lax.axis_index("row")
    column_index = lax.axis_index("col")
    tiles = kernel.reshape(NT, NT, tile_rows, tile_cols)
    corner = gather_corner(jnp.stack([tiles[0, 0], tiles[1, 0], tiles[1, 1]]))
    own_rows = tiles[:, 0:2].transpose(0, 2, 1, 3).reshape(NT * tile_rows, 2 * tile_cols)
    own_rows = lax.all_gather(own_rows, "col", axis=0, tiled=False)
    own_rows = own_rows.reshape(col_count, NT * tile_rows, 2, tile_cols).transpose(1, 2, 0, 3)
    own_rows = own_rows.reshape(NT * tile_rows, 2, P_SIZE)
    own_cols = tiles[0:2].transpose(0, 2, 1, 3).reshape(2 * tile_rows, NT * tile_cols)
    own_cols = lax.all_gather(own_cols, "row", axis=0, tiled=False)
    own_cols = own_cols.reshape(row_count, 2, tile_rows, NT * tile_cols).transpose(1, 0, 2, 3)
    own_cols = own_cols.reshape(2, P_SIZE, NT * tile_cols)

    first_corner, cross_corner, second_corner = (corner[i].astype(jnp.float32) for i in range(3))
    first_factor, first_inverse = factor_corner(0.5 * (first_corner + first_corner.T))
    cross = exact_dot(cross_corner, first_inverse, ((1,), (1,))).astype(jnp.bfloat16)
    updated_corner = second_corner - fast_dot(cross, cross, ((1,), (1,)))
    second_factor, second_inverse = factor_corner(0.5 * (updated_corner + updated_corner.T))

    first_rows = exact_dot(
        own_rows[tile_rows:, 0].astype(jnp.float32), first_inverse, ((1,), (1,))
    )
    first_cols = exact_dot(first_inverse, own_cols[0, :, tile_cols:].astype(jnp.float32))
    first_rows_rounded = first_rows.astype(jnp.bfloat16)
    first_cols_rounded = first_cols.astype(jnp.bfloat16)
    second_rows = own_rows[2 * tile_rows :, 1].astype(jnp.float32) - fast_dot(
        first_rows_rounded[tile_rows:], cross, ((1,), (1,))
    )
    second_cols = own_cols[1, :, 2 * tile_cols :].astype(jnp.float32) - fast_dot(
        cross, first_cols_rounded[:, tile_cols:]
    )
    second_rows = exact_dot(second_rows, second_inverse, ((1,), (1,)))
    second_cols = exact_dot(second_inverse, second_cols)
    left_side = jnp.concatenate(
        [first_rows_rounded[tile_rows:], second_rows.astype(jnp.bfloat16)], axis=1
    )
    right_side = jnp.concatenate(
        [first_cols_rounded[:, tile_cols:], second_cols.astype(jnp.bfloat16)], axis=0
    )
    inner = NT - 2
    product = fast_dot(left_side, right_side).reshape(inner, tile_rows, inner, tile_cols)
    trailing = tiles[2:, 2:].astype(jnp.float32) - product.transpose(0, 2, 1, 3)
    own = (row_index * tile_rows, column_index * tile_cols)
    first_own = lax.dynamic_slice_in_dim(first_rows, own[1], tile_cols, 1)
    second_own = lax.dynamic_slice_in_dim(second_rows, own[1], tile_cols, 1)
    first_tile = lax.dynamic_slice(first_factor, own, (tile_rows, tile_cols))
    second_tile = lax.dynamic_slice(second_factor, own, (tile_rows, tile_cols))
    result = jnp.zeros(tiles.shape, jnp.float32)
    result = result.at[2:, 2:].set(trailing)
    result = result.at[0, 0].set(first_tile)
    result = result.at[1:, 0].set(first_own.reshape(NT - 1, tile_rows, tile_cols))
    result = result.at[1, 1].set(second_tile)
    result = result.at[2:, 1].set(second_own.reshape(NT - 2, tile_rows, tile_cols))
    return result.reshape(kernel.shape)


def whole(shape):
    return pl.BlockSpec(shape, lambda *_: (0,) * len(shape))


def natural_tile(tiles, spread_rows, tile_rows):
    for r in range(tile_rows):
        spread_rows[r * NT : (r + 1) * NT, :] = tiles[:, r * BLOCK : (r + 1) * BLOCK].astype(
            jnp.float32
        )


def top_kernel(tiles, corner, top, spread_rows):
    tile_rows = corner.shape[1]
    for t in range(2):
        natural_tile(tiles[t], spread_rows, tile_rows)
        for s in range(NT):
            tile = spread_rows[pl.ds(s, tile_rows, stride=NT), :].astype(jnp.bfloat16)
            top[t * tile_rows : (t + 1) * tile_rows, s * BLOCK : (s + 1) * BLOCK] = tile
            if s <= t:
                corner[t + s] = tile


def natural_kernel(tiles, natural, left, spread_rows):
    tile_rows = natural.shape[0]
    natural_tile(tiles[0], spread_rows, tile_rows)
    for s in range(NT):
        tile = spread_rows[pl.ds(s, tile_rows, stride=NT), :].astype(jnp.bfloat16)
        natural[:, s * BLOCK : (s + 1) * BLOCK] = tile
        if s < 2:
            left[:, s * BLOCK : (s + 1) * BLOCK] = tile


def take_top(tiles, tile_rows):
    return pl.pallas_call(
        top_kernel,
        grid=(1,),
        in_specs=[pl.BlockSpec((2, NT, tile_rows * BLOCK), lambda i: (0, 0, 0))],
        out_specs=[whole((3, tile_rows, BLOCK)), whole((2 * tile_rows, NT * BLOCK))],
        out_shape=[
            jax.ShapeDtypeStruct((3, tile_rows, BLOCK), jnp.bfloat16),
            jax.ShapeDtypeStruct((2 * tile_rows, NT * BLOCK), jnp.bfloat16),
        ],
        scratch_shapes=[pltpu.VMEM((tile_rows * NT, BLOCK), jnp.float32)],
        compiler_params=pltpu.CompilerParams(vmem_limit_bytes=16 * 2**20),
    )(tiles)


def take_natural(tiles, tile_rows):
    return pl.pallas_call(
        natural_kernel,
        grid=(NT,),
        in_specs=[pl.BlockSpec((1, NT, tile_rows * BLOCK), lambda t: (t, 0, 0))],
        out_specs=[
            pl.BlockSpec((tile_rows, NT * BLOCK), lambda t: (t, 0)),
            pl.BlockSpec((tile_rows, 2 * BLOCK), lambda t: (t, 0)),
        ],
        out_shape=[
            jax.ShapeDtypeStruct((NT * tile_rows, NT * BLOCK), jnp.bfloat16),
            jax.ShapeDtypeStruct((NT * tile_rows, 2 * BLOCK), jnp.bfloat16),
        ],
        scratch_shapes=[pltpu.VMEM((tile_rows * NT, BLOCK), jnp.float32)],
        compiler_params=pltpu.CompilerParams(vmem_limit_bytes=16 * 2**20),
        cost_estimate=pl.CostEstimate(
            flops=0, bytes_accessed=16 * NT * tile_rows * NT * BLOCK, transcendentals=0
        ),
    )(tiles)


def place_corner(place, slots, which, corner):
    row_index, column_index = place[0], place[1]
    chips, col_count, _, tile_rows, _ = slots[0].shape
    for core, held in enumerate(slots):
        for chip in range(chips):
            first_row = pl.multiple_of((row_index ^ (2 * chip + core)) * tile_rows, tile_rows)
            for col in range(col_count):
                first_col = pl.multiple_of((column_index ^ col) * BLOCK, BLOCK)
                corner[pl.ds(first_row, tile_rows), pl.ds(first_col, BLOCK)] = held[
                    chip, col, which
                ].astype(jnp.float32)


def first_kernel(place, near, far, factor, inverse, rest, work, done):
    place_corner(place, (near, far), 0, rest)
    factor_rest(rest, factor, inverse, work, done)


def second_kernel(
    place, near, far, first_inverse, factor, inverse, cross, rest, work, done
):
    place_corner(place, (near, far), 0, rest)
    given = rest[...].astype(jnp.bfloat16)
    high, low = split(first_inverse[...])
    solved = fast_dot(
        jnp.concatenate([given, given], axis=1),
        jnp.concatenate([high, low], axis=1),
        ((1,), (1,)),
    ).astype(jnp.bfloat16)
    cross[...] = solved
    place_corner(place, (near, far), 1, rest)
    rest[...] = rest[...] - fast_dot(solved, solved, ((1,), (1,)))
    factor_rest(rest, factor, inverse, work, done)


def factor_call(body, place, slots, extra, extra_out):
    square = jax.ShapeDtypeStruct((P_SIZE, P_SIZE), jnp.float32)
    on_vmem = pl.BlockSpec(memory_space=pltpu.VMEM)
    return pl.pallas_call(
        body,
        in_specs=[pl.BlockSpec(memory_space=pltpu.SMEM)] + [on_vmem] * (2 + len(extra)),
        out_shape=[square, square] + extra_out,
        scratch_shapes=factor_scratch(),
        compiler_params=pltpu.CompilerParams(vmem_limit_bytes=32 * 2**20),
        cost_estimate=pl.CostEstimate(
            flops=20 * 10**9, bytes_accessed=4 * 2**20, transcendentals=0
        ),
    )(place, *slots, *extra)


def rows_kernel(place, *refs):
    lefts = refs[:-9]
    first_inverse, second_inverse, cross, rounded, own, *scratch = refs[-9:]
    first_side, cross_side, second_side, solved_rows = scratch
    column_index = place[1]
    own_col = pl.multiple_of(column_index * BLOCK, BLOCK)
    order = P_SIZE

    @pl.when(pl.program_id(0) == 0)
    def _():
        for offset in range(len(lefts)):
            first = pl.multiple_of((column_index ^ offset) * BLOCK, BLOCK)
            here = pl.ds(first, BLOCK)
            for k in range(3):
                to = slice(k * order + offset * BLOCK, k * order + (offset + 1) * BLOCK)
                if k < 2:
                    first_side[to, :] = split(first_inverse[:, here].T)[k]
                second_side[to, :] = split(second_inverse[:, here].T)[k // 2]
            to = slice(offset * BLOCK, (offset + 1) * BLOCK)
            cross_side[:, to] = cross[here, :].astype(jnp.float32).T.astype(jnp.bfloat16)

    given = [left[:, 0:BLOCK] for left in lefts]
    solved = fast_dot(jnp.concatenate(given + given, axis=1), first_side[...])
    solved_rows[:, 0:order] = solved
    first_rounded = solved.astype(jnp.bfloat16)
    given = jnp.concatenate([left[:, BLOCK : 2 * BLOCK] for left in lefts], axis=1)
    left_over = given.astype(jnp.float32) - fast_dot(first_rounded, cross_side[...])
    high, low = split(left_over)
    solved = fast_dot(jnp.concatenate([high, low, high], axis=1), second_side[...])
    solved_rows[:, order:] = solved
    rounded[:, 0:order] = first_rounded
    rounded[:, order:] = solved.astype(jnp.bfloat16)
    own[:, 0:BLOCK] = solved_rows[:, pl.ds(own_col, BLOCK)]
    own[:, BLOCK:] = solved_rows[:, pl.ds(order + own_col, BLOCK)]


def solve_rows(place, lefts, first_inverse, second_inverse, cross):
    count = lefts[0].shape[0]
    rows = count // 2
    square = whole((P_SIZE, P_SIZE))
    return pl.pallas_call(
        rows_kernel,
        grid=(count // rows,),
        in_specs=[
            pl.BlockSpec(memory_space=pltpu.SMEM),
            *[pl.BlockSpec((rows, 2 * BLOCK), lambda i: (i, 0)) for _ in lefts],
            *[square] * 3,
        ],
        out_specs=[
            pl.BlockSpec((rows, 2 * P_SIZE), lambda i: (i, 0)),
            pl.BlockSpec((rows, 2 * BLOCK), lambda i: (i, 0)),
        ],
        out_shape=[
            jax.ShapeDtypeStruct((count, 2 * P_SIZE), jnp.bfloat16),
            jax.ShapeDtypeStruct((count, 2 * BLOCK), jnp.float32),
        ],
        scratch_shapes=[
            pltpu.VMEM((2 * P_SIZE, P_SIZE), jnp.bfloat16),
            pltpu.VMEM((P_SIZE, P_SIZE), jnp.bfloat16),
            pltpu.VMEM((3 * P_SIZE, P_SIZE), jnp.bfloat16),
            pltpu.VMEM((rows, 2 * P_SIZE), jnp.float32),
        ],
        compiler_params=pltpu.CompilerParams(vmem_limit_bytes=32 * 2**20),
        cost_estimate=pl.CostEstimate(
            flops=12 * count * P_SIZE**2, bytes_accessed=10 * 2**20, transcendentals=0
        ),
    )(place, *lefts, first_inverse, second_inverse, cross)


def cols_kernel(chips, place, natural, *refs):
    evens, odds = refs[:chips], refs[chips]
    first_factor, first_inverse, second_factor, second_inverse, cross = refs[chips + 1 : chips + 6]
    rounded, own, result = refs[chips + 6 : chips + 9]
    given_cols, first_side, second_side, copied = refs[chips + 9 :]
    row_index, column_index = place[0], place[1]
    tile_rows = evens[0].shape[0] // 2
    order, half = P_SIZE, P_SIZE // 2
    step = pl.program_id(0)
    width = 2 * BLOCK

    def copies():
        for chip in range(chips):
            for core in range(2):
                source = odds.at[chip] if core else evens[chip]
                first = pl.multiple_of((row_index ^ (2 * chip + core)) * tile_rows, tile_rows)
                for t in range(2):
                    yield pltpu.make_async_copy(
                        source.at[pl.ds(t * tile_rows, tile_rows), :],
                        given_cols.at[pl.ds(t * order + first, tile_rows), :],
                        copied.at[(2 * chip + core) * 2 + t],
                    )

    @pl.when(step == 0)
    def _():
        for copy in copies():
            copy.start()
        high, low = split(first_inverse[...])
        first_side[:, 0:order] = high
        first_side[:, order:] = low
        high, low = split(second_inverse[...])
        second_side[:, 0:order] = high
        second_side[:, order : 2 * order] = high
        second_side[:, 2 * order :] = low
        own_row = pl.multiple_of(row_index * tile_rows, tile_rows)
        own_col = pl.multiple_of(column_index * BLOCK, BLOCK)
        tile = (pl.ds(own_row, tile_rows), pl.ds(own_col, BLOCK))
        for t in range(NT):
            rows = slice(t * tile_rows, (t + 1) * tile_rows)
            result[t, 0] = first_factor[tile] if t == 0 else own[rows, 0:BLOCK]
            if t == 0:
                result[t, 1] = jnp.zeros((tile_rows, BLOCK), jnp.float32)
            else:
                result[t, 1] = second_factor[tile] if t == 1 else own[rows, BLOCK:]
        for copy in copies():
            copy.wait()

    @pl.when(step > 0)
    def _():
        here = pl.ds(pl.multiple_of(step * width, width), width)

        def lower_dot(side, parts):
            upper_side = jnp.concatenate(
                [side[0:half, k * order : k * order + half] for k in range(len(parts))], axis=1
            )
            upper = fast_dot(upper_side, jnp.concatenate([part[0:half] for part in parts]))
            lower = fast_dot(side[half:order, :], jnp.concatenate(parts))
            return jnp.concatenate([upper, lower])

        given = given_cols[0:order, here]
        first = lower_dot(first_side, [given, given]).astype(jnp.bfloat16)
        left_over = given_cols[order:, here].astype(jnp.float32) - fast_dot(cross[...], first)
        high, low = split(left_over)
        second = lower_dot(second_side, [high, low, high]).astype(jnp.bfloat16)
        begin = 2 * tile_rows
        product = fast_dot(rounded[begin:, :], jnp.concatenate([first, second]))
        kept = natural[begin:, :].astype(jnp.float32) - product
        for s in range(2):
            for t in range(NT):
                if t < 2:
                    result[t, s] = jnp.zeros((tile_rows, BLOCK), jnp.float32)
                else:
                    result[t, s] = kept[
                        (t - 2) * tile_rows : (t - 1) * tile_rows, s * BLOCK : (s + 1) * BLOCK
                    ]


def solve_cols(place, natural, evens, odds, factors, rounded, own, tile_rows):
    chips = len(evens)
    square = whole((P_SIZE, P_SIZE))
    return pl.pallas_call(
        functools.partial(cols_kernel, chips),
        grid=(NT // 2,),
        in_specs=[
            pl.BlockSpec(memory_space=pltpu.SMEM),
            pl.BlockSpec((NT * tile_rows, 2 * BLOCK), lambda j: (0, j)),
            *[pl.BlockSpec(memory_space=pl.ANY)] * (chips + 1),
            *[square] * 5,
            whole(rounded.shape),
            whole(own.shape),
        ],
        out_specs=pl.BlockSpec((NT, 2, tile_rows, BLOCK), lambda j: (0, j, 0, 0)),
        out_shape=jax.ShapeDtypeStruct((NT, NT, tile_rows, BLOCK), jnp.float32),
        scratch_shapes=[
            pltpu.VMEM((2 * P_SIZE, NT * BLOCK), jnp.bfloat16),
            pltpu.VMEM((P_SIZE, 2 * P_SIZE), jnp.bfloat16),
            pltpu.VMEM((P_SIZE, 3 * P_SIZE), jnp.bfloat16),
            pltpu.SemaphoreType.DMA((4 * chips,)),
        ],
        compiler_params=pltpu.CompilerParams(vmem_limit_bytes=48 * 2**20),
        cost_estimate=pl.CostEstimate(
            flops=10 * 10**9, bytes_accessed=24 * 2**20, transcendentals=0
        ),
    )(place, natural, *evens, odds, *factors, rounded, own)


def swap(value, axis, offset):
    count = lax.axis_size(axis)
    return lax.ppermute(value, axis, [(i, i ^ offset) for i in range(count)])


def double(value, axis, offsets):
    value = value[None]
    for offset in offsets:
        value = jnp.concatenate([value, swap(value, axis, offset)])
    return value


def powers(begin, count):
    offsets = []
    while begin < count:
        offsets.append(begin)
        begin *= 2
    return offsets


def per_device(kernel):
    row_count = lax.axis_size("row")
    col_count = lax.axis_size("col")
    tile_rows = P_SIZE // row_count
    if P_SIZE != col_count * BLOCK or tile_rows % STEP:
        return per_device_general(kernel)
    place = jnp.stack([lax.axis_index("row"), lax.axis_index("col")]).astype(jnp.int32)
    tiles = kernel.reshape(NT, NT, tile_rows * BLOCK)
    corner, top = take_top(tiles, tile_rows)
    natural, left = take_natural(tiles, tile_rows)
    chips = range(2, row_count, 2)
    over_cols = double(corner, "col", powers(1, col_count))
    near = double(over_cols[:, 0:1], "row", powers(2, row_count))
    far = swap(near, "row", 1)
    other = over_cols[:, 1:]
    other_near = jnp.stack([other] + [swap(other, "row", d) for d in chips])
    first_factor, first_inverse = factor_call(first_kernel, place, (near, far), (), [])
    other_far = swap(other_near, "row", 1)
    lefts = [left] + [swap(left, "col", d) for d in range(1, col_count)]
    evens = [top] + [swap(top, "row", d) for d in chips]
    half = jax.ShapeDtypeStruct((P_SIZE, P_SIZE), jnp.bfloat16)
    second_factor, second_inverse, cross = factor_call(
        second_kernel, place, (other_near, other_far), (first_inverse,), [half]
    )
    odds = swap(jnp.stack(evens), "row", 1)
    rounded, own = solve_rows(place, lefts, first_inverse, second_inverse, cross)
    factors = (first_factor, first_inverse, second_factor, second_inverse, cross)
    result = solve_cols(place, natural, evens, odds, factors, rounded, own, tile_rows)
    return result.reshape(kernel.shape)


def solution(mesh):
    placed = P(None, "row", None, "col", None)
    return jax.shard_map(
        per_device, mesh=mesh, in_specs=(placed,), out_specs=placed, check_vma=False
    )
```

```python
import functools

import jax
import jax.numpy as jnp
from jax import lax
from jax.experimental import pallas as pl
from jax.experimental.pallas import tpu as pltpu
from jax.sharding import PartitionSpec as P

P_SIZE = 512
NT = 16
STEP = 16
BLOCK = 128
EXACT = lax.Precision.HIGHEST


def exact_dot(left_side, right_side, contract=((1,), (0,))):
    return lax.dot_general(
        left_side,
        right_side,
        (contract, ((), ())),
        preferred_element_type=jnp.float32,
        precision=EXACT,
    )


def split(value):
    high = value.astype(jnp.bfloat16)
    return high, (value - high.astype(jnp.float32)).astype(jnp.bfloat16)


def split_three(value):
    high = value.astype(jnp.bfloat16)
    value = value - high.astype(jnp.float32)
    return high, *split(value)


def fast_dot(left_side, right_side, contract=((1,), (0,))):
    return lax.dot_general(
        left_side, right_side, (contract, ((), ())), preferred_element_type=jnp.float32
    )


def repeat_columns(rows, start):
    slot = lax.broadcasted_iota(jnp.int32, rows.shape, 1) // STEP
    spread_out = rows if start == 0 else pltpu.roll(rows, BLOCK - start, 1)
    at_start = spread_out
    for place in range(1, 6):
        spread_out = jnp.where(slot == place, pltpu.roll(at_start, place * STEP, 1), spread_out)
    high, middle, low = (part.astype(jnp.float32) for part in split_three(spread_out))
    parts = jnp.where(slot < 3, high, jnp.where(slot < 5, middle, low))
    return jnp.where(slot < 6, parts, 0.0).astype(jnp.bfloat16)


def factor_block(work, done):
    row_id = lax.broadcasted_iota(jnp.int32, (STEP, BLOCK), 0)
    for start in range(0, BLOCK, STEP):
        here = slice(start, start + STEP)
        halves = [work[here, 0:BLOCK], work[here, BLOCK : 2 * BLOCK]]
        columns = [
            jnp.broadcast_to(halves[0][:, start + j : start + j + 1], (STEP, BLOCK))
            for j in range(STEP)
        ]
        if start + STEP < BLOCK:
            raw = repeat_columns(work[start + STEP :, 0:BLOCK], start)
        kept = [jnp.zeros((STEP, BLOCK), jnp.float32)] * 2
        pivots = jnp.ones((STEP, BLOCK), jnp.float32)
        for k in range(STEP):
            pivot = jnp.broadcast_to(columns[k][k : k + 1, :], (STEP, BLOCK))
            factors = jnp.where(row_id == k, 0.0, columns[k] * (1.0 / pivot))
            for j in range(k + 1, STEP):
                top = jnp.broadcast_to(columns[j][k : k + 1, :], (STEP, BLOCK))
                columns[j] = columns[j] - factors * top
            pivots = jnp.where(row_id == k, pivot, pivots)
            for h in range(2):
                top = jnp.broadcast_to(halves[h][k : k + 1, :], (STEP, BLOCK))
                kept[h] = jnp.where(row_id == k, top, kept[h])
                halves[h] = halves[h] - factors * top
        scale = lax.rsqrt(pivots)
        inverse = 1.0 / pivots
        for h in range(2):
            done[here, h * BLOCK : (h + 1) * BLOCK] = kept[h] * scale
        if start + STEP < BLOCK:
            solved = jnp.concatenate([halves[0] * inverse, halves[1] * inverse], axis=1)
            high, middle, low = split_three(solved)
            parts = jnp.concatenate(
                [high, middle, low, high, middle, high, jnp.zeros_like(high), jnp.zeros_like(high)]
            )
            work[start + STEP :, :] = work[start + STEP :, :] - fast_dot(raw, parts)


def factor_kernel(given, factor, inverse, rest, work, done):
    rest[...] = given[...]
    factor_rest(rest, factor, inverse, work, done)


def factor_rest(rest, factor, inverse, work, done):
    order = rest.shape[0]
    inverse[...] = jnp.zeros_like(inverse)
    factor[...] = jnp.zeros_like(factor)
    row_id = lax.broadcasted_iota(jnp.int32, (BLOCK, BLOCK), 0)
    column_id = lax.broadcasted_iota(jnp.int32, (BLOCK, BLOCK), 1)
    for start in range(0, order, BLOCK):
        here = slice(start, start + BLOCK)
        work[:, 0:BLOCK] = rest[here, here]
        work[:, BLOCK:] = (row_id == column_id).astype(jnp.float32)
        factor_block(work, done)
        factor[here, here] = jnp.where(column_id >= row_id, done[:, 0:BLOCK], 0.0).T
        block_inverse = done[:, BLOCK:]
        if start:
            inverse[here, 0:start] = exact_dot(block_inverse, inverse[here, 0:start])
        inverse[here, here] = block_inverse
        if start + BLOCK < order:
            after = slice(start + BLOCK, order)
            upper = exact_dot(block_inverse, rest[here, after])
            lower = upper.T
            factor[after, here] = lower
            rest[after, after] = rest[after, after] - exact_dot(lower, upper)
            so_far = slice(0, start + BLOCK)
            inverse[after, so_far] = inverse[after, so_far] - exact_dot(
                lower, inverse[here, so_far]
            )


def factor_scratch():
    return [
        pltpu.VMEM((P_SIZE, P_SIZE), jnp.float32),
        pltpu.VMEM((BLOCK, 2 * BLOCK), jnp.float32),
        pltpu.VMEM((BLOCK, 2 * BLOCK), jnp.float32),
    ]


def factor_corner(corner):
    order = corner.shape[0]
    square = jax.ShapeDtypeStruct((order, order), jnp.float32)
    return pl.pallas_call(
        factor_kernel,
        out_shape=[square, square],
        scratch_shapes=factor_scratch(),
        compiler_params=pltpu.CompilerParams(vmem_limit_bytes=20 * 2**20),
    )(corner)


def spread(value, axis, offsets):
    count = lax.axis_size(axis)
    parts = [value]
    for offset in offsets[1:]:
        parts.append(lax.ppermute(value, axis, [(i, i ^ offset) for i in range(count)]))
    return jnp.stack(parts)


def gather_corner(mine):
    row_count = lax.axis_size("row")
    col_count = lax.axis_size("col")
    row_index = lax.axis_index("row")
    column_index = lax.axis_index("col")
    over_cols = spread(mine, "col", list(range(col_count)))
    over_chips = spread(over_cols, "row", list(range(0, row_count, 2)))
    slots = spread(over_chips, "row", [0, 1])
    slots = slots.transpose(1, 0, 2, 3, 4, 5).reshape(row_count, col_count, *mine.shape)
    slots = jnp.take(slots, jnp.arange(row_count) ^ row_index, axis=0, mode="clip")
    slots = jnp.take(slots, jnp.arange(col_count) ^ column_index, axis=1, mode="clip")
    return slots.transpose(2, 0, 3, 1, 4).reshape(3, P_SIZE, P_SIZE)


def per_device_general(kernel):
    row_count = lax.axis_size("row")
    col_count = lax.axis_size("col")
    tile_rows = P_SIZE // row_count
    tile_cols = P_SIZE // col_count
    row_index = lax.axis_index("row")
    column_index = lax.axis_index("col")
    tiles = kernel.reshape(NT, NT, tile_rows, tile_cols)
    corner = gather_corner(jnp.stack([tiles[0, 0], tiles[1, 0], tiles[1, 1]]))
    own_rows = tiles[:, 0:2].transpose(0, 2, 1, 3).reshape(NT * tile_rows, 2 * tile_cols)
    own_rows = lax.all_gather(own_rows, "col", axis=0, tiled=False)
    own_rows = own_rows.reshape(col_count, NT * tile_rows, 2, tile_cols).transpose(1, 2, 0, 3)
    own_rows = own_rows.reshape(NT * tile_rows, 2, P_SIZE)
    own_cols = tiles[0:2].transpose(0, 2, 1, 3).reshape(2 * tile_rows, NT * tile_cols)
    own_cols = lax.all_gather(own_cols, "row", axis=0, tiled=False)
    own_cols = own_cols.reshape(row_count, 2, tile_rows, NT * tile_cols).transpose(1, 0, 2, 3)
    own_cols = own_cols.reshape(2, P_SIZE, NT * tile_cols)

    first_corner, cross_corner, second_corner = (corner[i].astype(jnp.float32) for i in range(3))
    first_factor, first_inverse = factor_corner(0.5 * (first_corner + first_corner.T))
    cross = exact_dot(cross_corner, first_inverse, ((1,), (1,))).astype(jnp.bfloat16)
    updated_corner = second_corner - fast_dot(cross, cross, ((1,), (1,)))
    second_factor, second_inverse = factor_corner(0.5 * (updated_corner + updated_corner.T))

    first_rows = exact_dot(
        own_rows[tile_rows:, 0].astype(jnp.float32), first_inverse, ((1,), (1,))
    )
    first_cols = exact_dot(first_inverse, own_cols[0, :, tile_cols:].astype(jnp.float32))
    first_rows_rounded = first_rows.astype(jnp.bfloat16)
    first_cols_rounded = first_cols.astype(jnp.bfloat16)
    second_rows = own_rows[2 * tile_rows :, 1].astype(jnp.float32) - fast_dot(
        first_rows_rounded[tile_rows:], cross, ((1,), (1,))
    )
    second_cols = own_cols[1, :, 2 * tile_cols :].astype(jnp.float32) - fast_dot(
        cross, first_cols_rounded[:, tile_cols:]
    )
    second_rows = exact_dot(second_rows, second_inverse, ((1,), (1,)))
    second_cols = exact_dot(second_inverse, second_cols)
    left_side = jnp.concatenate(
        [first_rows_rounded[tile_rows:], second_rows.astype(jnp.bfloat16)], axis=1
    )
    right_side = jnp.concatenate(
        [first_cols_rounded[:, tile_cols:], second_cols.astype(jnp.bfloat16)], axis=0
    )
    inner = NT - 2
    product = fast_dot(left_side, right_side).reshape(inner, tile_rows, inner, tile_cols)
    trailing = tiles[2:, 2:].astype(jnp.float32) - product.transpose(0, 2, 1, 3)
    own = (row_index * tile_rows, column_index * tile_cols)
    first_own = lax.dynamic_slice_in_dim(first_rows, own[1], tile_cols, 1)
    second_own = lax.dynamic_slice_in_dim(second_rows, own[1], tile_cols, 1)
    first_tile = lax.dynamic_slice(first_factor, own, (tile_rows, tile_cols))
    second_tile = lax.dynamic_slice(second_factor, own, (tile_rows, tile_cols))
    result = jnp.zeros(tiles.shape, jnp.float32)
    result = result.at[2:, 2:].set(trailing)
    result = result.at[0, 0].set(first_tile)
    result = result.at[1:, 0].set(first_own.reshape(NT - 1, tile_rows, tile_cols))
    result = result.at[1, 1].set(second_tile)
    result = result.at[2:, 1].set(second_own.reshape(NT - 2, tile_rows, tile_cols))
    return result.reshape(kernel.shape)


def whole(shape):
    return pl.BlockSpec(shape, lambda *_: (0,) * len(shape))


def natural_tile(tiles, spread_rows, tile_rows):
    for r in range(tile_rows):
        spread_rows[r * NT : (r + 1) * NT, :] = tiles[:, r * BLOCK : (r + 1) * BLOCK].astype(
            jnp.float32
        )


def top_kernel(tiles, corner, top, held, spread_rows, copied):
    tile_rows = corner.shape[1]
    copies = [pltpu.make_async_copy(tiles.at[t], held.at[t], copied.at[t]) for t in range(2)]
    for copy in copies:
        copy.start()
    for t in range(2):
        copies[t].wait()
        natural_tile(held[t], spread_rows, tile_rows)
        for s in range(NT):
            tile = spread_rows[pl.ds(s, tile_rows, stride=NT), :].astype(jnp.bfloat16)
            if s >= 2:
                here = slice((s - 2) * BLOCK, (s - 1) * BLOCK)
                top[t * tile_rows : (t + 1) * tile_rows, here] = tile
            elif s <= t:
                corner[t + s] = tile


def natural_kernel(tiles, natural, left, spread_rows):
    tile_rows = natural.shape[0]
    natural_tile(tiles[0], spread_rows, tile_rows)
    for s in range(NT):
        tile = spread_rows[pl.ds(s, tile_rows, stride=NT), :].astype(jnp.bfloat16)
        natural[:, s * BLOCK : (s + 1) * BLOCK] = tile
        if s < 2:
            left[:, s * BLOCK : (s + 1) * BLOCK] = tile


def take_top(tiles, tile_rows):
    return pl.pallas_call(
        top_kernel,
        in_specs=[pl.BlockSpec(memory_space=pltpu.HBM)],
        out_shape=[
            jax.ShapeDtypeStruct((3, tile_rows, BLOCK), jnp.bfloat16),
            jax.ShapeDtypeStruct((2 * tile_rows, (NT - 2) * BLOCK), jnp.bfloat16),
        ],
        scratch_shapes=[
            pltpu.VMEM((2, NT, tile_rows * BLOCK), jnp.bfloat16),
            pltpu.VMEM((tile_rows * NT, BLOCK), jnp.float32),
            pltpu.SemaphoreType.DMA((2,)),
        ],
        compiler_params=pltpu.CompilerParams(vmem_limit_bytes=60 * 2**20),
    )(tiles)


def take_natural(tiles, tile_rows):
    return pl.pallas_call(
        natural_kernel,
        grid=(NT,),
        in_specs=[pl.BlockSpec((1, NT, tile_rows * BLOCK), lambda t: (t, 0, 0))],
        out_specs=[
            pl.BlockSpec((tile_rows, NT * BLOCK), lambda t: (t, 0)),
            pl.BlockSpec((tile_rows, 2 * BLOCK), lambda t: (jnp.maximum(t - 2, 0), 0)),
        ],
        out_shape=[
            jax.ShapeDtypeStruct((NT * tile_rows, NT * BLOCK), jnp.bfloat16),
            jax.ShapeDtypeStruct(((NT - 2) * tile_rows, 2 * BLOCK), jnp.bfloat16),
        ],
        scratch_shapes=[pltpu.VMEM((tile_rows * NT, BLOCK), jnp.float32)],
        compiler_params=pltpu.CompilerParams(vmem_limit_bytes=60 * 2**20),
        cost_estimate=pl.CostEstimate(
            flops=0, bytes_accessed=16 * NT * tile_rows * NT * BLOCK, transcendentals=0
        ),
    )(tiles)


def place_corner(place, slots, which, corner):
    row_index, column_index = place[0], place[1]
    chips, col_count, _, tile_rows, _ = slots[0].shape
    for core, held in enumerate(slots):
        for chip in range(chips):
            first_row = pl.multiple_of((row_index ^ (2 * chip + core)) * tile_rows, tile_rows)
            for col in range(col_count):
                first_col = pl.multiple_of((column_index ^ col) * BLOCK, BLOCK)
                corner[pl.ds(first_row, tile_rows), pl.ds(first_col, BLOCK)] = held[
                    chip, col, which
                ].astype(jnp.float32)


def first_kernel(place, near, far, factor, inverse, rest, work, done):
    place_corner(place, (near, far), 0, rest)
    factor_rest(rest, factor, inverse, work, done)


def second_kernel(
    place, near, far, first_inverse, factor, inverse, cross, own, rest, work, done
):
    place_corner(place, (near, far), 0, rest)
    given = rest[...].astype(jnp.bfloat16)
    high, low = split(first_inverse[...])
    solved = fast_dot(
        jnp.concatenate([given, given], axis=1),
        jnp.concatenate([high, low], axis=1),
        ((1,), (1,)),
    )
    rest[...] = solved
    tile_rows, tile_cols = own.shape
    own[...] = rest[
        pl.ds(pl.multiple_of(place[0] * tile_rows, tile_rows), tile_rows),
        pl.ds(pl.multiple_of(place[1] * tile_cols, tile_cols), tile_cols),
    ]
    solved = solved.astype(jnp.bfloat16)
    cross[...] = solved
    place_corner(place, (near, far), 1, rest)
    rest[...] = rest[...] - fast_dot(solved, solved, ((1,), (1,)))
    factor_rest(rest, factor, inverse, work, done)


def factor_call(body, place, slots, extra, extra_out, cost):
    square = jax.ShapeDtypeStruct((P_SIZE, P_SIZE), jnp.float32)
    on_vmem = pl.BlockSpec(memory_space=pltpu.VMEM)
    return pl.pallas_call(
        body,
        in_specs=[pl.BlockSpec(memory_space=pltpu.SMEM)] + [on_vmem] * (2 + len(extra)),
        out_shape=[square, square] + extra_out,
        scratch_shapes=factor_scratch(),
        compiler_params=pltpu.CompilerParams(vmem_limit_bytes=20 * 2**20),
        cost_estimate=pl.CostEstimate(
            flops=cost, bytes_accessed=4 * 2**20, transcendentals=0
        ),
    )(place, *slots, *extra)


def rows_kernel(place, *refs):
    lefts = refs[:-9]
    first_inverse, second_inverse, cross, rounded, own, *scratch = refs[-9:]
    first_side, cross_side, second_side, solved_rows = scratch
    column_index = place[1]
    own_col = pl.multiple_of(column_index * BLOCK, BLOCK)
    order = P_SIZE

    @pl.when(pl.program_id(0) == 0)
    def _():
        for offset in range(len(lefts)):
            first = pl.multiple_of((column_index ^ offset) * BLOCK, BLOCK)
            here = pl.ds(first, BLOCK)
            for k in range(3):
                to = slice(k * order + offset * BLOCK, k * order + (offset + 1) * BLOCK)
                if k < 2:
                    first_side[to, :] = split(first_inverse[:, here].T)[k]
                second_side[to, :] = split(second_inverse[:, here].T)[k // 2]
            to = slice(offset * BLOCK, (offset + 1) * BLOCK)
            cross_side[:, to] = cross[here, :].astype(jnp.float32).T.astype(jnp.bfloat16)

    given = [left[:, 0:BLOCK] for left in lefts]
    solved = fast_dot(jnp.concatenate(given + given, axis=1), first_side[...])
    solved_rows[:, 0:order] = solved
    first_rounded = solved.astype(jnp.bfloat16)
    given = jnp.concatenate([left[:, BLOCK : 2 * BLOCK] for left in lefts], axis=1)
    left_over = given.astype(jnp.float32) - fast_dot(first_rounded, cross_side[...])
    high, low = split(left_over)
    solved = fast_dot(jnp.concatenate([high, low, high], axis=1), second_side[...])
    solved_rows[:, order:] = solved
    rounded[:, 0:order] = first_rounded
    rounded[:, order:] = solved.astype(jnp.bfloat16)
    own[:, 0:BLOCK] = solved_rows[:, pl.ds(own_col, BLOCK)]
    own[:, BLOCK:] = solved_rows[:, pl.ds(order + own_col, BLOCK)]


def solve_rows(place, lefts, first_inverse, second_inverse, cross):
    count = lefts[0].shape[0]
    rows = count // 2
    square = whole((P_SIZE, P_SIZE))
    return pl.pallas_call(
        rows_kernel,
        grid=(count // rows,),
        in_specs=[
            pl.BlockSpec(memory_space=pltpu.SMEM),
            *[pl.BlockSpec((rows, 2 * BLOCK), lambda i: (i, 0)) for _ in lefts],
            *[square] * 3,
        ],
        out_specs=[
            pl.BlockSpec((rows, 2 * P_SIZE), lambda i: (i, 0)),
            pl.BlockSpec((rows, 2 * BLOCK), lambda i: (i, 0)),
        ],
        out_shape=[
            jax.ShapeDtypeStruct((count, 2 * P_SIZE), jnp.bfloat16),
            jax.ShapeDtypeStruct((count, 2 * BLOCK), jnp.float32),
        ],
        scratch_shapes=[
            pltpu.VMEM((2 * P_SIZE, P_SIZE), jnp.bfloat16),
            pltpu.VMEM((P_SIZE, P_SIZE), jnp.bfloat16),
            pltpu.VMEM((3 * P_SIZE, P_SIZE), jnp.bfloat16),
            pltpu.VMEM((rows, 2 * P_SIZE), jnp.float32),
        ],
        compiler_params=pltpu.CompilerParams(vmem_limit_bytes=24 * 2**20),
        cost_estimate=pl.CostEstimate(
            flops=12 * count * P_SIZE**2, bytes_accessed=10 * 2**20, transcendentals=0
        ),
    )(place, *lefts, first_inverse, second_inverse, cross)


def cols_kernel(chips, place, natural, *refs):
    evens, odds = refs[:chips], refs[chips]
    first_factor, first_inverse, second_factor, second_inverse, cross = refs[chips + 1 : chips + 6]
    rounded, own, own_cross, result = refs[chips + 6 : chips + 10]
    given_cols, first_side, second_side, copied = refs[chips + 10 :]
    row_index, column_index = place[0], place[1]
    tile_rows = evens[0].shape[0] // 2
    order, half = P_SIZE, P_SIZE // 2
    step = pl.program_id(0)
    width = 2 * BLOCK

    def copies():
        for chip in range(chips):
            for core in range(2):
                source = odds.at[chip] if core else evens[chip]
                first = pl.multiple_of((row_index ^ (2 * chip + core)) * tile_rows, tile_rows)
                for t in range(2):
                    yield pltpu.make_async_copy(
                        source.at[pl.ds(t * tile_rows, tile_rows), :],
                        given_cols.at[pl.ds(t * order + first, tile_rows), :],
                        copied.at[(2 * chip + core) * 2 + t],
                    )

    @pl.when(step == 0)
    def _():
        for copy in copies():
            copy.start()
        high, low = split(first_inverse[...])
        first_side[:, 0:order] = high
        first_side[:, order:] = low
        high, low = split(second_inverse[...])
        second_side[:, 0:order] = high
        second_side[:, order : 2 * order] = high
        second_side[:, 2 * order :] = low
        own_row = pl.multiple_of(row_index * tile_rows, tile_rows)
        own_col = pl.multiple_of(column_index * BLOCK, BLOCK)
        tile = (pl.ds(own_row, tile_rows), pl.ds(own_col, BLOCK))
        result[0, 0] = first_factor[tile]
        result[0, 1] = jnp.zeros((tile_rows, BLOCK), jnp.float32)
        result[1, 0] = own_cross[...]
        result[1, 1] = second_factor[tile]
        for t in range(2, NT):
            rows = slice((t - 2) * tile_rows, (t - 1) * tile_rows)
            result[t, 0] = own[rows, 0:BLOCK]
            result[t, 1] = own[rows, BLOCK:]
        for copy in copies():
            copy.wait()

    @pl.when(step > 0)
    def _():
        here = pl.ds(pl.multiple_of((step - 1) * width, width), width)

        def lower_dot(side, parts):
            upper_side = jnp.concatenate(
                [side[0:half, k * order : k * order + half] for k in range(len(parts))], axis=1
            )
            upper = fast_dot(upper_side, jnp.concatenate([part[0:half] for part in parts]))
            lower = fast_dot(side[half:order, :], jnp.concatenate(parts))
            return jnp.concatenate([upper, lower])

        given = given_cols[0:order, here]
        first = lower_dot(first_side, [given, given]).astype(jnp.bfloat16)
        left_over = given_cols[order:, here].astype(jnp.float32) - fast_dot(cross[...], first)
        high, low = split(left_over)
        second = lower_dot(second_side, [high, low, high]).astype(jnp.bfloat16)
        begin = 2 * tile_rows
        product = fast_dot(rounded[...], jnp.concatenate([first, second]))
        kept = natural[begin:, :].astype(jnp.float32) - product
        for s in range(2):
            for t in range(NT):
                if t < 2:
                    result[t, s] = jnp.zeros((tile_rows, BLOCK), jnp.float32)
                else:
                    result[t, s] = kept[
                        (t - 2) * tile_rows : (t - 1) * tile_rows, s * BLOCK : (s + 1) * BLOCK
                    ]


def solve_cols(place, natural, evens, odds, factors, rounded, own, own_cross, tile_rows):
    chips = len(evens)
    square = whole((P_SIZE, P_SIZE))
    return pl.pallas_call(
        functools.partial(cols_kernel, chips),
        grid=(NT // 2,),
        in_specs=[
            pl.BlockSpec(memory_space=pltpu.SMEM),
            pl.BlockSpec((NT * tile_rows, 2 * BLOCK), lambda j: (0, j)),
            *[pl.BlockSpec(memory_space=pl.ANY)] * (chips + 1),
            *[square] * 5,
            whole(rounded.shape),
            whole(own.shape),
            whole(own_cross.shape),
        ],
        out_specs=pl.BlockSpec((NT, 2, tile_rows, BLOCK), lambda j: (0, j, 0, 0)),
        out_shape=jax.ShapeDtypeStruct((NT, NT, tile_rows, BLOCK), jnp.float32),
        scratch_shapes=[
            pltpu.VMEM((2 * P_SIZE, (NT - 2) * BLOCK), jnp.bfloat16),
            pltpu.VMEM((P_SIZE, 2 * P_SIZE), jnp.bfloat16),
            pltpu.VMEM((P_SIZE, 3 * P_SIZE), jnp.bfloat16),
            pltpu.SemaphoreType.DMA((4 * chips,)),
        ],
        compiler_params=pltpu.CompilerParams(vmem_limit_bytes=40 * 2**20),
        cost_estimate=pl.CostEstimate(
            flops=10 * 10**9, bytes_accessed=24 * 2**20, transcendentals=0
        ),
    )(place, natural, *evens, odds, *factors, rounded, own, own_cross)


def swap(value, axis, offset):
    count = lax.axis_size(axis)
    return lax.ppermute(value, axis, [(i, i ^ offset) for i in range(count)])


def double(value, axis, offsets):
    value = value[None]
    for offset in offsets:
        value = jnp.concatenate([value, swap(value, axis, offset)])
    return value


def powers(begin, count):
    offsets = []
    while begin < count:
        offsets.append(begin)
        begin *= 2
    return offsets


def per_device(kernel):
    row_count = lax.axis_size("row")
    col_count = lax.axis_size("col")
    tile_rows = P_SIZE // row_count
    if P_SIZE != col_count * BLOCK or tile_rows % STEP:
        return per_device_general(kernel)
    place = jnp.stack([lax.axis_index("row"), lax.axis_index("col")]).astype(jnp.int32)
    tiles = kernel.reshape(NT, NT, tile_rows * BLOCK)
    corner, top = take_top(tiles, tile_rows)
    natural, left = take_natural(tiles, tile_rows)
    chips = range(2, row_count, 2)
    over_cols = double(corner, "col", powers(1, col_count))
    near = double(over_cols[:, 0:1], "row", powers(2, row_count))
    far = swap(near, "row", 1)
    other, left, near, far = lax.optimization_barrier((over_cols[:, 1:], left, near, far))
    other_near = [other] + [swap(other, "row", d) for d in chips]
    lefts = {0: left}
    for d in range(1, col_count):
        if d != 2:
            lefts[d] = swap(left, "col", d)
    first_factor, first_inverse = factor_call(
        first_kernel, place, (near, far), (), [], 40 * 10**9
    )
    others = [lefts[d] for d in sorted(lefts) if d]
    *other_near, top, left, first_inverse = lax.optimization_barrier(
        (*other_near, top, left, first_inverse, *others)
    )[: len(other_near) + 3]
    other_near = jnp.stack(other_near)
    other_far = swap(other_near, "row", 1)
    if col_count > 2:
        lefts[2] = swap(left, "col", 2)
    lefts = [lefts[d] for d in range(col_count)]
    evens = [top] + [swap(top, "row", d) for d in chips]
    extra = [
        jax.ShapeDtypeStruct((P_SIZE, P_SIZE), jnp.bfloat16),
        jax.ShapeDtypeStruct((tile_rows, BLOCK), jnp.float32),
    ]
    second_factor, second_inverse, cross, own_cross = factor_call(
        second_kernel, place, (other_near, other_far), (first_inverse,), extra, 40 * 10**9
    )
    *evens, second_inverse, lefts[2 % col_count] = lax.optimization_barrier(
        (*evens, second_inverse, lefts[2 % col_count])
    )
    odds = swap(jnp.stack(evens), "row", 1)
    rounded, own = solve_rows(place, lefts, first_inverse, second_inverse, cross)
    factors = (first_factor, first_inverse, second_factor, second_inverse, cross)
    result = solve_cols(
        place, natural, evens, odds, factors, rounded, own, own_cross, tile_rows
    )
    return result.reshape(kernel.shape)


def solution(mesh):
    placed = P(None, "row", None, "col", None)
    return jax.shard_map(
        per_device, mesh=mesh, in_specs=(placed,), out_specs=placed, check_vma=False
    )
```

```python
import functools

import jax
import jax.numpy as jnp
from jax import lax
from jax.experimental import pallas as pl
from jax.experimental.pallas import tpu as pltpu
from jax.sharding import PartitionSpec as P

P_SIZE = 512
NT = 16
STEP = 16
BLOCK = 128
EXACT = lax.Precision.HIGHEST


def exact_dot(left_side, right_side, contract=((1,), (0,))):
    return lax.dot_general(
        left_side,
        right_side,
        (contract, ((), ())),
        preferred_element_type=jnp.float32,
        precision=EXACT,
    )


def split(value):
    high = value.astype(jnp.bfloat16)
    return high, (value - high.astype(jnp.float32)).astype(jnp.bfloat16)


def split_three(value):
    high = value.astype(jnp.bfloat16)
    value = value - high.astype(jnp.float32)
    return high, *split(value)


def fast_dot(left_side, right_side, contract=((1,), (0,))):
    return lax.dot_general(
        left_side, right_side, (contract, ((), ())), preferred_element_type=jnp.float32
    )


def repeat_columns(rows, start):
    slot = lax.broadcasted_iota(jnp.int32, rows.shape, 1) // STEP
    spread_out = rows if start == 0 else pltpu.roll(rows, BLOCK - start, 1)
    at_start = spread_out
    for place in range(1, 6):
        spread_out = jnp.where(slot == place, pltpu.roll(at_start, place * STEP, 1), spread_out)
    high, middle, low = (part.astype(jnp.float32) for part in split_three(spread_out))
    parts = jnp.where(slot < 3, high, jnp.where(slot < 5, middle, low))
    return jnp.where(slot < 6, parts, 0.0).astype(jnp.bfloat16)


def factor_block(work, done):
    row_id = lax.broadcasted_iota(jnp.int32, (STEP, BLOCK), 0)
    for start in range(0, BLOCK, STEP):
        here = slice(start, start + STEP)
        halves = [work[here, 0:BLOCK], work[here, BLOCK : 2 * BLOCK]]
        columns = [
            jnp.broadcast_to(halves[0][:, start + j : start + j + 1], (STEP, BLOCK))
            for j in range(STEP)
        ]
        if start + STEP < BLOCK:
            raw = repeat_columns(work[start + STEP :, 0:BLOCK], start)
        kept = [jnp.zeros((STEP, BLOCK), jnp.float32)] * 2
        pivots = jnp.ones((STEP, BLOCK), jnp.float32)
        for k in range(STEP):
            pivot = jnp.broadcast_to(columns[k][k : k + 1, :], (STEP, BLOCK))
            factors = jnp.where(row_id == k, 0.0, columns[k] * (1.0 / pivot))
            for j in range(k + 1, STEP):
                top = jnp.broadcast_to(columns[j][k : k + 1, :], (STEP, BLOCK))
                columns[j] = columns[j] - factors * top
            pivots = jnp.where(row_id == k, pivot, pivots)
            for h in range(2):
                top = jnp.broadcast_to(halves[h][k : k + 1, :], (STEP, BLOCK))
                kept[h] = jnp.where(row_id == k, top, kept[h])
                halves[h] = halves[h] - factors * top
        scale = lax.rsqrt(pivots)
        inverse = 1.0 / pivots
        for h in range(2):
            done[here, h * BLOCK : (h + 1) * BLOCK] = kept[h] * scale
        if start + STEP < BLOCK:
            solved = jnp.concatenate([halves[0] * inverse, halves[1] * inverse], axis=1)
            high, middle, low = split_three(solved)
            parts = jnp.concatenate(
                [high, middle, low, high, middle, high, jnp.zeros_like(high), jnp.zeros_like(high)]
            )
            work[start + STEP :, :] = work[start + STEP :, :] - fast_dot(raw, parts)


def factor_kernel(given, factor, inverse, rest, work, done):
    rest[...] = given[...]
    factor_rest(rest, factor, inverse, work, done)


def factor_rest(rest, factor, inverse, work, done):
    order = rest.shape[0]
    inverse[...] = jnp.zeros_like(inverse)
    factor[...] = jnp.zeros_like(factor)
    row_id = lax.broadcasted_iota(jnp.int32, (BLOCK, BLOCK), 0)
    column_id = lax.broadcasted_iota(jnp.int32, (BLOCK, BLOCK), 1)
    for start in range(0, order, BLOCK):
        here = slice(start, start + BLOCK)
        work[:, 0:BLOCK] = rest[here, here]
        work[:, BLOCK:] = (row_id == column_id).astype(jnp.float32)
        factor_block(work, done)
        factor[here, here] = jnp.where(column_id >= row_id, done[:, 0:BLOCK], 0.0).T
        block_inverse = done[:, BLOCK:]
        if start:
            inverse[here, 0:start] = exact_dot(block_inverse, inverse[here, 0:start])
        inverse[here, here] = block_inverse
        if start + BLOCK < order:
            after = slice(start + BLOCK, order)
            upper = exact_dot(block_inverse, rest[here, after])
            lower = upper.T
            factor[after, here] = lower
            rest[after, after] = rest[after, after] - exact_dot(lower, upper)
            so_far = slice(0, start + BLOCK)
            inverse[after, so_far] = inverse[after, so_far] - exact_dot(
                lower, inverse[here, so_far]
            )


def factor_scratch():
    return [
        pltpu.VMEM((P_SIZE, P_SIZE), jnp.float32),
        pltpu.VMEM((BLOCK, 2 * BLOCK), jnp.float32),
        pltpu.VMEM((BLOCK, 2 * BLOCK), jnp.float32),
    ]


def factor_corner(corner):
    order = corner.shape[0]
    square = jax.ShapeDtypeStruct((order, order), jnp.float32)
    return pl.pallas_call(
        factor_kernel,
        out_shape=[square, square],
        scratch_shapes=factor_scratch(),
        compiler_params=pltpu.CompilerParams(vmem_limit_bytes=20 * 2**20),
    )(corner)


def spread(value, axis, offsets):
    count = lax.axis_size(axis)
    parts = [value]
    for offset in offsets[1:]:
        parts.append(lax.ppermute(value, axis, [(i, i ^ offset) for i in range(count)]))
    return jnp.stack(parts)


def gather_corner(mine):
    row_count = lax.axis_size("row")
    col_count = lax.axis_size("col")
    row_index = lax.axis_index("row")
    column_index = lax.axis_index("col")
    over_cols = spread(mine, "col", list(range(col_count)))
    over_chips = spread(over_cols, "row", list(range(0, row_count, 2)))
    slots = spread(over_chips, "row", [0, 1])
    slots = slots.transpose(1, 0, 2, 3, 4, 5).reshape(row_count, col_count, *mine.shape)
    slots = jnp.take(slots, jnp.arange(row_count) ^ row_index, axis=0, mode="clip")
    slots = jnp.take(slots, jnp.arange(col_count) ^ column_index, axis=1, mode="clip")
    return slots.transpose(2, 0, 3, 1, 4).reshape(3, P_SIZE, P_SIZE)


def per_device_general(kernel):
    row_count = lax.axis_size("row")
    col_count = lax.axis_size("col")
    tile_rows = P_SIZE // row_count
    tile_cols = P_SIZE // col_count
    row_index = lax.axis_index("row")
    column_index = lax.axis_index("col")
    tiles = kernel.reshape(NT, NT, tile_rows, tile_cols)
    corner = gather_corner(jnp.stack([tiles[0, 0], tiles[1, 0], tiles[1, 1]]))
    own_rows = tiles[:, 0:2].transpose(0, 2, 1, 3).reshape(NT * tile_rows, 2 * tile_cols)
    own_rows = lax.all_gather(own_rows, "col", axis=0, tiled=False)
    own_rows = own_rows.reshape(col_count, NT * tile_rows, 2, tile_cols).transpose(1, 2, 0, 3)
    own_rows = own_rows.reshape(NT * tile_rows, 2, P_SIZE)
    own_cols = tiles[0:2].transpose(0, 2, 1, 3).reshape(2 * tile_rows, NT * tile_cols)
    own_cols = lax.all_gather(own_cols, "row", axis=0, tiled=False)
    own_cols = own_cols.reshape(row_count, 2, tile_rows, NT * tile_cols).transpose(1, 0, 2, 3)
    own_cols = own_cols.reshape(2, P_SIZE, NT * tile_cols)

    first_corner, cross_corner, second_corner = (corner[i].astype(jnp.float32) for i in range(3))
    first_factor, first_inverse = factor_corner(0.5 * (first_corner + first_corner.T))
    cross = exact_dot(cross_corner, first_inverse, ((1,), (1,))).astype(jnp.bfloat16)
    updated_corner = second_corner - fast_dot(cross, cross, ((1,), (1,)))
    second_factor, second_inverse = factor_corner(0.5 * (updated_corner + updated_corner.T))

    first_rows = exact_dot(
        own_rows[tile_rows:, 0].astype(jnp.float32), first_inverse, ((1,), (1,))
    )
    first_cols = exact_dot(first_inverse, own_cols[0, :, tile_cols:].astype(jnp.float32))
    first_rows_rounded = first_rows.astype(jnp.bfloat16)
    first_cols_rounded = first_cols.astype(jnp.bfloat16)
    second_rows = own_rows[2 * tile_rows :, 1].astype(jnp.float32) - fast_dot(
        first_rows_rounded[tile_rows:], cross, ((1,), (1,))
    )
    second_cols = own_cols[1, :, 2 * tile_cols :].astype(jnp.float32) - fast_dot(
        cross, first_cols_rounded[:, tile_cols:]
    )
    second_rows = exact_dot(second_rows, second_inverse, ((1,), (1,)))
    second_cols = exact_dot(second_inverse, second_cols)
    left_side = jnp.concatenate(
        [first_rows_rounded[tile_rows:], second_rows.astype(jnp.bfloat16)], axis=1
    )
    right_side = jnp.concatenate(
        [first_cols_rounded[:, tile_cols:], second_cols.astype(jnp.bfloat16)], axis=0
    )
    inner = NT - 2
    product = fast_dot(left_side, right_side).reshape(inner, tile_rows, inner, tile_cols)
    trailing = tiles[2:, 2:].astype(jnp.float32) - product.transpose(0, 2, 1, 3)
    own = (row_index * tile_rows, column_index * tile_cols)
    first_own = lax.dynamic_slice_in_dim(first_rows, own[1], tile_cols, 1)
    second_own = lax.dynamic_slice_in_dim(second_rows, own[1], tile_cols, 1)
    first_tile = lax.dynamic_slice(first_factor, own, (tile_rows, tile_cols))
    second_tile = lax.dynamic_slice(second_factor, own, (tile_rows, tile_cols))
    result = jnp.zeros(tiles.shape, jnp.float32)
    result = result.at[2:, 2:].set(trailing)
    result = result.at[0, 0].set(first_tile)
    result = result.at[1:, 0].set(first_own.reshape(NT - 1, tile_rows, tile_cols))
    result = result.at[1, 1].set(second_tile)
    result = result.at[2:, 1].set(second_own.reshape(NT - 2, tile_rows, tile_cols))
    return result.reshape(kernel.shape)


def whole(shape):
    return pl.BlockSpec(shape, lambda *_: (0,) * len(shape))


def natural_tile(tiles, spread_rows, tile_rows):
    for r in range(tile_rows):
        spread_rows[r * NT : (r + 1) * NT, :] = tiles[:, r * BLOCK : (r + 1) * BLOCK].astype(
            jnp.float32
        )


def top_kernel(tiles, corner, top, held, spread_rows, copied):
    tile_rows = corner.shape[1]
    copies = [pltpu.make_async_copy(tiles.at[t], held.at[t], copied.at[t]) for t in range(2)]
    for copy in copies:
        copy.start()
    for t in range(2):
        copies[t].wait()
        natural_tile(held[t], spread_rows, tile_rows)
        for s in range(NT):
            tile = spread_rows[pl.ds(s, tile_rows, stride=NT), :].astype(jnp.bfloat16)
            if s >= 2:
                here = slice((s - 2) * BLOCK, (s - 1) * BLOCK)
                top[t * tile_rows : (t + 1) * tile_rows, here] = tile
            elif s <= t:
                corner[t + s] = tile


def natural_kernel(tiles, natural, left, spread_rows):
    group = tiles.shape[0]
    tile_rows = natural.shape[0] // group
    step = pl.program_id(0)
    for t in range(group):
        natural_tile(tiles[t], spread_rows, tile_rows)
        rows = slice(t * tile_rows, (t + 1) * tile_rows)
        for s in range(NT):
            tile = spread_rows[pl.ds(s, tile_rows, stride=NT), :].astype(jnp.bfloat16)
            natural[rows, s * BLOCK : (s + 1) * BLOCK] = tile
            if s < 2:
                first = pl.multiple_of(jnp.maximum(step * group + t - 2, 0) * tile_rows, tile_rows)
                left[pl.ds(first, tile_rows), s * BLOCK : (s + 1) * BLOCK] = tile


def take_top(tiles, tile_rows):
    return pl.pallas_call(
        top_kernel,
        in_specs=[pl.BlockSpec(memory_space=pltpu.HBM)],
        out_shape=[
            jax.ShapeDtypeStruct((3, tile_rows, BLOCK), jnp.bfloat16),
            jax.ShapeDtypeStruct((2 * tile_rows, (NT - 2) * BLOCK), jnp.bfloat16),
        ],
        scratch_shapes=[
            pltpu.VMEM((2, NT, tile_rows * BLOCK), jnp.bfloat16),
            pltpu.VMEM((tile_rows * NT, BLOCK), jnp.float32),
            pltpu.SemaphoreType.DMA((2,)),
        ],
        compiler_params=pltpu.CompilerParams(vmem_limit_bytes=16 * 2**20),
    )(tiles)


def take_natural(tiles, tile_rows):
    group = 4
    below = ((NT - 2) * tile_rows, 2 * BLOCK)
    return pl.pallas_call(
        natural_kernel,
        grid=(NT // group,),
        in_specs=[pl.BlockSpec((group, NT, tile_rows * BLOCK), lambda t: (t, 0, 0))],
        out_specs=[
            pl.BlockSpec((group * tile_rows, NT * BLOCK), lambda t: (t, 0)),
            whole(below),
        ],
        out_shape=[
            jax.ShapeDtypeStruct((NT * tile_rows, NT * BLOCK), jnp.bfloat16),
            jax.ShapeDtypeStruct(below, jnp.bfloat16),
        ],
        scratch_shapes=[pltpu.VMEM((tile_rows * NT, BLOCK), jnp.float32)],
        compiler_params=pltpu.CompilerParams(vmem_limit_bytes=16 * 2**20),
        cost_estimate=pl.CostEstimate(
            flops=0, bytes_accessed=16 * NT * tile_rows * NT * BLOCK, transcendentals=0
        ),
    )(tiles)


def place_corner(place, slots, which, corner):
    row_index, column_index = place[0], place[1]
    chips, col_count, _, tile_rows, _ = slots[0].shape
    for core, held in enumerate(slots):
        for chip in range(chips):
            first_row = pl.multiple_of((row_index ^ (2 * chip + core)) * tile_rows, tile_rows)
            for col in range(col_count):
                first_col = pl.multiple_of((column_index ^ col) * BLOCK, BLOCK)
                corner[pl.ds(first_row, tile_rows), pl.ds(first_col, BLOCK)] = held[
                    chip, col, which
                ].astype(jnp.float32)


def first_kernel(place, near, far, factor, inverse, rest, work, done):
    place_corner(place, (near, far), 0, rest)
    factor_rest(rest, factor, inverse, work, done)


def second_kernel(
    place, near, far, first_inverse, factor, inverse, cross, own, rest, work, done
):
    place_corner(place, (near, far), 0, rest)
    given = rest[...].astype(jnp.bfloat16)
    high, low = split(first_inverse[...])
    solved = fast_dot(
        jnp.concatenate([given, given], axis=1),
        jnp.concatenate([high, low], axis=1),
        ((1,), (1,)),
    )
    rest[...] = solved
    tile_rows, tile_cols = own.shape
    own[...] = rest[
        pl.ds(pl.multiple_of(place[0] * tile_rows, tile_rows), tile_rows),
        pl.ds(pl.multiple_of(place[1] * tile_cols, tile_cols), tile_cols),
    ]
    solved = solved.astype(jnp.bfloat16)
    cross[...] = solved
    place_corner(place, (near, far), 1, rest)
    rest[...] = rest[...] - fast_dot(solved, solved, ((1,), (1,)))
    factor_rest(rest, factor, inverse, work, done)


def factor_call(body, place, slots, extra, extra_out, cost):
    square = jax.ShapeDtypeStruct((P_SIZE, P_SIZE), jnp.float32)
    on_vmem = pl.BlockSpec(memory_space=pltpu.VMEM)
    return pl.pallas_call(
        body,
        in_specs=[pl.BlockSpec(memory_space=pltpu.SMEM)] + [on_vmem] * (2 + len(extra)),
        out_shape=[square, square] + extra_out,
        scratch_shapes=factor_scratch(),
        compiler_params=pltpu.CompilerParams(vmem_limit_bytes=20 * 2**20),
        cost_estimate=pl.CostEstimate(
            flops=cost, bytes_accessed=4 * 2**20, transcendentals=0
        ),
    )(place, *slots, *extra)


def rows_kernel(place, *refs):
    lefts = refs[:-9]
    first_inverse, second_inverse, cross, rounded, own, *scratch = refs[-9:]
    first_side, cross_side, second_side, solved_rows = scratch
    column_index = place[1]
    own_col = pl.multiple_of(column_index * BLOCK, BLOCK)
    order = P_SIZE

    @pl.when(pl.program_id(0) == 0)
    def _():
        for offset in range(len(lefts)):
            first = pl.multiple_of((column_index ^ offset) * BLOCK, BLOCK)
            here = pl.ds(first, BLOCK)
            for k in range(3):
                to = slice(k * order + offset * BLOCK, k * order + (offset + 1) * BLOCK)
                if k < 2:
                    first_side[to, :] = split(first_inverse[:, here].T)[k]
                second_side[to, :] = split(second_inverse[:, here].T)[k // 2]
            to = slice(offset * BLOCK, (offset + 1) * BLOCK)
            cross_side[:, to] = cross[here, :].astype(jnp.float32).T.astype(jnp.bfloat16)

    given = [left[:, 0:BLOCK] for left in lefts]
    solved = fast_dot(jnp.concatenate(given + given, axis=1), first_side[...])
    solved_rows[:, 0:order] = solved
    first_rounded = solved.astype(jnp.bfloat16)
    given = jnp.concatenate([left[:, BLOCK : 2 * BLOCK] for left in lefts], axis=1)
    left_over = given.astype(jnp.float32) - fast_dot(first_rounded, cross_side[...])
    high, low = split(left_over)
    solved = fast_dot(jnp.concatenate([high, low, high], axis=1), second_side[...])
    solved_rows[:, order:] = solved
    rounded[:, 0:order] = first_rounded
    rounded[:, order:] = solved.astype(jnp.bfloat16)
    own[:, 0:BLOCK] = solved_rows[:, pl.ds(own_col, BLOCK)]
    own[:, BLOCK:] = solved_rows[:, pl.ds(order + own_col, BLOCK)]


def solve_rows(place, lefts, first_inverse, second_inverse, cross):
    count = lefts[0].shape[0]
    rows = count
    square = whole((P_SIZE, P_SIZE))
    return pl.pallas_call(
        rows_kernel,
        grid=(count // rows,),
        in_specs=[
            pl.BlockSpec(memory_space=pltpu.SMEM),
            *[pl.BlockSpec((rows, 2 * BLOCK), lambda i: (i, 0)) for _ in lefts],
            *[square] * 3,
        ],
        out_specs=[
            pl.BlockSpec((rows, 2 * P_SIZE), lambda i: (i, 0)),
            pl.BlockSpec((rows, 2 * BLOCK), lambda i: (i, 0)),
        ],
        out_shape=[
            jax.ShapeDtypeStruct((count, 2 * P_SIZE), jnp.bfloat16),
            jax.ShapeDtypeStruct((count, 2 * BLOCK), jnp.float32),
        ],
        scratch_shapes=[
            pltpu.VMEM((2 * P_SIZE, P_SIZE), jnp.bfloat16),
            pltpu.VMEM((P_SIZE, P_SIZE), jnp.bfloat16),
            pltpu.VMEM((3 * P_SIZE, P_SIZE), jnp.bfloat16),
            pltpu.VMEM((rows, 2 * P_SIZE), jnp.float32),
        ],
        compiler_params=pltpu.CompilerParams(vmem_limit_bytes=24 * 2**20),
        cost_estimate=pl.CostEstimate(
            flops=12 * count * P_SIZE**2, bytes_accessed=10 * 2**20, transcendentals=0
        ),
    )(place, *lefts, first_inverse, second_inverse, cross)


def cols_kernel(chips, place, natural, *refs):
    evens, odds = refs[:chips], refs[chips]
    first_factor, first_inverse, second_factor, second_inverse, cross = refs[chips + 1 : chips + 6]
    rounded, own, own_cross, result = refs[chips + 6 : chips + 10]
    given_cols, solved_cols, first_side, second_side, copied = refs[chips + 10 :]
    row_index, column_index = place[0], place[1]
    tile_rows = evens[0].shape[0] // 2
    order = P_SIZE
    step = pl.program_id(0)
    group = result.shape[1]
    count = given_cols.shape[1]

    def copies():
        for chip in range(chips):
            for core in range(2):
                source = odds.at[chip] if core else evens[chip]
                first = pl.multiple_of((row_index ^ (2 * chip + core)) * tile_rows, tile_rows)
                for t in range(2):
                    yield pltpu.make_async_copy(
                        source.at[pl.ds(t * tile_rows, tile_rows), :],
                        given_cols.at[pl.ds(t * order + first, tile_rows), :],
                        copied.at[(2 * chip + core) * 2 + t],
                    )

    def write(first_col, tile_cols):
        here = pl.ds(pl.multiple_of(first_col, BLOCK), tile_cols * BLOCK)
        skipped = (group - tile_cols) * BLOCK
        product = fast_dot(rounded[...], solved_cols[:, here])
        kept = natural[2 * tile_rows :, skipped:].astype(jnp.float32) - product
        for s in range(tile_cols):
            at = group - tile_cols + s
            for t in range(2):
                result[t, at] = jnp.zeros((tile_rows, BLOCK), jnp.float32)
            for t in range(2, NT):
                result[t, at] = kept[
                    (t - 2) * tile_rows : (t - 1) * tile_rows, s * BLOCK : (s + 1) * BLOCK
                ]

    @pl.when(step == 0)
    def _():
        for copy in copies():
            copy.start()
        high, low = split(first_inverse[...])
        first_side[:, 0:order] = high
        first_side[:, order:] = low
        high, low = split(second_inverse[...])
        second_side[:, 0:order] = high
        second_side[:, order : 2 * order] = high
        second_side[:, 2 * order :] = low
        own_row = pl.multiple_of(row_index * tile_rows, tile_rows)
        own_col = pl.multiple_of(column_index * BLOCK, BLOCK)
        tile = (pl.ds(own_row, tile_rows), pl.ds(own_col, BLOCK))
        result[0, 0] = first_factor[tile]
        result[0, 1] = jnp.zeros((tile_rows, BLOCK), jnp.float32)
        result[1, 0] = own_cross[...]
        result[1, 1] = second_factor[tile]
        for t in range(2, NT):
            rows = slice((t - 2) * tile_rows, (t - 1) * tile_rows)
            result[t, 0] = own[rows, 0:BLOCK]
            result[t, 1] = own[rows, BLOCK:]
        for copy in copies():
            copy.wait()
        begin = 0
        while begin < count:
            width = min(1024, count - begin)
            here = slice(begin, begin + width)
            begin += width
            given = given_cols[0:order, here]
            first = fast_dot(first_side[...], jnp.concatenate([given, given]))
            first = first.astype(jnp.bfloat16)
            solved_cols[0:order, here] = first
            left_over = given_cols[order:, here].astype(jnp.float32) - fast_dot(cross[...], first)
            high, low = split(left_over)
            second = fast_dot(second_side[...], jnp.concatenate([high, low, high]))
            solved_cols[order:, here] = second.astype(jnp.bfloat16)
        write(0, group - 2)

    @pl.when(step > 0)
    def _():
        write((step * group - 2) * BLOCK, group)


def solve_cols(place, natural, evens, odds, factors, rounded, own, own_cross, tile_rows):
    chips = len(evens)
    group = 4
    square = whole((P_SIZE, P_SIZE))
    solved = pltpu.VMEM((2 * P_SIZE, (NT - 2) * BLOCK), jnp.bfloat16)
    return pl.pallas_call(
        functools.partial(cols_kernel, chips),
        grid=(NT // group,),
        in_specs=[
            pl.BlockSpec(memory_space=pltpu.SMEM),
            pl.BlockSpec((NT * tile_rows, group * BLOCK), lambda j: (0, j)),
            *[pl.BlockSpec(memory_space=pl.ANY)] * (chips + 1),
            *[square] * 5,
            whole(rounded.shape),
            whole(own.shape),
            whole(own_cross.shape),
        ],
        out_specs=pl.BlockSpec((NT, group, tile_rows, BLOCK), lambda j: (0, j, 0, 0)),
        out_shape=jax.ShapeDtypeStruct((NT, NT, tile_rows, BLOCK), jnp.float32),
        scratch_shapes=[
            solved,
            solved,
            pltpu.VMEM((P_SIZE, 2 * P_SIZE), jnp.bfloat16),
            pltpu.VMEM((P_SIZE, 3 * P_SIZE), jnp.bfloat16),
            pltpu.SemaphoreType.DMA((4 * chips,)),
        ],
        compiler_params=pltpu.CompilerParams(vmem_limit_bytes=38 * 2**20),
        cost_estimate=pl.CostEstimate(
            flops=10 * 10**9, bytes_accessed=24 * 2**20, transcendentals=0
        ),
    )(place, natural, *evens, odds, *factors, rounded, own, own_cross)


def swap(value, axis, offset):
    count = lax.axis_size(axis)
    return lax.ppermute(value, axis, [(i, i ^ offset) for i in range(count)])


def double(value, axis, offsets):
    value = value[None]
    for offset in offsets:
        value = jnp.concatenate([value, swap(value, axis, offset)])
    return value


def powers(begin, count):
    offsets = []
    while begin < count:
        offsets.append(begin)
        begin *= 2
    return offsets


def per_device(kernel):
    row_count = lax.axis_size("row")
    col_count = lax.axis_size("col")
    tile_rows = P_SIZE // row_count
    if P_SIZE != col_count * BLOCK or tile_rows % STEP:
        return per_device_general(kernel)
    place = jnp.stack([lax.axis_index("row"), lax.axis_index("col")]).astype(jnp.int32)
    tiles = kernel.reshape(NT, NT, tile_rows * BLOCK)
    corner, top = take_top(tiles, tile_rows)
    natural, left = take_natural(tiles, tile_rows)
    chips = range(2, row_count, 2)
    over_cols = double(corner, "col", powers(1, col_count))
    near = double(over_cols[:, 0:1], "row", powers(2, row_count))
    far = swap(near, "row", 1)
    other, left, near, far = lax.optimization_barrier((over_cols[:, 1:], left, near, far))
    other_near = [other] + [swap(other, "row", d) for d in chips]
    lefts = {0: left}
    for d in range(1, col_count):
        if d != 2:
            lefts[d] = swap(left, "col", d)
    first_factor, first_inverse = factor_call(
        first_kernel, place, (near, far), (), [], 40 * 10**9
    )
    others = [lefts[d] for d in sorted(lefts) if d]
    *other_near, top, left, first_inverse = lax.optimization_barrier(
        (*other_near, top, left, first_inverse, *others)
    )[: len(other_near) + 3]
    other_near = jnp.stack(other_near)
    other_far = swap(other_near, "row", 1)
    if col_count > 2:
        lefts[2] = swap(left, "col", 2)
    lefts = [lefts[d] for d in range(col_count)]
    evens = [top] + [swap(top, "row", d) for d in chips]
    extra = [
        jax.ShapeDtypeStruct((P_SIZE, P_SIZE), jnp.bfloat16),
        jax.ShapeDtypeStruct((tile_rows, BLOCK), jnp.float32),
    ]
    second_factor, second_inverse, cross, own_cross = factor_call(
        second_kernel, place, (other_near, other_far), (first_inverse,), extra, 40 * 10**9
    )
    *evens, second_inverse, lefts[2 % col_count] = lax.optimization_barrier(
        (*evens, second_inverse, lefts[2 % col_count])
    )
    odds = swap(jnp.stack(evens), "row", 1)
    rounded, own = solve_rows(place, lefts, first_inverse, second_inverse, cross)
    factors = (first_factor, first_inverse, second_factor, second_inverse, cross)
    result = solve_cols(
        place, natural, evens, odds, factors, rounded, own, own_cross, tile_rows
    )
    return result.reshape(kernel.shape)


def solution(mesh):
    placed = P(None, "row", None, "col", None)
    return jax.shard_map(
        per_device, mesh=mesh, in_specs=(placed,), out_specs=placed, check_vma=False
    )
```

```python
import functools

import jax
import jax.numpy as jnp
from jax import lax
from jax.experimental import pallas as pl
from jax.experimental.pallas import tpu as pltpu
from jax.sharding import PartitionSpec as P

P_SIZE = 512
NT = 16
STEP = 16
BLOCK = 128
EXACT = lax.Precision.HIGHEST


def exact_dot(left_side, right_side, contract=((1,), (0,))):
    return lax.dot_general(
        left_side,
        right_side,
        (contract, ((), ())),
        preferred_element_type=jnp.float32,
        precision=EXACT,
    )


def split(value):
    high = value.astype(jnp.bfloat16)
    return high, (value - high.astype(jnp.float32)).astype(jnp.bfloat16)


def split_three(value):
    high = value.astype(jnp.bfloat16)
    value = value - high.astype(jnp.float32)
    return high, *split(value)


def fast_dot(left_side, right_side, contract=((1,), (0,))):
    return lax.dot_general(
        left_side, right_side, (contract, ((), ())), preferred_element_type=jnp.float32
    )


def repeat_columns(rows, start):
    slot = lax.broadcasted_iota(jnp.int32, rows.shape, 1) // STEP
    spread_out = rows if start == 0 else pltpu.roll(rows, BLOCK - start, 1)
    at_start = spread_out
    for place in range(1, 6):
        spread_out = jnp.where(slot == place, pltpu.roll(at_start, place * STEP, 1), spread_out)
    high, middle, low = (part.astype(jnp.float32) for part in split_three(spread_out))
    parts = jnp.where(slot < 3, high, jnp.where(slot < 5, middle, low))
    return jnp.where(slot < 6, parts, 0.0).astype(jnp.bfloat16)


def factor_block(work, done):
    row_id = lax.broadcasted_iota(jnp.int32, (STEP, BLOCK), 0)
    for start in range(0, BLOCK, STEP):
        here = slice(start, start + STEP)
        halves = [work[here, 0:BLOCK], work[here, BLOCK : 2 * BLOCK]]
        columns = [
            jnp.broadcast_to(halves[0][:, start + j : start + j + 1], (STEP, BLOCK))
            for j in range(STEP)
        ]
        if start + STEP < BLOCK:
            raw = repeat_columns(work[start + STEP :, 0:BLOCK], start)
        kept = [jnp.zeros((STEP, BLOCK), jnp.float32)] * 2
        pivots = jnp.ones((STEP, BLOCK), jnp.float32)
        for k in range(STEP):
            pivot = jnp.broadcast_to(columns[k][k : k + 1, :], (STEP, BLOCK))
            factors = jnp.where(row_id == k, 0.0, columns[k] * (1.0 / pivot))
            for j in range(k + 1, STEP):
                top = jnp.broadcast_to(columns[j][k : k + 1, :], (STEP, BLOCK))
                columns[j] = columns[j] - factors * top
            pivots = jnp.where(row_id == k, pivot, pivots)
            for h in range(2):
                top = jnp.broadcast_to(halves[h][k : k + 1, :], (STEP, BLOCK))
                kept[h] = jnp.where(row_id == k, top, kept[h])
                halves[h] = halves[h] - factors * top
        scale = lax.rsqrt(pivots)
        inverse = 1.0 / pivots
        for h in range(2):
            done[here, h * BLOCK : (h + 1) * BLOCK] = kept[h] * scale
        if start + STEP < BLOCK:
            solved = jnp.concatenate([halves[0] * inverse, halves[1] * inverse], axis=1)
            high, middle, low = split_three(solved)
            parts = jnp.concatenate(
                [high, middle, low, high, middle, high, jnp.zeros_like(high), jnp.zeros_like(high)]
            )
            work[start + STEP :, :] = work[start + STEP :, :] - fast_dot(raw, parts)


def factor_kernel(given, factor, inverse, rest, work, done):
    rest[...] = given[...]
    factor_rest(rest, factor, inverse, work, done)


def factor_rest(rest, factor, inverse, work, done):
    order = rest.shape[0]
    inverse[...] = jnp.zeros_like(inverse)
    factor[...] = jnp.zeros_like(factor)
    row_id = lax.broadcasted_iota(jnp.int32, (BLOCK, BLOCK), 0)
    column_id = lax.broadcasted_iota(jnp.int32, (BLOCK, BLOCK), 1)
    for start in range(0, order, BLOCK):
        here = slice(start, start + BLOCK)
        work[:, 0:BLOCK] = rest[here, here]
        work[:, BLOCK:] = (row_id == column_id).astype(jnp.float32)
        factor_block(work, done)
        factor[here, here] = jnp.where(column_id >= row_id, done[:, 0:BLOCK], 0.0).T
        block_inverse = done[:, BLOCK:]
        if start:
            inverse[here, 0:start] = exact_dot(block_inverse, inverse[here, 0:start])
        inverse[here, here] = block_inverse
        if start + BLOCK < order:
            after = slice(start + BLOCK, order)
            upper = exact_dot(block_inverse, rest[here, after])
            lower = upper.T
            factor[after, here] = lower
            rest[after, after] = rest[after, after] - exact_dot(lower, upper)
            so_far = slice(0, start + BLOCK)
            inverse[after, so_far] = inverse[after, so_far] - exact_dot(
                lower, inverse[here, so_far]
            )


def factor_scratch():
    return [
        pltpu.VMEM((P_SIZE, P_SIZE), jnp.float32),
        pltpu.VMEM((BLOCK, 2 * BLOCK), jnp.float32),
        pltpu.VMEM((BLOCK, 2 * BLOCK), jnp.float32),
    ]


def factor_corner(corner):
    order = corner.shape[0]
    square = jax.ShapeDtypeStruct((order, order), jnp.float32)
    return pl.pallas_call(
        factor_kernel,
        out_shape=[square, square],
        scratch_shapes=factor_scratch(),
        compiler_params=pltpu.CompilerParams(vmem_limit_bytes=20 * 2**20),
    )(corner)


def spread(value, axis, offsets):
    count = lax.axis_size(axis)
    parts = [value]
    for offset in offsets[1:]:
        parts.append(lax.ppermute(value, axis, [(i, i ^ offset) for i in range(count)]))
    return jnp.stack(parts)


def gather_corner(mine):
    row_count = lax.axis_size("row")
    col_count = lax.axis_size("col")
    row_index = lax.axis_index("row")
    column_index = lax.axis_index("col")
    over_cols = spread(mine, "col", list(range(col_count)))
    over_chips = spread(over_cols, "row", list(range(0, row_count, 2)))
    slots = spread(over_chips, "row", [0, 1])
    slots = slots.transpose(1, 0, 2, 3, 4, 5).reshape(row_count, col_count, *mine.shape)
    slots = jnp.take(slots, jnp.arange(row_count) ^ row_index, axis=0, mode="clip")
    slots = jnp.take(slots, jnp.arange(col_count) ^ column_index, axis=1, mode="clip")
    return slots.transpose(2, 0, 3, 1, 4).reshape(3, P_SIZE, P_SIZE)


def per_device_general(kernel):
    row_count = lax.axis_size("row")
    col_count = lax.axis_size("col")
    tile_rows = P_SIZE // row_count
    tile_cols = P_SIZE // col_count
    row_index = lax.axis_index("row")
    column_index = lax.axis_index("col")
    tiles = kernel.reshape(NT, NT, tile_rows, tile_cols)
    corner = gather_corner(jnp.stack([tiles[0, 0], tiles[1, 0], tiles[1, 1]]))
    own_rows = tiles[:, 0:2].transpose(0, 2, 1, 3).reshape(NT * tile_rows, 2 * tile_cols)
    own_rows = lax.all_gather(own_rows, "col", axis=0, tiled=False)
    own_rows = own_rows.reshape(col_count, NT * tile_rows, 2, tile_cols).transpose(1, 2, 0, 3)
    own_rows = own_rows.reshape(NT * tile_rows, 2, P_SIZE)
    own_cols = tiles[0:2].transpose(0, 2, 1, 3).reshape(2 * tile_rows, NT * tile_cols)
    own_cols = lax.all_gather(own_cols, "row", axis=0, tiled=False)
    own_cols = own_cols.reshape(row_count, 2, tile_rows, NT * tile_cols).transpose(1, 0, 2, 3)
    own_cols = own_cols.reshape(2, P_SIZE, NT * tile_cols)

    first_corner, cross_corner, second_corner = (corner[i].astype(jnp.float32) for i in range(3))
    first_factor, first_inverse = factor_corner(0.5 * (first_corner + first_corner.T))
    cross = exact_dot(cross_corner, first_inverse, ((1,), (1,))).astype(jnp.bfloat16)
    updated_corner = second_corner - fast_dot(cross, cross, ((1,), (1,)))
    second_factor, second_inverse = factor_corner(0.5 * (updated_corner + updated_corner.T))

    first_rows = exact_dot(
        own_rows[tile_rows:, 0].astype(jnp.float32), first_inverse, ((1,), (1,))
    )
    first_cols = exact_dot(first_inverse, own_cols[0, :, tile_cols:].astype(jnp.float32))
    first_rows_rounded = first_rows.astype(jnp.bfloat16)
    first_cols_rounded = first_cols.astype(jnp.bfloat16)
    second_rows = own_rows[2 * tile_rows :, 1].astype(jnp.float32) - fast_dot(
        first_rows_rounded[tile_rows:], cross, ((1,), (1,))
    )
    second_cols = own_cols[1, :, 2 * tile_cols :].astype(jnp.float32) - fast_dot(
        cross, first_cols_rounded[:, tile_cols:]
    )
    second_rows = exact_dot(second_rows, second_inverse, ((1,), (1,)))
    second_cols = exact_dot(second_inverse, second_cols)
    left_side = jnp.concatenate(
        [first_rows_rounded[tile_rows:], second_rows.astype(jnp.bfloat16)], axis=1
    )
    right_side = jnp.concatenate(
        [first_cols_rounded[:, tile_cols:], second_cols.astype(jnp.bfloat16)], axis=0
    )
    inner = NT - 2
    product = fast_dot(left_side, right_side).reshape(inner, tile_rows, inner, tile_cols)
    trailing = tiles[2:, 2:].astype(jnp.float32) - product.transpose(0, 2, 1, 3)
    own = (row_index * tile_rows, column_index * tile_cols)
    first_own = lax.dynamic_slice_in_dim(first_rows, own[1], tile_cols, 1)
    second_own = lax.dynamic_slice_in_dim(second_rows, own[1], tile_cols, 1)
    first_tile = lax.dynamic_slice(first_factor, own, (tile_rows, tile_cols))
    second_tile = lax.dynamic_slice(second_factor, own, (tile_rows, tile_cols))
    result = jnp.zeros(tiles.shape, jnp.float32)
    result = result.at[2:, 2:].set(trailing)
    result = result.at[0, 0].set(first_tile)
    result = result.at[1:, 0].set(first_own.reshape(NT - 1, tile_rows, tile_cols))
    result = result.at[1, 1].set(second_tile)
    result = result.at[2:, 1].set(second_own.reshape(NT - 2, tile_rows, tile_cols))
    return result.reshape(kernel.shape)


def whole(shape):
    return pl.BlockSpec(shape, lambda *_: (0,) * len(shape))


def natural_tile(tiles, spread_rows, tile_rows):
    for r in range(tile_rows):
        spread_rows[r * NT : (r + 1) * NT, :] = tiles[:, r * BLOCK : (r + 1) * BLOCK].astype(
            jnp.float32
        )


def top_kernel(tiles, corner, top, held, spread_rows, copied):
    tile_rows = corner.shape[1]
    copies = [pltpu.make_async_copy(tiles.at[t], held.at[t], copied.at[t]) for t in range(2)]
    for copy in copies:
        copy.start()
    for t in range(2):
        copies[t].wait()
        natural_tile(held[t], spread_rows, tile_rows)
        for s in range(NT):
            tile = spread_rows[pl.ds(s, tile_rows, stride=NT), :].astype(jnp.bfloat16)
            if s >= 2:
                here = slice((s - 2) * BLOCK, (s - 1) * BLOCK)
                top[t * tile_rows : (t + 1) * tile_rows, here] = tile
            elif s <= t:
                corner[t + s] = tile


def natural_kernel(tiles, natural, left, spread_rows, held, copied):
    tile_rows = natural.shape[0] // NT
    group = 4
    copies = []
    for t in range(NT):
        natural_tile(tiles[t], spread_rows, tile_rows)
        for s in range(NT):
            tile = spread_rows[pl.ds(s, tile_rows, stride=NT), :].astype(jnp.bfloat16)
            held[t * tile_rows : (t + 1) * tile_rows, s * BLOCK : (s + 1) * BLOCK] = tile
            if s < 2 <= t:
                rows = slice((t - 2) * tile_rows, (t - 1) * tile_rows)
                left[rows, s * BLOCK : (s + 1) * BLOCK] = tile
        if t % group == group - 1:
            rows = pl.ds((t + 1 - group) * tile_rows, group * tile_rows)
            copies.append(
                pltpu.make_async_copy(held.at[rows], natural.at[rows], copied.at[t // group])
            )
            copies[-1].start()
    for copy in copies:
        copy.wait()


def take_top(tiles, tile_rows):
    return pl.pallas_call(
        top_kernel,
        in_specs=[pl.BlockSpec(memory_space=pltpu.HBM)],
        out_shape=[
            jax.ShapeDtypeStruct((3, tile_rows, BLOCK), jnp.bfloat16),
            jax.ShapeDtypeStruct((2 * tile_rows, (NT - 2) * BLOCK), jnp.bfloat16),
        ],
        scratch_shapes=[
            pltpu.VMEM((2, NT, tile_rows * BLOCK), jnp.bfloat16),
            pltpu.VMEM((tile_rows * NT, BLOCK), jnp.float32),
            pltpu.SemaphoreType.DMA((2,)),
        ],
        compiler_params=pltpu.CompilerParams(vmem_limit_bytes=16 * 2**20),
    )(tiles)


def take_natural(tiles, tile_rows):
    shape = (NT * tile_rows, NT * BLOCK)
    return pl.pallas_call(
        natural_kernel,
        in_specs=[pl.BlockSpec(memory_space=pltpu.VMEM)],
        out_specs=[
            pl.BlockSpec(memory_space=pltpu.HBM),
            pl.BlockSpec(memory_space=pltpu.VMEM),
        ],
        out_shape=[
            jax.ShapeDtypeStruct(shape, jnp.bfloat16),
            jax.ShapeDtypeStruct(((NT - 2) * tile_rows, 2 * BLOCK), jnp.bfloat16),
        ],
        scratch_shapes=[
            pltpu.VMEM((tile_rows * NT, BLOCK), jnp.float32),
            pltpu.VMEM(shape, jnp.bfloat16),
            pltpu.SemaphoreType.DMA((NT // 4,)),
        ],
        compiler_params=pltpu.CompilerParams(vmem_limit_bytes=24 * 2**20),
        cost_estimate=pl.CostEstimate(
            flops=0, bytes_accessed=16 * NT * tile_rows * NT * BLOCK, transcendentals=0
        ),
    )(tiles)


def place_corner(place, slots, which, corner):
    row_index, column_index = place[0], place[1]
    chips, col_count, _, tile_rows, _ = slots[0].shape
    for core, held in enumerate(slots):
        for chip in range(chips):
            first_row = pl.multiple_of((row_index ^ (2 * chip + core)) * tile_rows, tile_rows)
            for col in range(col_count):
                first_col = pl.multiple_of((column_index ^ col) * BLOCK, BLOCK)
                corner[pl.ds(first_row, tile_rows), pl.ds(first_col, BLOCK)] = held[
                    chip, col, which
                ].astype(jnp.float32)


def first_kernel(place, near, far, factor, inverse, rest, work, done):
    place_corner(place, (near, far), 0, rest)
    factor_rest(rest, factor, inverse, work, done)


def second_kernel(
    place, near, far, first_inverse, factor, inverse, cross, own, rest, work, done
):
    place_corner(place, (near, far), 0, rest)
    given = rest[...].astype(jnp.bfloat16)
    high, low = split(first_inverse[...])
    solved = fast_dot(
        jnp.concatenate([given, given], axis=1),
        jnp.concatenate([high, low], axis=1),
        ((1,), (1,)),
    )
    rest[...] = solved
    tile_rows, tile_cols = own.shape
    own[...] = rest[
        pl.ds(pl.multiple_of(place[0] * tile_rows, tile_rows), tile_rows),
        pl.ds(pl.multiple_of(place[1] * tile_cols, tile_cols), tile_cols),
    ]
    solved = solved.astype(jnp.bfloat16)
    cross[...] = solved
    place_corner(place, (near, far), 1, rest)
    rest[...] = rest[...] - fast_dot(solved, solved, ((1,), (1,)))
    factor_rest(rest, factor, inverse, work, done)


def factor_call(body, place, slots, extra, extra_out, cost):
    square = jax.ShapeDtypeStruct((P_SIZE, P_SIZE), jnp.float32)
    on_vmem = pl.BlockSpec(memory_space=pltpu.VMEM)
    return pl.pallas_call(
        body,
        in_specs=[pl.BlockSpec(memory_space=pltpu.SMEM)] + [on_vmem] * (2 + len(extra)),
        out_shape=[square, square] + extra_out,
        scratch_shapes=factor_scratch(),
        compiler_params=pltpu.CompilerParams(vmem_limit_bytes=20 * 2**20),
        cost_estimate=pl.CostEstimate(
            flops=cost, bytes_accessed=4 * 2**20, transcendentals=0
        ),
    )(place, *slots, *extra)


def rows_kernel(place, *refs):
    lefts = refs[:-9]
    first_inverse, second_inverse, cross, rounded, own, *scratch = refs[-9:]
    first_side, cross_side, second_side, solved_rows = scratch
    column_index = place[1]
    own_col = pl.multiple_of(column_index * BLOCK, BLOCK)
    order = P_SIZE

    @pl.when(pl.program_id(0) == 0)
    def _():
        for offset in range(len(lefts)):
            first = pl.multiple_of((column_index ^ offset) * BLOCK, BLOCK)
            here = pl.ds(first, BLOCK)
            for k in range(3):
                to = slice(k * order + offset * BLOCK, k * order + (offset + 1) * BLOCK)
                if k < 2:
                    first_side[to, :] = split(first_inverse[:, here].T)[k]
                second_side[to, :] = split(second_inverse[:, here].T)[k // 2]
            to = slice(offset * BLOCK, (offset + 1) * BLOCK)
            cross_side[:, to] = cross[here, :].astype(jnp.float32).T.astype(jnp.bfloat16)

    given = [left[:, 0:BLOCK] for left in lefts]
    solved = fast_dot(jnp.concatenate(given + given, axis=1), first_side[...])
    solved_rows[:, 0:order] = solved
    first_rounded = solved.astype(jnp.bfloat16)
    given = jnp.concatenate([left[:, BLOCK : 2 * BLOCK] for left in lefts], axis=1)
    left_over = given.astype(jnp.float32) - fast_dot(first_rounded, cross_side[...])
    high, low = split(left_over)
    solved = fast_dot(jnp.concatenate([high, low, high], axis=1), second_side[...])
    solved_rows[:, order:] = solved
    rounded[:, 0:order] = first_rounded
    rounded[:, order:] = solved.astype(jnp.bfloat16)
    own[:, 0:BLOCK] = solved_rows[:, pl.ds(own_col, BLOCK)]
    own[:, BLOCK:] = solved_rows[:, pl.ds(order + own_col, BLOCK)]


def solve_rows(place, lefts, first_inverse, second_inverse, cross):
    count = lefts[0].shape[0]
    rows = count
    square = whole((P_SIZE, P_SIZE))
    return pl.pallas_call(
        rows_kernel,
        grid=(count // rows,),
        in_specs=[
            pl.BlockSpec(memory_space=pltpu.SMEM),
            *[pl.BlockSpec((rows, 2 * BLOCK), lambda i: (i, 0)) for _ in lefts],
            *[square] * 3,
        ],
        out_specs=[
            pl.BlockSpec((rows, 2 * P_SIZE), lambda i: (i, 0)),
            pl.BlockSpec((rows, 2 * BLOCK), lambda i: (i, 0)),
        ],
        out_shape=[
            jax.ShapeDtypeStruct((count, 2 * P_SIZE), jnp.bfloat16),
            jax.ShapeDtypeStruct((count, 2 * BLOCK), jnp.float32),
        ],
        scratch_shapes=[
            pltpu.VMEM((2 * P_SIZE, P_SIZE), jnp.bfloat16),
            pltpu.VMEM((P_SIZE, P_SIZE), jnp.bfloat16),
            pltpu.VMEM((3 * P_SIZE, P_SIZE), jnp.bfloat16),
            pltpu.VMEM((rows, 2 * P_SIZE), jnp.float32),
        ],
        compiler_params=pltpu.CompilerParams(vmem_limit_bytes=24 * 2**20),
        cost_estimate=pl.CostEstimate(
            flops=12 * count * P_SIZE**2, bytes_accessed=10 * 2**20, transcendentals=0
        ),
    )(place, *lefts, first_inverse, second_inverse, cross)


def cols_kernel(chips, place, natural, *refs):
    evens, odds = refs[:chips], refs[chips]
    first_factor, first_inverse, second_factor, second_inverse, cross = refs[chips + 1 : chips + 6]
    rounded, own, own_cross, result = refs[chips + 6 : chips + 10]
    given_cols, solved_cols, first_side, second_side, copied = refs[chips + 10 :]
    row_index, column_index = place[0], place[1]
    tile_rows = evens[0].shape[0] // 2
    order = P_SIZE
    step = pl.program_id(0)
    group = result.shape[1]
    count = given_cols.shape[1]

    def copies():
        for chip in range(chips):
            for core in range(2):
                source = odds.at[chip] if core else evens[chip]
                first = pl.multiple_of((row_index ^ (2 * chip + core)) * tile_rows, tile_rows)
                for t in range(2):
                    yield pltpu.make_async_copy(
                        source.at[pl.ds(t * tile_rows, tile_rows), :],
                        given_cols.at[pl.ds(t * order + first, tile_rows), :],
                        copied.at[(2 * chip + core) * 2 + t],
                    )

    def write(first_col, tile_cols):
        here = pl.ds(pl.multiple_of(first_col, BLOCK), tile_cols * BLOCK)
        skipped = (group - tile_cols) * BLOCK
        product = fast_dot(rounded[...], solved_cols[:, here])
        kept = natural[2 * tile_rows :, skipped:].astype(jnp.float32) - product
        for s in range(tile_cols):
            at = group - tile_cols + s
            for t in range(2):
                result[t, at] = jnp.zeros((tile_rows, BLOCK), jnp.float32)
            for t in range(2, NT):
                result[t, at] = kept[
                    (t - 2) * tile_rows : (t - 1) * tile_rows, s * BLOCK : (s + 1) * BLOCK
                ]

    @pl.when(step == 0)
    def _():
        for copy in copies():
            copy.start()
        high, low = split(first_inverse[...])
        first_side[:, 0:order] = high
        first_side[:, order:] = low
        high, low = split(second_inverse[...])
        second_side[:, 0:order] = high
        second_side[:, order : 2 * order] = high
        second_side[:, 2 * order :] = low
        own_row = pl.multiple_of(row_index * tile_rows, tile_rows)
        own_col = pl.multiple_of(column_index * BLOCK, BLOCK)
        tile = (pl.ds(own_row, tile_rows), pl.ds(own_col, BLOCK))
        result[0, 0] = first_factor[tile]
        result[0, 1] = jnp.zeros((tile_rows, BLOCK), jnp.float32)
        result[1, 0] = own_cross[...]
        result[1, 1] = second_factor[tile]
        for t in range(2, NT):
            rows = slice((t - 2) * tile_rows, (t - 1) * tile_rows)
            result[t, 0] = own[rows, 0:BLOCK]
            result[t, 1] = own[rows, BLOCK:]
        for copy in copies():
            copy.wait()
        begin = 0
        while begin < count:
            width = min(1024, count - begin)
            here = slice(begin, begin + width)
            begin += width
            given = given_cols[0:order, here]
            first = fast_dot(first_side[...], jnp.concatenate([given, given]))
            first = first.astype(jnp.bfloat16)
            solved_cols[0:order, here] = first
            left_over = given_cols[order:, here].astype(jnp.float32) - fast_dot(cross[...], first)
            high, low = split(left_over)
            second = fast_dot(second_side[...], jnp.concatenate([high, low, high]))
            solved_cols[order:, here] = second.astype(jnp.bfloat16)
        write(0, group - 2)

    @pl.when(step > 0)
    def _():
        write((step * group - 2) * BLOCK, group)


def solve_cols(place, natural, evens, odds, factors, rounded, own, own_cross, tile_rows):
    chips = len(evens)
    group = 4
    square = whole((P_SIZE, P_SIZE))
    solved = pltpu.VMEM((2 * P_SIZE, (NT - 2) * BLOCK), jnp.bfloat16)
    return pl.pallas_call(
        functools.partial(cols_kernel, chips),
        grid=(NT // group,),
        in_specs=[
            pl.BlockSpec(memory_space=pltpu.SMEM),
            pl.BlockSpec((NT * tile_rows, group * BLOCK), lambda j: (0, j)),
            *[pl.BlockSpec(memory_space=pl.ANY)] * (chips + 1),
            *[square] * 5,
            whole(rounded.shape),
            whole(own.shape),
            whole(own_cross.shape),
        ],
        out_specs=pl.BlockSpec((NT, group, tile_rows, BLOCK), lambda j: (0, j, 0, 0)),
        out_shape=jax.ShapeDtypeStruct((NT, NT, tile_rows, BLOCK), jnp.float32),
        scratch_shapes=[
            solved,
            solved,
            pltpu.VMEM((P_SIZE, 2 * P_SIZE), jnp.bfloat16),
            pltpu.VMEM((P_SIZE, 3 * P_SIZE), jnp.bfloat16),
            pltpu.SemaphoreType.DMA((4 * chips,)),
        ],
        compiler_params=pltpu.CompilerParams(vmem_limit_bytes=38 * 2**20),
        cost_estimate=pl.CostEstimate(
            flops=10 * 10**9, bytes_accessed=24 * 2**20, transcendentals=0
        ),
    )(place, natural, *evens, odds, *factors, rounded, own, own_cross)


def swap(value, axis, offset):
    count = lax.axis_size(axis)
    return lax.ppermute(value, axis, [(i, i ^ offset) for i in range(count)])


def per_device(kernel):
    row_count = lax.axis_size("row")
    col_count = lax.axis_size("col")
    tile_rows = P_SIZE // row_count
    if P_SIZE != col_count * BLOCK or tile_rows % STEP:
        return per_device_general(kernel)
    place = jnp.stack([lax.axis_index("row"), lax.axis_index("col")]).astype(jnp.int32)
    tiles = kernel.reshape(NT, NT, tile_rows * BLOCK)
    corner, top = take_top(tiles, tile_rows)
    natural, left = take_natural(tiles, tile_rows)
    chips = range(2, row_count, 2)
    over_cols = jnp.stack([corner] + [swap(corner, "col", d) for d in range(1, col_count)])
    over_cols, left = lax.optimization_barrier((over_cols, left))
    first = over_cols[:, 0:1]
    near = jnp.stack([first] + [swap(first, "row", d) for d in chips])
    lefts = {0: left}
    for d in range(1, col_count):
        if d != 2:
            lefts[d] = swap(left, "col", d)
    near, other = lax.optimization_barrier((near, over_cols[:, 1:]))
    far = swap(near, "row", 1)
    other_near = [other] + [swap(other, "row", d) for d in chips]
    first_factor, first_inverse = factor_call(
        first_kernel, place, (near, far), (), [], 40 * 10**9
    )
    others = [lefts[d] for d in sorted(lefts) if d]
    *other_near, top, left, first_inverse = lax.optimization_barrier(
        (*other_near, top, left, first_inverse, *others)
    )[: len(other_near) + 3]
    other_near = jnp.stack(other_near)
    other_far = swap(other_near, "row", 1)
    if col_count > 2:
        lefts[2] = swap(left, "col", 2)
    lefts = [lefts[d] for d in range(col_count)]
    evens = [top] + [swap(top, "row", d) for d in chips]
    extra = [
        jax.ShapeDtypeStruct((P_SIZE, P_SIZE), jnp.bfloat16),
        jax.ShapeDtypeStruct((tile_rows, BLOCK), jnp.float32),
    ]
    second_factor, second_inverse, cross, own_cross = factor_call(
        second_kernel, place, (other_near, other_far), (first_inverse,), extra, 40 * 10**9
    )
    *evens, second_inverse, lefts[2 % col_count] = lax.optimization_barrier(
        (*evens, second_inverse, lefts[2 % col_count])
    )
    odds = swap(jnp.stack(evens), "row", 1)
    rounded, own = solve_rows(place, lefts, first_inverse, second_inverse, cross)
    factors = (first_factor, first_inverse, second_factor, second_inverse, cross)
    result = solve_cols(
        place, natural, evens, odds, factors, rounded, own, own_cross, tile_rows
    )
    return result.reshape(kernel.shape)


def solution(mesh):
    placed = P(None, "row", None, "col", None)
    return jax.shard_map(
        per_device, mesh=mesh, in_specs=(placed,), out_specs=placed, check_vma=False
    )
```

```python
import functools

import jax
import jax.numpy as jnp
from jax import lax
from jax.experimental import pallas as pl
from jax.experimental.pallas import tpu as pltpu
from jax.sharding import PartitionSpec as P

P_SIZE = 512
NT = 16
STEP = 16
BLOCK = 128
EXACT = lax.Precision.HIGHEST


def exact_dot(left_side, right_side, contract=((1,), (0,))):
    return lax.dot_general(
        left_side,
        right_side,
        (contract, ((), ())),
        preferred_element_type=jnp.float32,
        precision=EXACT,
    )


def split(value):
    high = value.astype(jnp.bfloat16)
    return high, (value - high.astype(jnp.float32)).astype(jnp.bfloat16)


def split_three(value):
    high = value.astype(jnp.bfloat16)
    value = value - high.astype(jnp.float32)
    return high, *split(value)


def fast_dot(left_side, right_side, contract=((1,), (0,))):
    return lax.dot_general(
        left_side, right_side, (contract, ((), ())), preferred_element_type=jnp.float32
    )


def repeat_columns(rows, start):
    slots = BLOCK // STEP
    slot = lax.broadcasted_iota(jnp.int32, rows.shape, 1) // STEP
    slot = (slot + (slots - start // STEP)) % slots
    spread_out = rows
    for place in range(1, 6):
        spread_out = jnp.where(slot == place, pltpu.roll(rows, place * STEP, 1), spread_out)
    high, middle, low = (part.astype(jnp.float32) for part in split_three(spread_out))
    parts = jnp.where(slot < 3, high, jnp.where(slot < 5, middle, low))
    return jnp.where(slot < 6, parts, 0.0).astype(jnp.bfloat16)


def factor_block(work, done):
    row_id = lax.broadcasted_iota(jnp.int32, (STEP, BLOCK), 0)
    for start in range(0, BLOCK, STEP):
        here = slice(start, start + STEP)
        halves = [work[here, 0:BLOCK], work[here, BLOCK : 2 * BLOCK]]
        columns = [
            jnp.broadcast_to(halves[0][:, start + j : start + j + 1], (STEP, BLOCK))
            for j in range(STEP)
        ]
        if start + STEP < BLOCK:
            raw = repeat_columns(work[start + STEP :, 0:BLOCK], start)
        kept = [jnp.zeros((STEP, BLOCK), jnp.float32)] * 2
        pivots = jnp.ones((STEP, BLOCK), jnp.float32)
        for k in range(STEP):
            pivot = jnp.broadcast_to(columns[k][k : k + 1, :], (STEP, BLOCK))
            factors = jnp.where(row_id == k, 0.0, columns[k] * (1.0 / pivot))
            for j in range(k + 1, STEP):
                top = jnp.broadcast_to(columns[j][k : k + 1, :], (STEP, BLOCK))
                columns[j] = columns[j] - factors * top
            pivots = jnp.where(row_id == k, pivot, pivots)
            for h in range(2):
                top = jnp.broadcast_to(halves[h][k : k + 1, :], (STEP, BLOCK))
                kept[h] = jnp.where(row_id == k, top, kept[h])
                halves[h] = halves[h] - factors * top
        scale = lax.rsqrt(pivots)
        inverse = 1.0 / pivots
        for h in range(2):
            done[here, h * BLOCK : (h + 1) * BLOCK] = kept[h] * scale
        if start + STEP < BLOCK:
            solved = jnp.concatenate([halves[0] * inverse, halves[1] * inverse], axis=1)
            high, middle, low = split_three(solved)
            blank = jnp.zeros_like(high)
            parts = [high, middle, low, high, middle, high, blank, blank]
            slots = BLOCK // STEP
            parts = [parts[(at - start // STEP) % slots] for at in range(slots)]
            parts = jnp.concatenate(parts)
            after, later = start + STEP, start + 2 * STEP
            blocks = [(after, later, 0), (later, BLOCK, 0), (after, BLOCK, BLOCK)]
            for first, last, column in blocks:
                if first < last:
                    here = (slice(first, last), slice(column, column + BLOCK))
                    work[here] = work[here] - fast_dot(
                        raw[first - after : last - after], parts[:, column : column + BLOCK]
                    )


def factor_kernel(given, factor, inverse, rest, work, done):
    rest[...] = given[...]
    factor_rest(rest, factor, inverse, work, done)


def factor_rest(rest, factor, inverse, work, done):
    order = rest.shape[0]
    inverse[...] = jnp.zeros_like(inverse)
    factor[...] = jnp.zeros_like(factor)
    row_id = lax.broadcasted_iota(jnp.int32, (BLOCK, BLOCK), 0)
    column_id = lax.broadcasted_iota(jnp.int32, (BLOCK, BLOCK), 1)
    for start in range(0, order, BLOCK):
        here = slice(start, start + BLOCK)
        work[:, 0:BLOCK] = rest[here, here]
        work[:, BLOCK:] = (row_id == column_id).astype(jnp.float32)
        factor_block(work, done)
        factor[here, here] = jnp.where(column_id >= row_id, done[:, 0:BLOCK], 0.0).T
        block_inverse = done[:, BLOCK:]
        if start:
            inverse[here, 0:start] = exact_dot(block_inverse, inverse[here, 0:start])
        inverse[here, here] = block_inverse
        if start + BLOCK < order:
            after = slice(start + BLOCK, order)
            upper = exact_dot(block_inverse, rest[here, after])
            lower = upper.T
            factor[after, here] = lower
            rest[after, after] = rest[after, after] - exact_dot(lower, upper)
            so_far = slice(0, start + BLOCK)
            inverse[after, so_far] = inverse[after, so_far] - exact_dot(
                lower, inverse[here, so_far]
            )


def factor_scratch():
    return [
        pltpu.VMEM((P_SIZE, P_SIZE), jnp.float32),
        pltpu.VMEM((BLOCK, 2 * BLOCK), jnp.float32),
        pltpu.VMEM((BLOCK, 2 * BLOCK), jnp.float32),
    ]


def factor_corner(corner):
    order = corner.shape[0]
    square = jax.ShapeDtypeStruct((order, order), jnp.float32)
    return pl.pallas_call(
        factor_kernel,
        out_shape=[square, square],
        scratch_shapes=factor_scratch(),
        compiler_params=pltpu.CompilerParams(vmem_limit_bytes=20 * 2**20),
    )(corner)


def spread(value, axis, offsets):
    count = lax.axis_size(axis)
    parts = [value]
    for offset in offsets[1:]:
        parts.append(lax.ppermute(value, axis, [(i, i ^ offset) for i in range(count)]))
    return jnp.stack(parts)


def gather_corner(mine):
    row_count = lax.axis_size("row")
    col_count = lax.axis_size("col")
    row_index = lax.axis_index("row")
    column_index = lax.axis_index("col")
    over_cols = spread(mine, "col", list(range(col_count)))
    over_chips = spread(over_cols, "row", list(range(0, row_count, 2)))
    slots = spread(over_chips, "row", [0, 1])
    slots = slots.transpose(1, 0, 2, 3, 4, 5).reshape(row_count, col_count, *mine.shape)
    slots = jnp.take(slots, jnp.arange(row_count) ^ row_index, axis=0, mode="clip")
    slots = jnp.take(slots, jnp.arange(col_count) ^ column_index, axis=1, mode="clip")
    return slots.transpose(2, 0, 3, 1, 4).reshape(3, P_SIZE, P_SIZE)


def per_device_general(kernel):
    row_count = lax.axis_size("row")
    col_count = lax.axis_size("col")
    tile_rows = P_SIZE // row_count
    tile_cols = P_SIZE // col_count
    row_index = lax.axis_index("row")
    column_index = lax.axis_index("col")
    tiles = kernel.reshape(NT, NT, tile_rows, tile_cols)
    corner = gather_corner(jnp.stack([tiles[0, 0], tiles[1, 0], tiles[1, 1]]))
    own_rows = tiles[:, 0:2].transpose(0, 2, 1, 3).reshape(NT * tile_rows, 2 * tile_cols)
    own_rows = lax.all_gather(own_rows, "col", axis=0, tiled=False)
    own_rows = own_rows.reshape(col_count, NT * tile_rows, 2, tile_cols).transpose(1, 2, 0, 3)
    own_rows = own_rows.reshape(NT * tile_rows, 2, P_SIZE)
    own_cols = tiles[0:2].transpose(0, 2, 1, 3).reshape(2 * tile_rows, NT * tile_cols)
    own_cols = lax.all_gather(own_cols, "row", axis=0, tiled=False)
    own_cols = own_cols.reshape(row_count, 2, tile_rows, NT * tile_cols).transpose(1, 0, 2, 3)
    own_cols = own_cols.reshape(2, P_SIZE, NT * tile_cols)

    first_corner, cross_corner, second_corner = (corner[i].astype(jnp.float32) for i in range(3))
    first_factor, first_inverse = factor_corner(0.5 * (first_corner + first_corner.T))
    cross = exact_dot(cross_corner, first_inverse, ((1,), (1,))).astype(jnp.bfloat16)
    updated_corner = second_corner - fast_dot(cross, cross, ((1,), (1,)))
    second_factor, second_inverse = factor_corner(0.5 * (updated_corner + updated_corner.T))

    first_rows = exact_dot(
        own_rows[tile_rows:, 0].astype(jnp.float32), first_inverse, ((1,), (1,))
    )
    first_cols = exact_dot(first_inverse, own_cols[0, :, tile_cols:].astype(jnp.float32))
    first_rows_rounded = first_rows.astype(jnp.bfloat16)
    first_cols_rounded = first_cols.astype(jnp.bfloat16)
    second_rows = own_rows[2 * tile_rows :, 1].astype(jnp.float32) - fast_dot(
        first_rows_rounded[tile_rows:], cross, ((1,), (1,))
    )
    second_cols = own_cols[1, :, 2 * tile_cols :].astype(jnp.float32) - fast_dot(
        cross, first_cols_rounded[:, tile_cols:]
    )
    second_rows = exact_dot(second_rows, second_inverse, ((1,), (1,)))
    second_cols = exact_dot(second_inverse, second_cols)
    left_side = jnp.concatenate(
        [first_rows_rounded[tile_rows:], second_rows.astype(jnp.bfloat16)], axis=1
    )
    right_side = jnp.concatenate(
        [first_cols_rounded[:, tile_cols:], second_cols.astype(jnp.bfloat16)], axis=0
    )
    inner = NT - 2
    product = fast_dot(left_side, right_side).reshape(inner, tile_rows, inner, tile_cols)
    trailing = tiles[2:, 2:].astype(jnp.float32) - product.transpose(0, 2, 1, 3)
    own = (row_index * tile_rows, column_index * tile_cols)
    first_own = lax.dynamic_slice_in_dim(first_rows, own[1], tile_cols, 1)
    second_own = lax.dynamic_slice_in_dim(second_rows, own[1], tile_cols, 1)
    first_tile = lax.dynamic_slice(first_factor, own, (tile_rows, tile_cols))
    second_tile = lax.dynamic_slice(second_factor, own, (tile_rows, tile_cols))
    result = jnp.zeros(tiles.shape, jnp.float32)
    result = result.at[2:, 2:].set(trailing)
    result = result.at[0, 0].set(first_tile)
    result = result.at[1:, 0].set(first_own.reshape(NT - 1, tile_rows, tile_cols))
    result = result.at[1, 1].set(second_tile)
    result = result.at[2:, 1].set(second_own.reshape(NT - 2, tile_rows, tile_cols))
    return result.reshape(kernel.shape)


def whole(shape):
    return pl.BlockSpec(shape, lambda *_: (0,) * len(shape))


def natural_tile(tiles, spread_rows, tile_rows):
    for r in range(tile_rows):
        spread_rows[r * NT : (r + 1) * NT, :] = tiles[:, r * BLOCK : (r + 1) * BLOCK].astype(
            jnp.float32
        )


def top_kernel(tiles, corner, top, held, spread_rows, copied):
    tile_rows = corner.shape[1]
    copies = [pltpu.make_async_copy(tiles.at[t], held.at[t], copied.at[t]) for t in range(2)]
    for copy in copies:
        copy.start()
    for t in range(2):
        copies[t].wait()
        natural_tile(held[t], spread_rows, tile_rows)
        for s in range(NT):
            tile = spread_rows[pl.ds(s, tile_rows, stride=NT), :].astype(jnp.bfloat16)
            if s >= 2:
                here = slice((s - 2) * BLOCK, (s - 1) * BLOCK)
                top[t * tile_rows : (t + 1) * tile_rows, here] = tile
            elif s <= t:
                corner[t + s] = tile


def left_kernel(tiles, left, spread_rows):
    tile_rows = left.shape[0] // (NT - 2)
    half = NT // 2
    for t in range(2, NT):
        for r in range(tile_rows):
            part = tiles[t, :, r * BLOCK : (r + 1) * BLOCK].astype(jnp.float32)
            spread_rows[r * half : (r + 1) * half, :] = part[0:half]
        rows = slice((t - 2) * tile_rows, (t - 1) * tile_rows)
        for s in range(2):
            tile = spread_rows[pl.ds(s, tile_rows, stride=half), :].astype(jnp.bfloat16)
            left[rows, s * BLOCK : (s + 1) * BLOCK] = tile


def take_top(tiles, tile_rows):
    return pl.pallas_call(
        top_kernel,
        in_specs=[pl.BlockSpec(memory_space=pltpu.HBM)],
        out_shape=[
            jax.ShapeDtypeStruct((3, tile_rows, BLOCK), jnp.bfloat16),
            jax.ShapeDtypeStruct((2 * tile_rows, (NT - 2) * BLOCK), jnp.bfloat16),
        ],
        scratch_shapes=[
            pltpu.VMEM((2, NT, tile_rows * BLOCK), jnp.bfloat16),
            pltpu.VMEM((tile_rows * NT, BLOCK), jnp.float32),
            pltpu.SemaphoreType.DMA((2,)),
        ],
        compiler_params=pltpu.CompilerParams(vmem_limit_bytes=16 * 2**20),
    )(tiles)


def take_left(tiles, tile_rows):
    on_vmem = pl.BlockSpec(memory_space=pltpu.VMEM)
    return pl.pallas_call(
        left_kernel,
        in_specs=[on_vmem],
        out_specs=on_vmem,
        out_shape=jax.ShapeDtypeStruct(((NT - 2) * tile_rows, 2 * BLOCK), jnp.bfloat16),
        scratch_shapes=[pltpu.VMEM((tile_rows * NT // 2, BLOCK), jnp.float32)],
        compiler_params=pltpu.CompilerParams(vmem_limit_bytes=16 * 2**20),
        cost_estimate=pl.CostEstimate(
            flops=0, bytes_accessed=2 * NT * tile_rows * NT * BLOCK, transcendentals=0
        ),
    )(tiles)


def place_corner(place, slots, which, corner):
    row_index, column_index = place[0], place[1]
    chips, col_count, _, tile_rows, _ = slots[0].shape
    for core, held in enumerate(slots):
        for chip in range(chips):
            first_row = pl.multiple_of((row_index ^ (2 * chip + core)) * tile_rows, tile_rows)
            for col in range(col_count):
                first_col = pl.multiple_of((column_index ^ col) * BLOCK, BLOCK)
                corner[pl.ds(first_row, tile_rows), pl.ds(first_col, BLOCK)] = held[
                    chip, col, which
                ].astype(jnp.float32)


def own_tile(place, matrix, tile):
    tile_rows, tile_cols = tile.shape
    first_row = pl.multiple_of(place[0] * tile_rows, tile_rows)
    first_col = pl.multiple_of(place[1] * tile_cols, tile_cols)
    tile[...] = matrix[pl.ds(first_row, tile_rows), pl.ds(first_col, tile_cols)]


def first_kernel(place, near, far, own, side, inverse, rest, work, done, factor):
    place_corner(place, (near, far), 0, rest)
    factor_rest(rest, factor, inverse, work, done)
    own_tile(place, factor, own)
    order = rest.shape[0]
    high, low = split(inverse[...])
    side[:, 0:order] = high
    side[:, order:] = low


def second_kernel(
    place, near, far, first_side, own, side, inverse, cross, own_cross, rest, work, done, factor
):
    place_corner(place, (near, far), 0, rest)
    given = rest[...].astype(jnp.bfloat16)
    solved = fast_dot(jnp.concatenate([given, given], axis=1), first_side[...], ((1,), (1,)))
    rest[...] = solved
    own_tile(place, rest, own_cross)
    solved = solved.astype(jnp.bfloat16)
    cross[...] = solved
    place_corner(place, (near, far), 1, rest)
    rest[...] = rest[...] - fast_dot(solved, solved, ((1,), (1,)))
    factor_rest(rest, factor, inverse, work, done)
    own_tile(place, factor, own)
    order = rest.shape[0]
    high, low = split(inverse[...])
    side[:, 0:order] = high
    side[:, order : 2 * order] = high
    side[:, 2 * order :] = low


def factor_call(body, place, slots, extra, out_shape, cost):
    on_vmem = pl.BlockSpec(memory_space=pltpu.VMEM)
    square = pltpu.VMEM((P_SIZE, P_SIZE), jnp.float32)
    return pl.pallas_call(
        body,
        in_specs=[pl.BlockSpec(memory_space=pltpu.SMEM)] + [on_vmem] * (2 + len(extra)),
        out_shape=out_shape,
        scratch_shapes=[*factor_scratch(), square],
        compiler_params=pltpu.CompilerParams(vmem_limit_bytes=20 * 2**20),
        cost_estimate=pl.CostEstimate(
            flops=cost, bytes_accessed=4 * 2**20, transcendentals=0
        ),
    )(place, *slots, *extra)


def rows_kernel(place, *refs):
    lefts = refs[:-9]
    first_inverse, second_inverse, cross, rounded, own, *scratch = refs[-9:]
    first_side, cross_side, second_side, solved_rows = scratch
    column_index = place[1]
    own_col = pl.multiple_of(column_index * BLOCK, BLOCK)
    order = P_SIZE

    @pl.when(pl.program_id(0) == 0)
    def _():
        for offset in range(len(lefts)):
            first = pl.multiple_of((column_index ^ offset) * BLOCK, BLOCK)
            here = pl.ds(first, BLOCK)
            to = [
                slice(k * order + offset * BLOCK, k * order + (offset + 1) * BLOCK)
                for k in range(3)
            ]
            high, low = split(first_inverse[:, here].T)
            first_side[to[0], :] = high
            first_side[to[1], :] = low
            high, low = split(second_inverse[:, here].T)
            second_side[to[0], :] = high
            second_side[to[1], :] = high
            second_side[to[2], :] = low
            cross_side[:, to[0]] = cross[here, :].astype(jnp.float32).T.astype(jnp.bfloat16)

    given = [left[:, 0:BLOCK] for left in lefts]
    solved = fast_dot(jnp.concatenate(given + given, axis=1), first_side[...])
    solved_rows[:, 0:order] = solved
    first_rounded = solved.astype(jnp.bfloat16)
    given = jnp.concatenate([left[:, BLOCK : 2 * BLOCK] for left in lefts], axis=1)
    left_over = given.astype(jnp.float32) - fast_dot(first_rounded, cross_side[...])
    high, low = split(left_over)
    solved = fast_dot(jnp.concatenate([high, low, high], axis=1), second_side[...])
    solved_rows[:, order:] = solved
    rounded[:, 0:order] = first_rounded
    rounded[:, order:] = solved.astype(jnp.bfloat16)
    own[:, 0:BLOCK] = solved_rows[:, pl.ds(own_col, BLOCK)]
    own[:, BLOCK:] = solved_rows[:, pl.ds(order + own_col, BLOCK)]


def solve_rows(place, lefts, first_inverse, second_inverse, cross):
    count = lefts[0].shape[0]
    on_vmem = pl.BlockSpec(memory_space=pltpu.VMEM)
    return pl.pallas_call(
        rows_kernel,
        grid=(1,),
        in_specs=[pl.BlockSpec(memory_space=pltpu.SMEM)] + [on_vmem] * (len(lefts) + 3),
        out_shape=[
            jax.ShapeDtypeStruct((count, 2 * P_SIZE), jnp.bfloat16),
            jax.ShapeDtypeStruct((count, 2 * BLOCK), jnp.float32),
        ],
        scratch_shapes=[
            pltpu.VMEM((2 * P_SIZE, P_SIZE), jnp.bfloat16),
            pltpu.VMEM((P_SIZE, P_SIZE), jnp.bfloat16),
            pltpu.VMEM((3 * P_SIZE, P_SIZE), jnp.bfloat16),
            pltpu.VMEM((count, 2 * P_SIZE), jnp.float32),
        ],
        compiler_params=pltpu.CompilerParams(vmem_limit_bytes=24 * 2**20),
        cost_estimate=pl.CostEstimate(
            flops=12 * count * P_SIZE**2, bytes_accessed=10 * 2**20, transcendentals=0
        ),
    )(place, *lefts, first_inverse, second_inverse, cross)


def cols_kernel(chips, place, tiles, *refs):
    evens, odds = refs[:chips], refs[chips]
    first_own, first_side, second_own, second_side, cross, own_cross = refs[chips + 1 : chips + 7]
    rounded, own, result = refs[chips + 7 : chips + 10]
    given_cols, solved_cols, spread_rows, held, gone = refs[chips + 10 :]
    tile_rows = own_cross.shape[0]
    order = P_SIZE
    group = 4
    count = given_cols.shape[1]
    blank = jnp.zeros((tile_rows, BLOCK), jnp.float32)
    leaving = []

    def send(begin, end):
        for t in range(NT):
            here = (t, pl.ds(begin, end - begin))
            copy = pltpu.make_async_copy(held.at[here], result.at[here], gone.at[begin // 2, t])
            copy.start()
            leaving.append(copy)

    held[0, 0] = first_own[...]
    held[0, 1] = blank
    held[1, 0] = own_cross[...]
    held[1, 1] = second_own[...]
    for t in range(2, NT):
        rows = slice((t - 2) * tile_rows, (t - 1) * tile_rows)
        held[t, 0] = own[rows, 0:BLOCK]
        held[t, 1] = own[rows, BLOCK:]
    send(0, 2)
    for chip in range(chips):
        for core in range(2):
            source = odds.at[chip] if core else evens[chip]
            first = pl.multiple_of((place[0] ^ (2 * chip + core)) * tile_rows, tile_rows)
            for t in range(2):
                given_cols[pl.ds(t * order + first, tile_rows), :] = source[
                    t * tile_rows : (t + 1) * tile_rows, :
                ]
    for t in range(2, NT):
        natural_tile(tiles[t], spread_rows.at[t - 2], tile_rows)
    width = 1024
    for first_col in range(0, count, width):
        last_col = min(first_col + width, count)
        here = slice(first_col, last_col)
        given = given_cols[0:order, here]
        first = fast_dot(first_side[...], jnp.concatenate([given, given]))
        first = first.astype(jnp.bfloat16)
        solved_cols[0:order, here] = first
        left_over = given_cols[order:, here].astype(jnp.float32) - fast_dot(cross[...], first)
        high, low = split(left_over)
        second = fast_dot(second_side[...], jnp.concatenate([high, low, high]))
        solved_cols[order:, here] = second.astype(jnp.bfloat16)
        for begin in range(first_col, last_col, group * BLOCK):
            end = min(begin + group * BLOCK, last_col)
            product = fast_dot(rounded[...], solved_cols[:, begin:end])
            for column in range(begin, end, BLOCK):
                s = column // BLOCK + 2
                held[0, s] = blank
                held[1, s] = blank
                for t in range(2, NT):
                    rows = slice((t - 2) * tile_rows, (t - 1) * tile_rows)
                    held[t, s] = (
                        spread_rows[t - 2, pl.ds(s, tile_rows, stride=NT), :]
                        - product[rows, column - begin : column - begin + BLOCK]
                    )
            send(begin // BLOCK + 2, end // BLOCK + 2)
    for copy in leaving:
        copy.wait()


def solve_cols(place, tiles, evens, odds, corners, rounded, own, tile_rows):
    chips = len(evens)
    on_vmem = pl.BlockSpec(memory_space=pltpu.VMEM)
    shape = (NT, NT, tile_rows, BLOCK)
    solved = pltpu.VMEM((2 * P_SIZE, (NT - 2) * BLOCK), jnp.bfloat16)
    return pl.pallas_call(
        functools.partial(cols_kernel, chips),
        in_specs=[pl.BlockSpec(memory_space=pltpu.SMEM)] + [on_vmem] * (chips + len(corners) + 4),
        out_specs=pl.BlockSpec(memory_space=pl.ANY),
        out_shape=jax.ShapeDtypeStruct(shape, jnp.float32),
        scratch_shapes=[
            solved,
            solved,
            pltpu.VMEM((NT - 2, NT * tile_rows, BLOCK), jnp.float32),
            pltpu.VMEM(shape, jnp.float32),
            pltpu.SemaphoreType.DMA((NT // 2, NT)),
        ],
        compiler_params=pltpu.CompilerParams(vmem_limit_bytes=44 * 2**20),
        cost_estimate=pl.CostEstimate(
            flops=10 * 10**9, bytes_accessed=24 * 2**20, transcendentals=0
        ),
    )(place, tiles, *evens, odds, *corners, rounded, own)


def swap(value, axis, offset):
    count = lax.axis_size(axis)
    return lax.ppermute(value, axis, [(i, i ^ offset) for i in range(count)])


def per_device(kernel):
    row_count = lax.axis_size("row")
    col_count = lax.axis_size("col")
    tile_rows = P_SIZE // row_count
    if P_SIZE != col_count * BLOCK or tile_rows % STEP:
        return per_device_general(kernel)
    place = jnp.stack([lax.axis_index("row"), lax.axis_index("col")]).astype(jnp.int32)
    tiles = kernel.reshape(NT, NT, tile_rows * BLOCK)
    corner, top = take_top(tiles, tile_rows)
    left = take_left(tiles, tile_rows)
    chips = range(2, row_count, 2)
    over_cols = jnp.stack([corner] + [swap(corner, "col", d) for d in range(1, col_count)])
    over_cols, left = lax.optimization_barrier((over_cols, left))
    first = over_cols[:, 0:1]
    near = jnp.stack([first] + [swap(first, "row", d) for d in chips])
    lefts = {0: left}
    for d in range(1, col_count):
        if d != 2:
            lefts[d] = swap(left, "col", d)
    near, other = lax.optimization_barrier((near, over_cols[:, 1:]))
    far = swap(near, "row", 1)
    other_near = [other] + [swap(other, "row", d) for d in chips]
    tile = jax.ShapeDtypeStruct((tile_rows, BLOCK), jnp.float32)
    square = jax.ShapeDtypeStruct((P_SIZE, P_SIZE), jnp.float32)
    first_own, first_side, first_inverse = factor_call(
        first_kernel,
        place,
        (near, far),
        (),
        [tile, jax.ShapeDtypeStruct((P_SIZE, 2 * P_SIZE), jnp.bfloat16), square],
        40 * 10**9,
    )
    others = [lefts[d] for d in sorted(lefts) if d]
    *other_near, top, left, first_side = lax.optimization_barrier(
        (*other_near, top, left, first_side, *others)
    )[: len(other_near) + 3]
    other_near = jnp.stack(other_near)
    other_far = swap(other_near, "row", 1)
    if col_count > 2:
        lefts[2] = swap(left, "col", 2)
    lefts = [lefts[d] for d in range(col_count)]
    evens = [top] + [swap(top, "row", d) for d in chips]
    second_own, second_side, second_inverse, cross, own_cross = factor_call(
        second_kernel,
        place,
        (other_near, other_far),
        (first_side,),
        [
            tile,
            jax.ShapeDtypeStruct((P_SIZE, 3 * P_SIZE), jnp.bfloat16),
            square,
            jax.ShapeDtypeStruct((P_SIZE, P_SIZE), jnp.bfloat16),
            tile,
        ],
        40 * 10**9,
    )
    *evens, second_side, lefts[2 % col_count] = lax.optimization_barrier(
        (*evens, second_side, lefts[2 % col_count])
    )
    odds = swap(jnp.stack(evens), "row", 1)
    rounded, own = solve_rows(place, lefts, first_inverse, second_inverse, cross)
    corners = (first_own, first_side, second_own, second_side, cross, own_cross)
    result = solve_cols(place, tiles, evens, odds, corners, rounded, own, tile_rows)
    return result.reshape(kernel.shape)


def solution(mesh):
    placed = P(None, "row", None, "col", None)
    return jax.shard_map(
        per_device, mesh=mesh, in_specs=(placed,), out_specs=placed, check_vma=False
    )
```

```python
import functools

import jax
import jax.numpy as jnp
from jax import lax
from jax.experimental import pallas as pl
from jax.experimental.pallas import tpu as pltpu
from jax.sharding import PartitionSpec as P

P_SIZE = 512
NT = 16
STEP = 16
BLOCK = 128
EXACT = lax.Precision.HIGHEST


def exact_dot(left_side, right_side, contract=((1,), (0,))):
    return lax.dot_general(
        left_side,
        right_side,
        (contract, ((), ())),
        preferred_element_type=jnp.float32,
        precision=EXACT,
    )


def split(value):
    high = value.astype(jnp.bfloat16)
    return high, (value - high.astype(jnp.float32)).astype(jnp.bfloat16)


def split_three(value):
    high = value.astype(jnp.bfloat16)
    value = value - high.astype(jnp.float32)
    return high, *split(value)


def beside(parts):
    return jnp.concatenate(parts, axis=1)


def fast_dot(left_side, right_side, contract=((1,), (0,))):
    return lax.dot_general(
        left_side, right_side, (contract, ((), ())), preferred_element_type=jnp.float32
    )


def repeat_columns(rows, start):
    slots = BLOCK // STEP
    slot = lax.broadcasted_iota(jnp.int32, rows.shape, 1) // STEP
    slot = (slot + (slots - start // STEP)) % slots
    spread_out = rows
    for place in range(1, 6):
        spread_out = jnp.where(slot == place, pltpu.roll(rows, place * STEP, 1), spread_out)
    high, middle, low = (part.astype(jnp.float32) for part in split_three(spread_out))
    parts = jnp.where(slot < 3, high, jnp.where(slot < 5, middle, low))
    return jnp.where(slot < 6, parts, 0.0).astype(jnp.bfloat16)


def factor_block(work, done):
    row_id = lax.broadcasted_iota(jnp.int32, (STEP, BLOCK), 0)
    for start in range(0, BLOCK, STEP):
        here = slice(start, start + STEP)
        halves = [work[here, 0:BLOCK], work[here, BLOCK : 2 * BLOCK]]
        columns = [
            jnp.broadcast_to(halves[0][:, start + j : start + j + 1], (STEP, BLOCK))
            for j in range(STEP)
        ]
        if start + STEP < BLOCK:
            raw = repeat_columns(work[start + STEP :, 0:BLOCK], start)
        kept = [jnp.zeros((STEP, BLOCK), jnp.float32)] * 2
        pivots = jnp.ones((STEP, BLOCK), jnp.float32)
        for k in range(STEP):
            pivot = jnp.broadcast_to(columns[k][k : k + 1, :], (STEP, BLOCK))
            factors = jnp.where(row_id == k, 0.0, columns[k] * (1.0 / pivot))
            for j in range(k + 1, STEP):
                top = jnp.broadcast_to(columns[j][k : k + 1, :], (STEP, BLOCK))
                columns[j] = columns[j] - factors * top
            pivots = jnp.where(row_id == k, pivot, pivots)
            for h in range(2):
                top = jnp.broadcast_to(halves[h][k : k + 1, :], (STEP, BLOCK))
                kept[h] = jnp.where(row_id == k, top, kept[h])
                halves[h] = halves[h] - factors * top
        scale = lax.rsqrt(pivots)
        inverse = 1.0 / pivots
        for h in range(2):
            done[here, h * BLOCK : (h + 1) * BLOCK] = kept[h] * scale
        if start + STEP < BLOCK:
            solved = jnp.concatenate([halves[0] * inverse, halves[1] * inverse], axis=1)
            high, middle, low = split_three(solved)
            blank = jnp.zeros_like(high)
            parts = [high, middle, low, high, middle, high, blank, blank]
            slots = BLOCK // STEP
            parts = [parts[(at - start // STEP) % slots] for at in range(slots)]
            parts = jnp.concatenate(parts)
            after, later = start + STEP, start + 2 * STEP
            blocks = [(after, later, 0), (later, BLOCK, 0), (after, BLOCK, BLOCK)]
            for first, last, column in blocks:
                if first < last:
                    here = (slice(first, last), slice(column, column + BLOCK))
                    work[here] = work[here] - fast_dot(
                        raw[first - after : last - after], parts[:, column : column + BLOCK]
                    )


def factor_kernel(given, factor, inverse, rest, work, done):
    rest[...] = given[...]
    factor_rest(rest, factor, inverse, work, done)


def factor_rest(rest, factor, inverse, work, done):
    order = rest.shape[0]
    inverse[...] = jnp.zeros_like(inverse)
    factor[...] = jnp.zeros_like(factor)
    row_id = lax.broadcasted_iota(jnp.int32, (BLOCK, BLOCK), 0)
    column_id = lax.broadcasted_iota(jnp.int32, (BLOCK, BLOCK), 1)

    def step(at, carry):
        now = pl.ds(pl.multiple_of(at * BLOCK, BLOCK), BLOCK)
        work[:, 0:BLOCK] = rest[now, now]
        work[:, BLOCK:] = (row_id == column_id).astype(jnp.float32)
        factor_block(work, done)
        factor[now, now] = jnp.where(column_id >= row_id, done[:, 0:BLOCK], 0.0).T
        for start in range(0, order, BLOCK):
            pl.when(at * BLOCK == start)(functools.partial(spread_block, start))
        return carry

    def spread_block(start):
        here = slice(start, start + BLOCK)
        block_inverse = done[:, BLOCK:]
        if start:
            inverse[here, 0:start] = exact_dot(block_inverse, inverse[here, 0:start])
        inverse[here, here] = block_inverse
        if start + BLOCK < order:
            after = slice(start + BLOCK, order)
            upper = exact_dot(block_inverse, rest[here, after])
            lower = upper.T
            factor[after, here] = lower
            rest[after, after] = rest[after, after] - exact_dot(lower, upper)
            so_far = slice(0, start + BLOCK)
            inverse[after, so_far] = inverse[after, so_far] - exact_dot(
                lower, inverse[here, so_far]
            )

    lax.fori_loop(0, order // BLOCK, step, 0)


def factor_scratch():
    return [
        pltpu.VMEM((P_SIZE, P_SIZE), jnp.float32),
        pltpu.VMEM((BLOCK, 2 * BLOCK), jnp.float32),
        pltpu.VMEM((BLOCK, 2 * BLOCK), jnp.float32),
    ]


def factor_corner(corner):
    order = corner.shape[0]
    square = jax.ShapeDtypeStruct((order, order), jnp.float32)
    return pl.pallas_call(
        factor_kernel,
        out_shape=[square, square],
        scratch_shapes=factor_scratch(),
        compiler_params=pltpu.CompilerParams(vmem_limit_bytes=20 * 2**20),
    )(corner)


def spread(value, axis, offsets):
    count = lax.axis_size(axis)
    parts = [value]
    for offset in offsets[1:]:
        parts.append(lax.ppermute(value, axis, [(i, i ^ offset) for i in range(count)]))
    return jnp.stack(parts)


def gather_corner(mine):
    row_count = lax.axis_size("row")
    col_count = lax.axis_size("col")
    row_index = lax.axis_index("row")
    column_index = lax.axis_index("col")
    over_cols = spread(mine, "col", list(range(col_count)))
    over_chips = spread(over_cols, "row", list(range(0, row_count, 2)))
    slots = spread(over_chips, "row", [0, 1])
    slots = slots.transpose(1, 0, 2, 3, 4, 5).reshape(row_count, col_count, *mine.shape)
    slots = jnp.take(slots, jnp.arange(row_count) ^ row_index, axis=0, mode="clip")
    slots = jnp.take(slots, jnp.arange(col_count) ^ column_index, axis=1, mode="clip")
    return slots.transpose(2, 0, 3, 1, 4).reshape(3, P_SIZE, P_SIZE)


def per_device_general(kernel):
    row_count = lax.axis_size("row")
    col_count = lax.axis_size("col")
    tile_rows = P_SIZE // row_count
    tile_cols = P_SIZE // col_count
    row_index = lax.axis_index("row")
    column_index = lax.axis_index("col")
    tiles = kernel.reshape(NT, NT, tile_rows, tile_cols)
    corner = gather_corner(jnp.stack([tiles[0, 0], tiles[1, 0], tiles[1, 1]]))
    own_rows = tiles[:, 0:2].transpose(0, 2, 1, 3).reshape(NT * tile_rows, 2 * tile_cols)
    own_rows = lax.all_gather(own_rows, "col", axis=0, tiled=False)
    own_rows = own_rows.reshape(col_count, NT * tile_rows, 2, tile_cols).transpose(1, 2, 0, 3)
    own_rows = own_rows.reshape(NT * tile_rows, 2, P_SIZE)
    own_cols = tiles[0:2].transpose(0, 2, 1, 3).reshape(2 * tile_rows, NT * tile_cols)
    own_cols = lax.all_gather(own_cols, "row", axis=0, tiled=False)
    own_cols = own_cols.reshape(row_count, 2, tile_rows, NT * tile_cols).transpose(1, 0, 2, 3)
    own_cols = own_cols.reshape(2, P_SIZE, NT * tile_cols)

    first_corner, cross_corner, second_corner = (corner[i].astype(jnp.float32) for i in range(3))
    first_factor, first_inverse = factor_corner(0.5 * (first_corner + first_corner.T))
    cross = exact_dot(cross_corner, first_inverse, ((1,), (1,))).astype(jnp.bfloat16)
    updated_corner = second_corner - fast_dot(cross, cross, ((1,), (1,)))
    second_factor, second_inverse = factor_corner(0.5 * (updated_corner + updated_corner.T))

    first_rows = exact_dot(
        own_rows[tile_rows:, 0].astype(jnp.float32), first_inverse, ((1,), (1,))
    )
    first_cols = exact_dot(first_inverse, own_cols[0, :, tile_cols:].astype(jnp.float32))
    first_rows_rounded = first_rows.astype(jnp.bfloat16)
    first_cols_rounded = first_cols.astype(jnp.bfloat16)
    second_rows = own_rows[2 * tile_rows :, 1].astype(jnp.float32) - fast_dot(
        first_rows_rounded[tile_rows:], cross, ((1,), (1,))
    )
    second_cols = own_cols[1, :, 2 * tile_cols :].astype(jnp.float32) - fast_dot(
        cross, first_cols_rounded[:, tile_cols:]
    )
    second_rows = exact_dot(second_rows, second_inverse, ((1,), (1,)))
    second_cols = exact_dot(second_inverse, second_cols)
    left_side = jnp.concatenate(
        [first_rows_rounded[tile_rows:], second_rows.astype(jnp.bfloat16)], axis=1
    )
    right_side = jnp.concatenate(
        [first_cols_rounded[:, tile_cols:], second_cols.astype(jnp.bfloat16)], axis=0
    )
    inner = NT - 2
    product = fast_dot(left_side, right_side).reshape(inner, tile_rows, inner, tile_cols)
    trailing = tiles[2:, 2:].astype(jnp.float32) - product.transpose(0, 2, 1, 3)
    own = (row_index * tile_rows, column_index * tile_cols)
    first_own = lax.dynamic_slice_in_dim(first_rows, own[1], tile_cols, 1)
    second_own = lax.dynamic_slice_in_dim(second_rows, own[1], tile_cols, 1)
    first_tile = lax.dynamic_slice(first_factor, own, (tile_rows, tile_cols))
    second_tile = lax.dynamic_slice(second_factor, own, (tile_rows, tile_cols))
    result = jnp.zeros(tiles.shape, jnp.float32)
    result = result.at[2:, 2:].set(trailing)
    result = result.at[0, 0].set(first_tile)
    result = result.at[1:, 0].set(first_own.reshape(NT - 1, tile_rows, tile_cols))
    result = result.at[1, 1].set(second_tile)
    result = result.at[2:, 1].set(second_own.reshape(NT - 2, tile_rows, tile_cols))
    return result.reshape(kernel.shape)


def whole(shape):
    return pl.BlockSpec(shape, lambda *_: (0,) * len(shape))


def natural_tile(tiles, spread_rows, tile_rows):
    for r in range(tile_rows):
        spread_rows[r * NT : (r + 1) * NT, :] = tiles[:, r * BLOCK : (r + 1) * BLOCK].astype(
            jnp.float32
        )


def top_kernel(tiles, corner, top, spread_rows):
    tile_rows = corner.shape[1]
    for t in range(2):
        natural_tile(tiles[t], spread_rows, tile_rows)
        for s in range(NT):
            tile = spread_rows[pl.ds(s, tile_rows, stride=NT), :].astype(jnp.bfloat16)
            if s >= 2:
                here = slice((s - 2) * BLOCK, (s - 1) * BLOCK)
                top[t * tile_rows : (t + 1) * tile_rows, here] = tile
            elif s <= t:
                corner[t + s] = tile


def left_kernel(tiles, left, spread_rows):
    tile_rows = left.shape[0] // (NT - 2)
    half = NT // 2
    for t in range(2, NT):
        for r in range(tile_rows):
            part = tiles[t, :, r * BLOCK : (r + 1) * BLOCK].astype(jnp.float32)
            spread_rows[r * half : (r + 1) * half, :] = part[0:half]
        rows = slice((t - 2) * tile_rows, (t - 1) * tile_rows)
        for s in range(2):
            tile = spread_rows[pl.ds(s, tile_rows, stride=half), :].astype(jnp.bfloat16)
            left[rows, s * BLOCK : (s + 1) * BLOCK] = tile


def take_top(tiles, tile_rows):
    return pl.pallas_call(
        top_kernel,
        in_specs=[pl.BlockSpec(memory_space=pltpu.VMEM)],
        out_shape=[
            jax.ShapeDtypeStruct((3, tile_rows, BLOCK), jnp.bfloat16),
            jax.ShapeDtypeStruct((2 * tile_rows, (NT - 2) * BLOCK), jnp.bfloat16),
        ],
        scratch_shapes=[pltpu.VMEM((tile_rows * NT, BLOCK), jnp.float32)],
        compiler_params=pltpu.CompilerParams(vmem_limit_bytes=16 * 2**20),
    )(tiles)


def take_left(tiles, tile_rows):
    on_vmem = pl.BlockSpec(memory_space=pltpu.VMEM)
    return pl.pallas_call(
        left_kernel,
        in_specs=[on_vmem],
        out_specs=on_vmem,
        out_shape=jax.ShapeDtypeStruct(((NT - 2) * tile_rows, 2 * BLOCK), jnp.bfloat16),
        scratch_shapes=[pltpu.VMEM((tile_rows * NT // 2, BLOCK), jnp.float32)],
        compiler_params=pltpu.CompilerParams(vmem_limit_bytes=16 * 2**20),
        cost_estimate=pl.CostEstimate(
            flops=0, bytes_accessed=2 * NT * tile_rows * NT * BLOCK, transcendentals=0
        ),
    )(tiles)


def place_corner(place, slots, which, corner):
    row_index, column_index = place[0], place[1]
    chips, col_count, _, tile_rows, _ = slots[0].shape
    for core, held in enumerate(slots):
        for chip in range(chips):
            first_row = pl.multiple_of((row_index ^ (2 * chip + core)) * tile_rows, tile_rows)
            for col in range(col_count):
                first_col = pl.multiple_of((column_index ^ col) * BLOCK, BLOCK)
                corner[pl.ds(first_row, tile_rows), pl.ds(first_col, BLOCK)] = held[
                    chip, col, which
                ].astype(jnp.float32)


def own_tile(place, matrix, tile):
    tile_rows, tile_cols = tile.shape
    first_row = pl.multiple_of(place[0] * tile_rows, tile_rows)
    first_col = pl.multiple_of(place[1] * tile_cols, tile_cols)
    tile[...] = matrix[pl.ds(first_row, tile_rows), pl.ds(first_col, tile_cols)]


def first_kernel(place, near, far, own, side, inverse, rest, work, done, factor):
    place_corner(place, (near, far), 0, rest)
    factor_rest(rest, factor, inverse, work, done)
    own_tile(place, factor, own)
    order = rest.shape[0]
    for at, part in enumerate(split_three(inverse[...])):
        side[:, at * order : (at + 1) * order] = part


def second_kernel(
    place, near, far, first_side, own, side, inverse, cross, own_cross, rest, work, done, factor
):
    place_corner(place, (near, far), 0, rest)
    given = rest[...].astype(jnp.bfloat16)
    solved = fast_dot(beside([given] * 3), first_side[...], ((1,), (1,)))
    rest[...] = solved
    own_tile(place, rest, own_cross)
    solved = solved.astype(jnp.bfloat16)
    cross[...] = solved
    place_corner(place, (near, far), 1, rest)
    rest[...] = rest[...] - fast_dot(solved, solved, ((1,), (1,)))
    factor_rest(rest, factor, inverse, work, done)
    own_tile(place, factor, own)
    order = rest.shape[0]
    for at, part in enumerate(split_three(inverse[...])):
        side[:, at * order : (at + 1) * order] = part


def factor_call(body, place, slots, extra, out_shape, cost):
    on_vmem = pl.BlockSpec(memory_space=pltpu.VMEM)
    square = pltpu.VMEM((P_SIZE, P_SIZE), jnp.float32)
    return pl.pallas_call(
        body,
        in_specs=[pl.BlockSpec(memory_space=pltpu.SMEM)] + [on_vmem] * (2 + len(extra)),
        out_shape=out_shape,
        scratch_shapes=[*factor_scratch(), square],
        compiler_params=pltpu.CompilerParams(vmem_limit_bytes=20 * 2**20),
        cost_estimate=pl.CostEstimate(
            flops=cost, bytes_accessed=4 * 2**20, transcendentals=0
        ),
    )(place, *slots, *extra)


def rows_kernel(place, *refs):
    lefts = refs[:-9]
    first_inverse, second_inverse, cross, rounded, own, *scratch = refs[-9:]
    first_side, cross_side, second_side, solved_rows = scratch
    column_index = place[1]
    own_col = pl.multiple_of(column_index * BLOCK, BLOCK)
    order = P_SIZE

    @pl.when(pl.program_id(0) == 0)
    def _():
        for offset in range(len(lefts)):
            first = pl.multiple_of((column_index ^ offset) * BLOCK, BLOCK)
            here = pl.ds(first, BLOCK)
            to = [
                slice(k * order + offset * BLOCK, k * order + (offset + 1) * BLOCK)
                for k in range(3)
            ]
            for k, part in enumerate(split_three(first_inverse[:, here].T)):
                first_side[to[k], :] = part
            for k, part in enumerate(split_three(second_inverse[:, here].T)):
                second_side[to[k], :] = part
            cross_side[:, to[0]] = cross[here, :].astype(jnp.float32).T.astype(jnp.bfloat16)

    given = [left[:, 0:BLOCK] for left in lefts]
    solved = fast_dot(beside(given * 3), first_side[...])
    solved_rows[:, 0:order] = solved
    first_rounded = solved.astype(jnp.bfloat16)
    given = jnp.concatenate([left[:, BLOCK : 2 * BLOCK] for left in lefts], axis=1)
    left_over = given.astype(jnp.float32) - fast_dot(first_rounded, cross_side[...])
    high, middle, low = split_three(left_over)
    solved = (
        fast_dot(beside([high] * 3), second_side[...])
        + fast_dot(beside([middle] * 2), second_side[0 : 2 * order, :])
        + fast_dot(low, second_side[0:order, :])
    )
    solved_rows[:, order:] = solved
    rounded[:, 0:order] = first_rounded
    rounded[:, order:] = solved.astype(jnp.bfloat16)
    own[:, 0:BLOCK] = solved_rows[:, pl.ds(own_col, BLOCK)]
    own[:, BLOCK:] = solved_rows[:, pl.ds(order + own_col, BLOCK)]


def solve_rows(place, lefts, first_inverse, second_inverse, cross):
    count = lefts[0].shape[0]
    on_vmem = pl.BlockSpec(memory_space=pltpu.VMEM)
    return pl.pallas_call(
        rows_kernel,
        grid=(1,),
        in_specs=[pl.BlockSpec(memory_space=pltpu.SMEM)] + [on_vmem] * (len(lefts) + 3),
        out_shape=[
            jax.ShapeDtypeStruct((count, 2 * P_SIZE), jnp.bfloat16),
            jax.ShapeDtypeStruct((count, 2 * BLOCK), jnp.float32),
        ],
        scratch_shapes=[
            pltpu.VMEM((3 * P_SIZE, P_SIZE), jnp.bfloat16),
            pltpu.VMEM((P_SIZE, P_SIZE), jnp.bfloat16),
            pltpu.VMEM((3 * P_SIZE, P_SIZE), jnp.bfloat16),
            pltpu.VMEM((count, 2 * P_SIZE), jnp.float32),
        ],
        compiler_params=pltpu.CompilerParams(vmem_limit_bytes=24 * 2**20),
        cost_estimate=pl.CostEstimate(
            flops=12 * count * P_SIZE**2, bytes_accessed=10 * 2**20, transcendentals=0
        ),
    )(place, *lefts, first_inverse, second_inverse, cross)


def cols_kernel(chips, place, tiles, *refs):
    evens, odds = refs[:chips], refs[chips]
    first_own, first_side, second_own, second_side, cross, own_cross = refs[chips + 1 : chips + 7]
    rounded, own, result = refs[chips + 7 : chips + 10]
    given_cols, solved_cols, spread_rows, held, gone = refs[chips + 10 :]
    tile_rows = own_cross.shape[0]
    order = P_SIZE
    group = 4
    count = given_cols.shape[1]
    blank = jnp.zeros((tile_rows, BLOCK), jnp.float32)
    leaving = []

    def send(begin, end):
        for t in range(NT):
            here = (t, pl.ds(begin, end - begin))
            copy = pltpu.make_async_copy(held.at[here], result.at[here], gone.at[begin // 2, t])
            copy.start()
            leaving.append(copy)

    held[0, 0] = first_own[...]
    held[0, 1] = blank
    held[1, 0] = own_cross[...]
    held[1, 1] = second_own[...]
    for t in range(2, NT):
        rows = slice((t - 2) * tile_rows, (t - 1) * tile_rows)
        held[t, 0] = own[rows, 0:BLOCK]
        held[t, 1] = own[rows, BLOCK:]
    send(0, 2)
    for chip in range(chips):
        for core in range(2):
            source = odds.at[chip] if core else evens[chip]
            first = pl.multiple_of((place[0] ^ (2 * chip + core)) * tile_rows, tile_rows)
            for t in range(2):
                given_cols[pl.ds(t * order + first, tile_rows), :] = source[
                    t * tile_rows : (t + 1) * tile_rows, :
                ]
    for t in range(2, NT):
        natural_tile(tiles[t], spread_rows.at[t - 2], tile_rows)
    width = 1024
    for first_col in range(0, count, width):
        last_col = min(first_col + width, count)
        here = slice(first_col, last_col)
        given = given_cols[0:order, here]
        first = fast_dot(first_side[...], jnp.concatenate([given] * 3))
        first = first.astype(jnp.bfloat16)
        solved_cols[0:order, here] = first
        left_over = given_cols[order:, here].astype(jnp.float32) - fast_dot(cross[...], first)
        high, middle, low = split_three(left_over)
        second = (
            fast_dot(second_side[...], jnp.concatenate([high] * 3))
            + fast_dot(second_side[:, 0 : 2 * order], jnp.concatenate([middle] * 2))
            + fast_dot(second_side[:, 0:order], low)
        )
        solved_cols[order:, here] = second.astype(jnp.bfloat16)
        for begin in range(first_col, last_col, group * BLOCK):
            end = min(begin + group * BLOCK, last_col)
            product = fast_dot(rounded[...], solved_cols[:, begin:end])
            for column in range(begin, end, BLOCK):
                s = column // BLOCK + 2
                held[0, s] = blank
                held[1, s] = blank
                for t in range(2, NT):
                    rows = slice((t - 2) * tile_rows, (t - 1) * tile_rows)
                    held[t, s] = (
                        spread_rows[t - 2, pl.ds(s, tile_rows, stride=NT), :]
                        - product[rows, column - begin : column - begin + BLOCK]
                    )
            send(begin // BLOCK + 2, end // BLOCK + 2)
    for copy in leaving:
        copy.wait()


def solve_cols(place, tiles, evens, odds, corners, rounded, own, tile_rows):
    chips = len(evens)
    on_vmem = pl.BlockSpec(memory_space=pltpu.VMEM)
    shape = (NT, NT, tile_rows, BLOCK)
    solved = pltpu.VMEM((2 * P_SIZE, (NT - 2) * BLOCK), jnp.bfloat16)
    return pl.pallas_call(
        functools.partial(cols_kernel, chips),
        in_specs=[pl.BlockSpec(memory_space=pltpu.SMEM)] + [on_vmem] * (chips + len(corners) + 4),
        out_specs=pl.BlockSpec(memory_space=pl.ANY),
        out_shape=jax.ShapeDtypeStruct(shape, jnp.float32),
        scratch_shapes=[
            solved,
            solved,
            pltpu.VMEM((NT - 2, NT * tile_rows, BLOCK), jnp.float32),
            pltpu.VMEM(shape, jnp.float32),
            pltpu.SemaphoreType.DMA((NT // 2, NT)),
        ],
        compiler_params=pltpu.CompilerParams(vmem_limit_bytes=44 * 2**20),
        cost_estimate=pl.CostEstimate(
            flops=10 * 10**9, bytes_accessed=24 * 2**20, transcendentals=0
        ),
    )(place, tiles, *evens, odds, *corners, rounded, own)


def swap(value, axis, offset):
    count = lax.axis_size(axis)
    return lax.ppermute(value, axis, [(i, i ^ offset) for i in range(count)])


def per_device(kernel):
    row_count = lax.axis_size("row")
    col_count = lax.axis_size("col")
    tile_rows = P_SIZE // row_count
    if P_SIZE != col_count * BLOCK or tile_rows % STEP:
        return per_device_general(kernel)
    place = jnp.stack([lax.axis_index("row"), lax.axis_index("col")]).astype(jnp.int32)
    tiles = kernel.reshape(NT, NT, tile_rows * BLOCK)
    corner, top = take_top(tiles[0:2], tile_rows)
    left = take_left(tiles, tile_rows)
    chips = range(2, row_count, 2)
    over_cols = jnp.stack([corner] + [swap(corner, "col", d) for d in range(1, col_count)])
    over_cols, left = lax.optimization_barrier((over_cols, left))
    first = over_cols[:, 0:1]
    near = jnp.stack([first] + [swap(first, "row", d) for d in chips])
    lefts = {0: left}
    for d in range(1, col_count):
        if d != 2:
            lefts[d] = swap(left, "col", d)
    near, other = lax.optimization_barrier((near, over_cols[:, 1:]))
    far = swap(near, "row", 1)
    other_near = [other] + [swap(other, "row", d) for d in chips]
    tile = jax.ShapeDtypeStruct((tile_rows, BLOCK), jnp.float32)
    square = jax.ShapeDtypeStruct((P_SIZE, P_SIZE), jnp.float32)
    first_own, first_side, first_inverse = factor_call(
        first_kernel,
        place,
        (near, far),
        (),
        [tile, jax.ShapeDtypeStruct((P_SIZE, 3 * P_SIZE), jnp.bfloat16), square],
        40 * 10**9,
    )
    others = [lefts[d] for d in sorted(lefts) if d]
    *other_near, top, left, first_side = lax.optimization_barrier(
        (*other_near, top, left, first_side, *others)
    )[: len(other_near) + 3]
    other_near = jnp.stack(other_near)
    other_far = swap(other_near, "row", 1)
    if col_count > 2:
        lefts[2] = swap(left, "col", 2)
    lefts = [lefts[d] for d in range(col_count)]
    evens = [top] + [swap(top, "row", d) for d in chips]
    second_own, second_side, second_inverse, cross, own_cross = factor_call(
        second_kernel,
        place,
        (other_near, other_far),
        (first_side,),
        [
            tile,
            jax.ShapeDtypeStruct((P_SIZE, 3 * P_SIZE), jnp.bfloat16),
            square,
            jax.ShapeDtypeStruct((P_SIZE, P_SIZE), jnp.bfloat16),
            tile,
        ],
        40 * 10**9,
    )
    *evens, second_side, lefts[2 % col_count] = lax.optimization_barrier(
        (*evens, second_side, lefts[2 % col_count])
    )
    odds = swap(jnp.stack(evens), "row", 1)
    rounded, own = solve_rows(place, lefts, first_inverse, second_inverse, cross)
    corners = (first_own, first_side, second_own, second_side, cross, own_cross)
    result = solve_cols(place, tiles, evens, odds, corners, rounded, own, tile_rows)
    return result.reshape(kernel.shape)


def solution(mesh):
    placed = P(None, "row", None, "col", None)
    return jax.shard_map(
        per_device, mesh=mesh, in_specs=(placed,), out_specs=placed, check_vma=False
    )
```

```python
import functools

import jax
import jax.numpy as jnp
from jax import lax
from jax.experimental import pallas as pl
from jax.experimental.pallas import tpu as pltpu
from jax.sharding import PartitionSpec as P

P_SIZE = 512
NT = 16
STEP = 16
BLOCK = 128
EXACT = lax.Precision.HIGHEST


def exact_dot(left_side, right_side, contract=((1,), (0,))):
    return lax.dot_general(
        left_side,
        right_side,
        (contract, ((), ())),
        preferred_element_type=jnp.float32,
        precision=EXACT,
    )


def split(value):
    high = value.astype(jnp.bfloat16)
    return high, (value - high.astype(jnp.float32)).astype(jnp.bfloat16)


def split_three(value):
    high = value.astype(jnp.bfloat16)
    value = value - high.astype(jnp.float32)
    return high, *split(value)


def beside(parts):
    return jnp.concatenate(parts, axis=1)


def fast_dot(left_side, right_side, contract=((1,), (0,))):
    return lax.dot_general(
        left_side, right_side, (contract, ((), ())), preferred_element_type=jnp.float32
    )


def repeat_columns(rows, start):
    slots = BLOCK // STEP
    slot = lax.broadcasted_iota(jnp.int32, rows.shape, 1) // STEP
    slot = (slot + (slots - start // STEP)) % slots
    spread_out = rows
    for place in range(1, 6):
        spread_out = jnp.where(slot == place, pltpu.roll(rows, place * STEP, 1), spread_out)
    high, middle, low = (part.astype(jnp.float32) for part in split_three(spread_out))
    parts = jnp.where(slot < 3, high, jnp.where(slot < 5, middle, low))
    return jnp.where(slot < 6, parts, 0.0).astype(jnp.bfloat16)


def factor_block(work, done):
    row_id = lax.broadcasted_iota(jnp.int32, (STEP, BLOCK), 0)
    for start in range(0, BLOCK, STEP):
        here = slice(start, start + STEP)
        halves = [work[here, 0:BLOCK], work[here, BLOCK : 2 * BLOCK]]
        columns = [
            jnp.broadcast_to(halves[0][:, start + j : start + j + 1], (STEP, BLOCK))
            for j in range(STEP)
        ]
        if start + STEP < BLOCK:
            raw = repeat_columns(work[start + STEP :, 0:BLOCK], start)
        kept = [jnp.zeros((STEP, BLOCK), jnp.float32)] * 2
        pivots = jnp.ones((STEP, BLOCK), jnp.float32)
        for k in range(STEP):
            pivot = jnp.broadcast_to(columns[k][k : k + 1, :], (STEP, BLOCK))
            factors = jnp.where(row_id == k, 0.0, columns[k] * (1.0 / pivot))
            for j in range(k + 1, STEP):
                top = jnp.broadcast_to(columns[j][k : k + 1, :], (STEP, BLOCK))
                columns[j] = columns[j] - factors * top
            pivots = jnp.where(row_id == k, pivot, pivots)
            for h in range(2):
                top = jnp.broadcast_to(halves[h][k : k + 1, :], (STEP, BLOCK))
                kept[h] = jnp.where(row_id == k, top, kept[h])
                halves[h] = halves[h] - factors * top
        scale = lax.rsqrt(pivots)
        inverse = 1.0 / pivots
        for h in range(2):
            done[here, h * BLOCK : (h + 1) * BLOCK] = kept[h] * scale
        if start + STEP < BLOCK:
            solved = jnp.concatenate([halves[0] * inverse, halves[1] * inverse], axis=1)
            high, middle, low = split_three(solved)
            blank = jnp.zeros_like(high)
            parts = [high, middle, low, high, middle, high, blank, blank]
            slots = BLOCK // STEP
            parts = [parts[(at - start // STEP) % slots] for at in range(slots)]
            parts = jnp.concatenate(parts)
            after, later = start + STEP, start + 2 * STEP
            blocks = [(after, later, 0), (later, BLOCK, 0), (after, BLOCK, BLOCK)]
            for first, last, column in blocks:
                if first < last:
                    here = (slice(first, last), slice(column, column + BLOCK))
                    work[here] = work[here] - fast_dot(
                        raw[first - after : last - after], parts[:, column : column + BLOCK]
                    )


def factor_kernel(given, factor, inverse, rest, work, done):
    rest[...] = given[...]
    factor_rest(rest, factor, inverse, work, done)


def factor_rest(rest, factor, inverse, work, done):
    order = rest.shape[0]
    inverse[...] = jnp.zeros_like(inverse)
    factor[...] = jnp.zeros_like(factor)
    row_id = lax.broadcasted_iota(jnp.int32, (BLOCK, BLOCK), 0)
    column_id = lax.broadcasted_iota(jnp.int32, (BLOCK, BLOCK), 1)

    def step(at, carry):
        now = pl.ds(pl.multiple_of(at * BLOCK, BLOCK), BLOCK)
        work[:, 0:BLOCK] = rest[now, now]
        work[:, BLOCK:] = (row_id == column_id).astype(jnp.float32)
        factor_block(work, done)
        factor[now, now] = jnp.where(column_id >= row_id, done[:, 0:BLOCK], 0.0).T
        for start in range(0, order, BLOCK):
            pl.when(at * BLOCK == start)(functools.partial(spread_block, start))
        return carry

    def spread_block(start):
        here = slice(start, start + BLOCK)
        block_inverse = done[:, BLOCK:]
        if start:
            inverse[here, 0:start] = exact_dot(block_inverse, inverse[here, 0:start])
        inverse[here, here] = block_inverse
        if start + BLOCK < order:
            after = slice(start + BLOCK, order)
            upper = exact_dot(block_inverse, rest[here, after])
            lower = upper.T
            factor[after, here] = lower
            rest[after, after] = rest[after, after] - exact_dot(lower, upper)
            so_far = slice(0, start + BLOCK)
            inverse[after, so_far] = inverse[after, so_far] - exact_dot(
                lower, inverse[here, so_far]
            )

    lax.fori_loop(0, order // BLOCK, step, 0)


def factor_scratch():
    return [
        pltpu.VMEM((P_SIZE, P_SIZE), jnp.float32),
        pltpu.VMEM((BLOCK, 2 * BLOCK), jnp.float32),
        pltpu.VMEM((BLOCK, 2 * BLOCK), jnp.float32),
    ]


def factor_corner(corner):
    order = corner.shape[0]
    square = jax.ShapeDtypeStruct((order, order), jnp.float32)
    return pl.pallas_call(
        factor_kernel,
        out_shape=[square, square],
        scratch_shapes=factor_scratch(),
        compiler_params=pltpu.CompilerParams(vmem_limit_bytes=20 * 2**20),
    )(corner)


def spread(value, axis, offsets):
    count = lax.axis_size(axis)
    parts = [value]
    for offset in offsets[1:]:
        parts.append(lax.ppermute(value, axis, [(i, i ^ offset) for i in range(count)]))
    return jnp.stack(parts)


def gather_corner(mine):
    row_count = lax.axis_size("row")
    col_count = lax.axis_size("col")
    row_index = lax.axis_index("row")
    column_index = lax.axis_index("col")
    over_cols = spread(mine, "col", list(range(col_count)))
    over_chips = spread(over_cols, "row", list(range(0, row_count, 2)))
    slots = spread(over_chips, "row", [0, 1])
    slots = slots.transpose(1, 0, 2, 3, 4, 5).reshape(row_count, col_count, *mine.shape)
    slots = jnp.take(slots, jnp.arange(row_count) ^ row_index, axis=0, mode="clip")
    slots = jnp.take(slots, jnp.arange(col_count) ^ column_index, axis=1, mode="clip")
    return slots.transpose(2, 0, 3, 1, 4).reshape(3, P_SIZE, P_SIZE)


def per_device_general(kernel):
    row_count = lax.axis_size("row")
    col_count = lax.axis_size("col")
    tile_rows = P_SIZE // row_count
    tile_cols = P_SIZE // col_count
    row_index = lax.axis_index("row")
    column_index = lax.axis_index("col")
    tiles = kernel.reshape(NT, NT, tile_rows, tile_cols)
    corner = gather_corner(jnp.stack([tiles[0, 0], tiles[1, 0], tiles[1, 1]]))
    own_rows = tiles[:, 0:2].transpose(0, 2, 1, 3).reshape(NT * tile_rows, 2 * tile_cols)
    own_rows = lax.all_gather(own_rows, "col", axis=0, tiled=False)
    own_rows = own_rows.reshape(col_count, NT * tile_rows, 2, tile_cols).transpose(1, 2, 0, 3)
    own_rows = own_rows.reshape(NT * tile_rows, 2, P_SIZE)
    own_cols = tiles[0:2].transpose(0, 2, 1, 3).reshape(2 * tile_rows, NT * tile_cols)
    own_cols = lax.all_gather(own_cols, "row", axis=0, tiled=False)
    own_cols = own_cols.reshape(row_count, 2, tile_rows, NT * tile_cols).transpose(1, 0, 2, 3)
    own_cols = own_cols.reshape(2, P_SIZE, NT * tile_cols)

    first_corner, cross_corner, second_corner = (corner[i].astype(jnp.float32) for i in range(3))
    first_factor, first_inverse = factor_corner(0.5 * (first_corner + first_corner.T))
    cross = exact_dot(cross_corner, first_inverse, ((1,), (1,))).astype(jnp.bfloat16)
    updated_corner = second_corner - fast_dot(cross, cross, ((1,), (1,)))
    second_factor, second_inverse = factor_corner(0.5 * (updated_corner + updated_corner.T))

    first_rows = exact_dot(
        own_rows[tile_rows:, 0].astype(jnp.float32), first_inverse, ((1,), (1,))
    )
    first_cols = exact_dot(first_inverse, own_cols[0, :, tile_cols:].astype(jnp.float32))
    first_rows_rounded = first_rows.astype(jnp.bfloat16)
    first_cols_rounded = first_cols.astype(jnp.bfloat16)
    second_rows = own_rows[2 * tile_rows :, 1].astype(jnp.float32) - fast_dot(
        first_rows_rounded[tile_rows:], cross, ((1,), (1,))
    )
    second_cols = own_cols[1, :, 2 * tile_cols :].astype(jnp.float32) - fast_dot(
        cross, first_cols_rounded[:, tile_cols:]
    )
    second_rows = exact_dot(second_rows, second_inverse, ((1,), (1,)))
    second_cols = exact_dot(second_inverse, second_cols)
    left_side = jnp.concatenate(
        [first_rows_rounded[tile_rows:], second_rows.astype(jnp.bfloat16)], axis=1
    )
    right_side = jnp.concatenate(
        [first_cols_rounded[:, tile_cols:], second_cols.astype(jnp.bfloat16)], axis=0
    )
    inner = NT - 2
    product = fast_dot(left_side, right_side).reshape(inner, tile_rows, inner, tile_cols)
    trailing = tiles[2:, 2:].astype(jnp.float32) - product.transpose(0, 2, 1, 3)
    own = (row_index * tile_rows, column_index * tile_cols)
    first_own = lax.dynamic_slice_in_dim(first_rows, own[1], tile_cols, 1)
    second_own = lax.dynamic_slice_in_dim(second_rows, own[1], tile_cols, 1)
    first_tile = lax.dynamic_slice(first_factor, own, (tile_rows, tile_cols))
    second_tile = lax.dynamic_slice(second_factor, own, (tile_rows, tile_cols))
    result = jnp.zeros(tiles.shape, jnp.float32)
    result = result.at[2:, 2:].set(trailing)
    result = result.at[0, 0].set(first_tile)
    result = result.at[1:, 0].set(first_own.reshape(NT - 1, tile_rows, tile_cols))
    result = result.at[1, 1].set(second_tile)
    result = result.at[2:, 1].set(second_own.reshape(NT - 2, tile_rows, tile_cols))
    return result.reshape(kernel.shape)


def whole(shape):
    return pl.BlockSpec(shape, lambda *_: (0,) * len(shape))


def natural_tile(tiles, spread_rows, tile_rows):
    for r in range(tile_rows):
        spread_rows[r * NT : (r + 1) * NT, :] = tiles[:, r * BLOCK : (r + 1) * BLOCK].astype(
            jnp.float32
        )


def top_kernel(tiles, corner, top, spread_rows):
    tile_rows = corner.shape[1]
    for t in range(2):
        natural_tile(tiles[t], spread_rows, tile_rows)
        for s in range(NT):
            tile = spread_rows[pl.ds(s, tile_rows, stride=NT), :].astype(jnp.bfloat16)
            if s >= 2:
                here = slice((s - 2) * BLOCK, (s - 1) * BLOCK)
                top[t * tile_rows : (t + 1) * tile_rows, here] = tile
            elif s <= t:
                corner[t + s] = tile


def left_kernel(tiles, left, spread_rows):
    tile_rows = left.shape[0] // (NT - 2)
    half = NT // 2
    for t in range(2, NT):
        for r in range(tile_rows):
            part = tiles[t, :, r * BLOCK : (r + 1) * BLOCK].astype(jnp.float32)
            spread_rows[r * half : (r + 1) * half, :] = part[0:half]
        rows = slice((t - 2) * tile_rows, (t - 1) * tile_rows)
        for s in range(2):
            tile = spread_rows[pl.ds(s, tile_rows, stride=half), :].astype(jnp.bfloat16)
            left[rows, s * BLOCK : (s + 1) * BLOCK] = tile


def take_top(tiles, tile_rows):
    return pl.pallas_call(
        top_kernel,
        in_specs=[pl.BlockSpec(memory_space=pltpu.VMEM)],
        out_shape=[
            jax.ShapeDtypeStruct((3, tile_rows, BLOCK), jnp.bfloat16),
            jax.ShapeDtypeStruct((2 * tile_rows, (NT - 2) * BLOCK), jnp.bfloat16),
        ],
        scratch_shapes=[pltpu.VMEM((tile_rows * NT, BLOCK), jnp.float32)],
        compiler_params=pltpu.CompilerParams(vmem_limit_bytes=16 * 2**20),
    )(tiles)


def take_left(tiles, tile_rows):
    on_vmem = pl.BlockSpec(memory_space=pltpu.VMEM)
    return pl.pallas_call(
        left_kernel,
        in_specs=[on_vmem],
        out_specs=on_vmem,
        out_shape=jax.ShapeDtypeStruct(((NT - 2) * tile_rows, 2 * BLOCK), jnp.bfloat16),
        scratch_shapes=[pltpu.VMEM((tile_rows * NT // 2, BLOCK), jnp.float32)],
        compiler_params=pltpu.CompilerParams(vmem_limit_bytes=16 * 2**20),
        cost_estimate=pl.CostEstimate(
            flops=0, bytes_accessed=2 * NT * tile_rows * NT * BLOCK, transcendentals=0
        ),
    )(tiles)


def place_corner(place, slots, which, corner):
    row_index, column_index = place[0], place[1]
    chips, col_count, _, tile_rows, _ = slots[0].shape
    for core, held in enumerate(slots):
        for chip in range(chips):
            first_row = pl.multiple_of((row_index ^ (2 * chip + core)) * tile_rows, tile_rows)
            for col in range(col_count):
                first_col = pl.multiple_of((column_index ^ col) * BLOCK, BLOCK)
                corner[pl.ds(first_row, tile_rows), pl.ds(first_col, BLOCK)] = held[
                    chip, col, which
                ].astype(jnp.float32)


def own_tile(place, matrix, tile):
    tile_rows, tile_cols = tile.shape
    first_row = pl.multiple_of(place[0] * tile_rows, tile_rows)
    first_col = pl.multiple_of(place[1] * tile_cols, tile_cols)
    tile[...] = matrix[pl.ds(first_row, tile_rows), pl.ds(first_col, tile_cols)]


def first_kernel(place, near, far, own, side, inverse, rest, work, done, factor):
    place_corner(place, (near, far), 0, rest)
    factor_rest(rest, factor, inverse, work, done)
    own_tile(place, factor, own)
    order = rest.shape[0]
    for at, part in enumerate(split_three(inverse[...])):
        side[:, at * order : (at + 1) * order] = part


def second_kernel(
    place, near, far, first_side, own, side, inverse, cross, own_cross, rest, work, done, factor
):
    place_corner(place, (near, far), 0, rest)
    given = rest[...].astype(jnp.bfloat16)
    solved = fast_dot(beside([given] * 3), first_side[...], ((1,), (1,)))
    rest[...] = solved
    own_tile(place, rest, own_cross)
    solved = solved.astype(jnp.bfloat16)
    cross[...] = solved
    place_corner(place, (near, far), 1, rest)
    rest[...] = rest[...] - fast_dot(solved, solved, ((1,), (1,)))
    factor_rest(rest, factor, inverse, work, done)
    own_tile(place, factor, own)
    order = rest.shape[0]
    for at, part in enumerate(split_three(inverse[...])):
        side[:, at * order : (at + 1) * order] = part


def factor_call(body, place, slots, extra, out_shape, cost):
    on_vmem = pl.BlockSpec(memory_space=pltpu.VMEM)
    square = pltpu.VMEM((P_SIZE, P_SIZE), jnp.float32)
    return pl.pallas_call(
        body,
        in_specs=[pl.BlockSpec(memory_space=pltpu.SMEM)] + [on_vmem] * (2 + len(extra)),
        out_shape=out_shape,
        scratch_shapes=[*factor_scratch(), square],
        compiler_params=pltpu.CompilerParams(vmem_limit_bytes=20 * 2**20),
        cost_estimate=pl.CostEstimate(
            flops=cost, bytes_accessed=4 * 2**20, transcendentals=0
        ),
    )(place, *slots, *extra)


def rows_kernel(place, *refs):
    lefts = refs[:-9]
    first_inverse, second_inverse, cross, rounded, own, *scratch = refs[-9:]
    first_side, cross_side, second_side, solved_rows = scratch
    column_index = place[1]
    own_col = pl.multiple_of(column_index * BLOCK, BLOCK)
    order = P_SIZE

    @pl.when(pl.program_id(0) == 0)
    def _():
        for offset in range(len(lefts)):
            first = pl.multiple_of((column_index ^ offset) * BLOCK, BLOCK)
            here = pl.ds(first, BLOCK)
            to = [
                slice(k * order + offset * BLOCK, k * order + (offset + 1) * BLOCK)
                for k in range(3)
            ]
            for k, part in enumerate(split_three(first_inverse[:, here].T)):
                first_side[to[k], :] = part
            for k, part in enumerate(split_three(second_inverse[:, here].T)):
                second_side[to[k], :] = part
            cross_side[:, to[0]] = cross[here, :].astype(jnp.float32).T.astype(jnp.bfloat16)

    given = [left[:, 0:BLOCK] for left in lefts]
    solved = fast_dot(beside(given * 3), first_side[...])
    solved_rows[:, 0:order] = solved
    first_rounded = solved.astype(jnp.bfloat16)
    given = jnp.concatenate([left[:, BLOCK : 2 * BLOCK] for left in lefts], axis=1)
    left_over = given.astype(jnp.float32) - fast_dot(first_rounded, cross_side[...])
    high, middle, low = split_three(left_over)
    solved = (
        fast_dot(beside([high] * 3), second_side[...])
        + fast_dot(beside([middle] * 2), second_side[0 : 2 * order, :])
        + fast_dot(low, second_side[0:order, :])
    )
    solved_rows[:, order:] = solved
    rounded[:, 0:order] = first_rounded
    rounded[:, order:] = solved.astype(jnp.bfloat16)
    own[:, 0:BLOCK] = solved_rows[:, pl.ds(own_col, BLOCK)]
    own[:, BLOCK:] = solved_rows[:, pl.ds(order + own_col, BLOCK)]


def solve_rows(place, lefts, first_inverse, second_inverse, cross):
    count = lefts[0].shape[0]
    on_vmem = pl.BlockSpec(memory_space=pltpu.VMEM)
    return pl.pallas_call(
        rows_kernel,
        grid=(1,),
        in_specs=[pl.BlockSpec(memory_space=pltpu.SMEM)] + [on_vmem] * (len(lefts) + 3),
        out_shape=[
            jax.ShapeDtypeStruct((count, 2 * P_SIZE), jnp.bfloat16),
            jax.ShapeDtypeStruct((count, 2 * BLOCK), jnp.float32),
        ],
        scratch_shapes=[
            pltpu.VMEM((3 * P_SIZE, P_SIZE), jnp.bfloat16),
            pltpu.VMEM((P_SIZE, P_SIZE), jnp.bfloat16),
            pltpu.VMEM((3 * P_SIZE, P_SIZE), jnp.bfloat16),
            pltpu.VMEM((count, 2 * P_SIZE), jnp.float32),
        ],
        compiler_params=pltpu.CompilerParams(vmem_limit_bytes=24 * 2**20),
        cost_estimate=pl.CostEstimate(
            flops=12 * count * P_SIZE**2, bytes_accessed=10 * 2**20, transcendentals=0
        ),
    )(place, *lefts, first_inverse, second_inverse, cross)


def lower_dot(side, parts):
    order = side.shape[0]
    half = order // 2
    corner = beside([side[0:half, k * order : k * order + half] for k in range(len(parts))])
    upper = fast_dot(corner, jnp.concatenate([part[0:half] for part in parts]))
    lower = fast_dot(side[half:order, 0 : len(parts) * order], jnp.concatenate(parts))
    return jnp.concatenate([upper, lower])


def cols_kernel(chips, place, tiles, *refs):
    evens, odds = refs[:chips], refs[chips]
    first_own, first_side, second_own, second_side, cross, own_cross = refs[chips + 1 : chips + 7]
    rounded, own, result = refs[chips + 7 : chips + 10]
    given_cols, solved_cols, spread_rows, held, gone = refs[chips + 10 :]
    tile_rows = own_cross.shape[0]
    order = P_SIZE
    group = 4
    count = given_cols.shape[1]
    blank = jnp.zeros((tile_rows, BLOCK), jnp.float32)
    leaving = []

    def send(begin, end):
        for t in range(NT):
            here = (t, pl.ds(begin, end - begin))
            copy = pltpu.make_async_copy(held.at[here], result.at[here], gone.at[begin // 2, t])
            copy.start()
            leaving.append(copy)

    held[0, 0] = first_own[...]
    held[0, 1] = blank
    held[1, 0] = own_cross[...]
    held[1, 1] = second_own[...]
    for t in range(2, NT):
        rows = slice((t - 2) * tile_rows, (t - 1) * tile_rows)
        held[t, 0] = own[rows, 0:BLOCK]
        held[t, 1] = own[rows, BLOCK:]
    send(0, 2)
    for chip in range(chips):
        for core in range(2):
            source = odds.at[chip] if core else evens[chip]
            first = pl.multiple_of((place[0] ^ (2 * chip + core)) * tile_rows, tile_rows)
            for t in range(2):
                given_cols[pl.ds(t * order + first, tile_rows), :] = source[
                    t * tile_rows : (t + 1) * tile_rows, :
                ]
    for t in range(2, NT):
        natural_tile(tiles[t], spread_rows.at[t - 2], tile_rows)
    width = 1024
    for first_col in range(0, count, width):
        last_col = min(first_col + width, count)
        here = slice(first_col, last_col)
        given = given_cols[0:order, here]
        first = lower_dot(first_side, [given] * 3).astype(jnp.bfloat16)
        solved_cols[0:order, here] = first
        left_over = given_cols[order:, here].astype(jnp.float32) - fast_dot(cross[...], first)
        high, middle, low = split_three(left_over)
        second = (
            lower_dot(second_side, [high] * 3)
            + lower_dot(second_side, [middle] * 2)
            + lower_dot(second_side, [low])
        )
        solved_cols[order:, here] = second.astype(jnp.bfloat16)
        for begin in range(first_col, last_col, group * BLOCK):
            end = min(begin + group * BLOCK, last_col)
            product = fast_dot(rounded[...], solved_cols[:, begin:end])
            for column in range(begin, end, BLOCK):
                s = column // BLOCK + 2
                held[0, s] = blank
                held[1, s] = blank
                for t in range(2, NT):
                    rows = slice((t - 2) * tile_rows, (t - 1) * tile_rows)
                    held[t, s] = (
                        spread_rows[t - 2, pl.ds(s, tile_rows, stride=NT), :]
                        - product[rows, column - begin : column - begin + BLOCK]
                    )
            send(begin // BLOCK + 2, end // BLOCK + 2)
    for copy in leaving:
        copy.wait()


def solve_cols(place, tiles, evens, odds, corners, rounded, own, tile_rows):
    chips = len(evens)
    on_vmem = pl.BlockSpec(memory_space=pltpu.VMEM)
    shape = (NT, NT, tile_rows, BLOCK)
    solved = pltpu.VMEM((2 * P_SIZE, (NT - 2) * BLOCK), jnp.bfloat16)
    return pl.pallas_call(
        functools.partial(cols_kernel, chips),
        in_specs=[pl.BlockSpec(memory_space=pltpu.SMEM)] + [on_vmem] * (chips + len(corners) + 4),
        out_specs=pl.BlockSpec(memory_space=pl.ANY),
        out_shape=jax.ShapeDtypeStruct(shape, jnp.float32),
        scratch_shapes=[
            solved,
            solved,
            pltpu.VMEM((NT - 2, NT * tile_rows, BLOCK), jnp.float32),
            pltpu.VMEM(shape, jnp.float32),
            pltpu.SemaphoreType.DMA((NT // 2, NT)),
        ],
        compiler_params=pltpu.CompilerParams(vmem_limit_bytes=44 * 2**20),
        cost_estimate=pl.CostEstimate(
            flops=10 * 10**9, bytes_accessed=24 * 2**20, transcendentals=0
        ),
    )(place, tiles, *evens, odds, *corners, rounded, own)


def swap(value, axis, offset):
    count = lax.axis_size(axis)
    return lax.ppermute(value, axis, [(i, i ^ offset) for i in range(count)])


def per_device(kernel):
    row_count = lax.axis_size("row")
    col_count = lax.axis_size("col")
    tile_rows = P_SIZE // row_count
    if P_SIZE != col_count * BLOCK or tile_rows % STEP:
        return per_device_general(kernel)
    place = jnp.stack([lax.axis_index("row"), lax.axis_index("col")]).astype(jnp.int32)
    tiles = kernel.reshape(NT, NT, tile_rows * BLOCK)
    corner, top = take_top(tiles[0:2], tile_rows)
    left = take_left(tiles, tile_rows)
    chips = range(2, row_count, 2)
    over_cols = jnp.stack([corner] + [swap(corner, "col", d) for d in range(1, col_count)])
    over_cols, left = lax.optimization_barrier((over_cols, left))
    first = over_cols[:, 0:1]
    near = jnp.stack([first] + [swap(first, "row", d) for d in chips])
    lefts = {0: left}
    for d in range(1, col_count):
        if d != 2:
            lefts[d] = swap(left, "col", d)
    near, other = lax.optimization_barrier((near, over_cols[:, 1:]))
    far = swap(near, "row", 1)
    other_near = [other] + [swap(other, "row", d) for d in chips]
    tile = jax.ShapeDtypeStruct((tile_rows, BLOCK), jnp.float32)
    square = jax.ShapeDtypeStruct((P_SIZE, P_SIZE), jnp.float32)
    first_own, first_side, first_inverse = factor_call(
        first_kernel,
        place,
        (near, far),
        (),
        [tile, jax.ShapeDtypeStruct((P_SIZE, 3 * P_SIZE), jnp.bfloat16), square],
        40 * 10**9,
    )
    others = [lefts[d] for d in sorted(lefts) if d]
    *other_near, top, left, first_side = lax.optimization_barrier(
        (*other_near, top, left, first_side, *others)
    )[: len(other_near) + 3]
    other_near = jnp.stack(other_near)
    other_far = swap(other_near, "row", 1)
    if col_count > 2:
        lefts[2] = swap(left, "col", 2)
    lefts = [lefts[d] for d in range(col_count)]
    evens = [top] + [swap(top, "row", d) for d in chips]
    second_own, second_side, second_inverse, cross, own_cross = factor_call(
        second_kernel,
        place,
        (other_near, other_far),
        (first_side,),
        [
            tile,
            jax.ShapeDtypeStruct((P_SIZE, 3 * P_SIZE), jnp.bfloat16),
            square,
            jax.ShapeDtypeStruct((P_SIZE, P_SIZE), jnp.bfloat16),
            tile,
        ],
        40 * 10**9,
    )
    *evens, second_side, lefts[2 % col_count] = lax.optimization_barrier(
        (*evens, second_side, lefts[2 % col_count])
    )
    odds = swap(jnp.stack(evens), "row", 1)
    rounded, own = solve_rows(place, lefts, first_inverse, second_inverse, cross)
    corners = (first_own, first_side, second_own, second_side, cross, own_cross)
    result = solve_cols(place, tiles, evens, odds, corners, rounded, own, tile_rows)
    return result.reshape(kernel.shape)


def solution(mesh):
    placed = P(None, "row", None, "col", None)
    return jax.shard_map(
        per_device, mesh=mesh, in_specs=(placed,), out_specs=placed, check_vma=False
    )
```

```python
import functools

import jax
import jax.numpy as jnp
from jax import lax
from jax.experimental import pallas as pl
from jax.experimental.pallas import tpu as pltpu
from jax.sharding import PartitionSpec as P

P_SIZE = 512
NT = 16
STEP = 16
BLOCK = 128
EXACT = lax.Precision.HIGHEST


def exact_dot(left_side, right_side, contract=((1,), (0,))):
    return lax.dot_general(
        left_side,
        right_side,
        (contract, ((), ())),
        preferred_element_type=jnp.float32,
        precision=EXACT,
    )


def split(value):
    high = value.astype(jnp.bfloat16)
    return high, (value - high.astype(jnp.float32)).astype(jnp.bfloat16)


def split_three(value):
    high = value.astype(jnp.bfloat16)
    value = value - high.astype(jnp.float32)
    return high, *split(value)


def beside(parts):
    return jnp.concatenate(parts, axis=1)


def fast_dot(left_side, right_side, contract=((1,), (0,))):
    return lax.dot_general(
        left_side, right_side, (contract, ((), ())), preferred_element_type=jnp.float32
    )


def repeat_columns(rows, start):
    slots = BLOCK // STEP
    slot = lax.broadcasted_iota(jnp.int32, rows.shape, 1) // STEP
    slot = (slot + (slots - start // STEP)) % slots
    spread_out = rows
    for place in range(1, 6):
        spread_out = jnp.where(slot == place, pltpu.roll(rows, place * STEP, 1), spread_out)
    high, middle, low = (part.astype(jnp.float32) for part in split_three(spread_out))
    parts = jnp.where(slot < 3, high, jnp.where(slot < 5, middle, low))
    return jnp.where(slot < 6, parts, 0.0).astype(jnp.bfloat16)


def factor_block(work, done):
    row_id = lax.broadcasted_iota(jnp.int32, (STEP, BLOCK), 0)
    for start in range(0, BLOCK, STEP):
        here = slice(start, start + STEP)
        halves = [work[here, 0:BLOCK], work[here, BLOCK : 2 * BLOCK]]
        columns = [
            jnp.broadcast_to(halves[0][:, start + j : start + j + 1], (STEP, BLOCK))
            for j in range(STEP)
        ]
        if start + STEP < BLOCK:
            raw = repeat_columns(work[start + STEP :, 0:BLOCK], start)
        kept = [jnp.zeros((STEP, BLOCK), jnp.float32)] * 2
        pivots = jnp.ones((STEP, BLOCK), jnp.float32)
        for k in range(STEP):
            pivot = jnp.broadcast_to(columns[k][k : k + 1, :], (STEP, BLOCK))
            factors = jnp.where(row_id == k, 0.0, columns[k] * (1.0 / pivot))
            for j in range(k + 1, STEP):
                top = jnp.broadcast_to(columns[j][k : k + 1, :], (STEP, BLOCK))
                columns[j] = columns[j] - factors * top
            pivots = jnp.where(row_id == k, pivot, pivots)
            for h in range(2):
                top = jnp.broadcast_to(halves[h][k : k + 1, :], (STEP, BLOCK))
                kept[h] = jnp.where(row_id == k, top, kept[h])
                halves[h] = halves[h] - factors * top
        scale = lax.rsqrt(pivots)
        inverse = 1.0 / pivots
        for h in range(2):
            done[here, h * BLOCK : (h + 1) * BLOCK] = kept[h] * scale
        if start + STEP < BLOCK:
            solved = jnp.concatenate([halves[0] * inverse, halves[1] * inverse], axis=1)
            high, middle, low = split_three(solved)
            blank = jnp.zeros_like(high)
            parts = [high, middle, low, high, middle, high, blank, blank]
            slots = BLOCK // STEP
            parts = [parts[(at - start // STEP) % slots] for at in range(slots)]
            parts = jnp.concatenate(parts)
            after, later = start + STEP, start + 2 * STEP
            blocks = [(after, later, 0), (later, BLOCK, 0), (after, BLOCK, BLOCK)]
            for first, last, column in blocks:
                if first < last:
                    here = (slice(first, last), slice(column, column + BLOCK))
                    work[here] = work[here] - fast_dot(
                        raw[first - after : last - after], parts[:, column : column + BLOCK]
                    )


def factor_kernel(given, factor, inverse, rest, work, done):
    rest[...] = given[...]
    factor_rest(rest, factor, inverse, work, done)


def parts_dot(left_side, right_side):
    high, middle, low = split_three(left_side)
    left_parts = beside([high, high, high, middle, middle, low])
    high, middle, low = split_three(right_side)
    return fast_dot(left_parts, jnp.concatenate([high, middle, low, high, middle, high]))


def factor_rest(rest, factor, inverse, work, done):
    order = rest.shape[0]
    inverse[...] = jnp.zeros_like(inverse)
    factor[...] = jnp.zeros_like(factor)
    row_id = lax.broadcasted_iota(jnp.int32, (BLOCK, BLOCK), 0)
    column_id = lax.broadcasted_iota(jnp.int32, (BLOCK, BLOCK), 1)

    def step(at, carry):
        now = pl.ds(pl.multiple_of(at * BLOCK, BLOCK), BLOCK)
        work[:, 0:BLOCK] = rest[now, now]
        work[:, BLOCK:] = (row_id == column_id).astype(jnp.float32)
        factor_block(work, done)
        factor[now, now] = jnp.where(column_id >= row_id, done[:, 0:BLOCK], 0.0).T
        for start in range(0, order, BLOCK):
            pl.when(at * BLOCK == start)(functools.partial(spread_block, start))
        return carry

    def spread_block(start):
        here = slice(start, start + BLOCK)
        block_inverse = done[:, BLOCK:]
        if start:
            inverse[here, 0:start] = parts_dot(block_inverse, inverse[here, 0:start])
        inverse[here, here] = block_inverse
        if start + BLOCK < order:
            after = slice(start + BLOCK, order)
            upper = parts_dot(block_inverse, rest[here, after])
            lower = upper.T
            factor[after, here] = lower
            rest[after, after] = rest[after, after] - parts_dot(lower, upper)
            so_far = slice(0, start + BLOCK)
            inverse[after, so_far] = inverse[after, so_far] - parts_dot(
                lower, inverse[here, so_far]
            )

    lax.fori_loop(0, order // BLOCK, step, 0)


def factor_scratch():
    return [
        pltpu.VMEM((P_SIZE, P_SIZE), jnp.float32),
        pltpu.VMEM((BLOCK, 2 * BLOCK), jnp.float32),
        pltpu.VMEM((BLOCK, 2 * BLOCK), jnp.float32),
    ]


def factor_corner(corner):
    order = corner.shape[0]
    square = jax.ShapeDtypeStruct((order, order), jnp.float32)
    return pl.pallas_call(
        factor_kernel,
        out_shape=[square, square],
        scratch_shapes=factor_scratch(),
        compiler_params=pltpu.CompilerParams(vmem_limit_bytes=20 * 2**20),
    )(corner)


def spread(value, axis, offsets):
    count = lax.axis_size(axis)
    parts = [value]
    for offset in offsets[1:]:
        parts.append(lax.ppermute(value, axis, [(i, i ^ offset) for i in range(count)]))
    return jnp.stack(parts)


def gather_corner(mine):
    row_count = lax.axis_size("row")
    col_count = lax.axis_size("col")
    row_index = lax.axis_index("row")
    column_index = lax.axis_index("col")
    over_cols = spread(mine, "col", list(range(col_count)))
    over_chips = spread(over_cols, "row", list(range(0, row_count, 2)))
    slots = spread(over_chips, "row", [0, 1])
    slots = slots.transpose(1, 0, 2, 3, 4, 5).reshape(row_count, col_count, *mine.shape)
    slots = jnp.take(slots, jnp.arange(row_count) ^ row_index, axis=0, mode="clip")
    slots = jnp.take(slots, jnp.arange(col_count) ^ column_index, axis=1, mode="clip")
    return slots.transpose(2, 0, 3, 1, 4).reshape(3, P_SIZE, P_SIZE)


def per_device_general(kernel):
    row_count = lax.axis_size("row")
    col_count = lax.axis_size("col")
    tile_rows = P_SIZE // row_count
    tile_cols = P_SIZE // col_count
    row_index = lax.axis_index("row")
    column_index = lax.axis_index("col")
    tiles = kernel.reshape(NT, NT, tile_rows, tile_cols)
    corner = gather_corner(jnp.stack([tiles[0, 0], tiles[1, 0], tiles[1, 1]]))
    own_rows = tiles[:, 0:2].transpose(0, 2, 1, 3).reshape(NT * tile_rows, 2 * tile_cols)
    own_rows = lax.all_gather(own_rows, "col", axis=0, tiled=False)
    own_rows = own_rows.reshape(col_count, NT * tile_rows, 2, tile_cols).transpose(1, 2, 0, 3)
    own_rows = own_rows.reshape(NT * tile_rows, 2, P_SIZE)
    own_cols = tiles[0:2].transpose(0, 2, 1, 3).reshape(2 * tile_rows, NT * tile_cols)
    own_cols = lax.all_gather(own_cols, "row", axis=0, tiled=False)
    own_cols = own_cols.reshape(row_count, 2, tile_rows, NT * tile_cols).transpose(1, 0, 2, 3)
    own_cols = own_cols.reshape(2, P_SIZE, NT * tile_cols)

    first_corner, cross_corner, second_corner = (corner[i].astype(jnp.float32) for i in range(3))
    first_factor, first_inverse = factor_corner(0.5 * (first_corner + first_corner.T))
    cross = exact_dot(cross_corner, first_inverse, ((1,), (1,))).astype(jnp.bfloat16)
    updated_corner = second_corner - fast_dot(cross, cross, ((1,), (1,)))
    second_factor, second_inverse = factor_corner(0.5 * (updated_corner + updated_corner.T))

    first_rows = exact_dot(
        own_rows[tile_rows:, 0].astype(jnp.float32), first_inverse, ((1,), (1,))
    )
    first_cols = exact_dot(first_inverse, own_cols[0, :, tile_cols:].astype(jnp.float32))
    first_rows_rounded = first_rows.astype(jnp.bfloat16)
    first_cols_rounded = first_cols.astype(jnp.bfloat16)
    second_rows = own_rows[2 * tile_rows :, 1].astype(jnp.float32) - fast_dot(
        first_rows_rounded[tile_rows:], cross, ((1,), (1,))
    )
    second_cols = own_cols[1, :, 2 * tile_cols :].astype(jnp.float32) - fast_dot(
        cross, first_cols_rounded[:, tile_cols:]
    )
    second_rows = exact_dot(second_rows, second_inverse, ((1,), (1,)))
    second_cols = exact_dot(second_inverse, second_cols)
    left_side = jnp.concatenate(
        [first_rows_rounded[tile_rows:], second_rows.astype(jnp.bfloat16)], axis=1
    )
    right_side = jnp.concatenate(
        [first_cols_rounded[:, tile_cols:], second_cols.astype(jnp.bfloat16)], axis=0
    )
    inner = NT - 2
    product = fast_dot(left_side, right_side).reshape(inner, tile_rows, inner, tile_cols)
    trailing = tiles[2:, 2:].astype(jnp.float32) - product.transpose(0, 2, 1, 3)
    own = (row_index * tile_rows, column_index * tile_cols)
    first_own = lax.dynamic_slice_in_dim(first_rows, own[1], tile_cols, 1)
    second_own = lax.dynamic_slice_in_dim(second_rows, own[1], tile_cols, 1)
    first_tile = lax.dynamic_slice(first_factor, own, (tile_rows, tile_cols))
    second_tile = lax.dynamic_slice(second_factor, own, (tile_rows, tile_cols))
    result = jnp.zeros(tiles.shape, jnp.float32)
    result = result.at[2:, 2:].set(trailing)
    result = result.at[0, 0].set(first_tile)
    result = result.at[1:, 0].set(first_own.reshape(NT - 1, tile_rows, tile_cols))
    result = result.at[1, 1].set(second_tile)
    result = result.at[2:, 1].set(second_own.reshape(NT - 2, tile_rows, tile_cols))
    return result.reshape(kernel.shape)


def whole(shape):
    return pl.BlockSpec(shape, lambda *_: (0,) * len(shape))


def natural_tile(tiles, spread_rows, tile_rows):
    for r in range(tile_rows):
        spread_rows[r * NT : (r + 1) * NT, :] = tiles[:, r * BLOCK : (r + 1) * BLOCK].astype(
            jnp.float32
        )


def top_kernel(tiles, corner, top, spread_rows):
    tile_rows = corner.shape[1]
    for t in range(2):
        natural_tile(tiles[t], spread_rows, tile_rows)
        for s in range(NT):
            tile = spread_rows[pl.ds(s, tile_rows, stride=NT), :].astype(jnp.bfloat16)
            if s >= 2:
                here = slice((s - 2) * BLOCK, (s - 1) * BLOCK)
                top[t * tile_rows : (t + 1) * tile_rows, here] = tile
            elif s <= t:
                corner[t + s] = tile


def left_kernel(tiles, left, spread_rows):
    tile_rows = left.shape[0] // (NT - 2)
    half = NT // 2
    for t in range(2, NT):
        for r in range(tile_rows):
            part = tiles[t, :, r * BLOCK : (r + 1) * BLOCK].astype(jnp.float32)
            spread_rows[r * half : (r + 1) * half, :] = part[0:half]
        rows = slice((t - 2) * tile_rows, (t - 1) * tile_rows)
        for s in range(2):
            tile = spread_rows[pl.ds(s, tile_rows, stride=half), :].astype(jnp.bfloat16)
            left[rows, s * BLOCK : (s + 1) * BLOCK] = tile


def take_top(tiles, tile_rows):
    return pl.pallas_call(
        top_kernel,
        in_specs=[pl.BlockSpec(memory_space=pltpu.VMEM)],
        out_shape=[
            jax.ShapeDtypeStruct((3, tile_rows, BLOCK), jnp.bfloat16),
            jax.ShapeDtypeStruct((2 * tile_rows, (NT - 2) * BLOCK), jnp.bfloat16),
        ],
        scratch_shapes=[pltpu.VMEM((tile_rows * NT, BLOCK), jnp.float32)],
        compiler_params=pltpu.CompilerParams(vmem_limit_bytes=16 * 2**20),
    )(tiles)


def take_left(tiles, tile_rows):
    on_vmem = pl.BlockSpec(memory_space=pltpu.VMEM)
    return pl.pallas_call(
        left_kernel,
        in_specs=[on_vmem],
        out_specs=on_vmem,
        out_shape=jax.ShapeDtypeStruct(((NT - 2) * tile_rows, 2 * BLOCK), jnp.bfloat16),
        scratch_shapes=[pltpu.VMEM((tile_rows * NT // 2, BLOCK), jnp.float32)],
        compiler_params=pltpu.CompilerParams(vmem_limit_bytes=16 * 2**20),
        cost_estimate=pl.CostEstimate(
            flops=0, bytes_accessed=2 * NT * tile_rows * NT * BLOCK, transcendentals=0
        ),
    )(tiles)


def place_corner(place, slots, which, corner):
    row_index, column_index = place[0], place[1]
    chips, col_count, _, tile_rows, _ = slots[0].shape
    for core, held in enumerate(slots):
        for chip in range(chips):
            first_row = pl.multiple_of((row_index ^ (2 * chip + core)) * tile_rows, tile_rows)
            for col in range(col_count):
                first_col = pl.multiple_of((column_index ^ col) * BLOCK, BLOCK)
                corner[pl.ds(first_row, tile_rows), pl.ds(first_col, BLOCK)] = held[
                    chip, col, which
                ].astype(jnp.float32)


def own_tile(place, matrix, tile):
    tile_rows, tile_cols = tile.shape
    first_row = pl.multiple_of(place[0] * tile_rows, tile_rows)
    first_col = pl.multiple_of(place[1] * tile_cols, tile_cols)
    tile[...] = matrix[pl.ds(first_row, tile_rows), pl.ds(first_col, tile_cols)]


def first_kernel(place, near, far, own, side, inverse, rest, work, done, factor):
    place_corner(place, (near, far), 0, rest)
    factor_rest(rest, factor, inverse, work, done)
    own_tile(place, factor, own)
    order = rest.shape[0]
    for at, part in enumerate(split_three(inverse[...])):
        side[:, at * order : (at + 1) * order] = part


def second_kernel(
    place, near, far, first_side, own, side, inverse, cross, own_cross, rest, work, done, factor
):
    place_corner(place, (near, far), 0, rest)
    given = rest[...].astype(jnp.bfloat16)
    solved = fast_dot(beside([given] * 3), first_side[...], ((1,), (1,)))
    rest[...] = solved
    own_tile(place, rest, own_cross)
    solved = solved.astype(jnp.bfloat16)
    cross[...] = solved
    place_corner(place, (near, far), 1, rest)
    rest[...] = rest[...] - fast_dot(solved, solved, ((1,), (1,)))
    factor_rest(rest, factor, inverse, work, done)
    own_tile(place, factor, own)
    order = rest.shape[0]
    for at, part in enumerate(split_three(inverse[...])):
        side[:, at * order : (at + 1) * order] = part


def factor_call(body, place, slots, extra, out_shape, cost):
    on_vmem = pl.BlockSpec(memory_space=pltpu.VMEM)
    square = pltpu.VMEM((P_SIZE, P_SIZE), jnp.float32)
    return pl.pallas_call(
        body,
        in_specs=[pl.BlockSpec(memory_space=pltpu.SMEM)] + [on_vmem] * (2 + len(extra)),
        out_shape=out_shape,
        scratch_shapes=[*factor_scratch(), square],
        compiler_params=pltpu.CompilerParams(vmem_limit_bytes=20 * 2**20),
        cost_estimate=pl.CostEstimate(
            flops=cost, bytes_accessed=4 * 2**20, transcendentals=0
        ),
    )(place, *slots, *extra)


def rows_kernel(place, *refs):
    lefts = refs[:-9]
    first_inverse, second_inverse, cross, rounded, own, *scratch = refs[-9:]
    first_side, cross_side, second_side, solved_rows = scratch
    column_index = place[1]
    own_col = pl.multiple_of(column_index * BLOCK, BLOCK)
    order = P_SIZE

    @pl.when(pl.program_id(0) == 0)
    def _():
        for offset in range(len(lefts)):
            first = pl.multiple_of((column_index ^ offset) * BLOCK, BLOCK)
            here = pl.ds(first, BLOCK)
            to = [
                slice(k * order + offset * BLOCK, k * order + (offset + 1) * BLOCK)
                for k in range(3)
            ]
            for k, part in enumerate(split_three(first_inverse[:, here].T)):
                first_side[to[k], :] = part
            for k, part in enumerate(split_three(second_inverse[:, here].T)):
                second_side[to[k], :] = part
            cross_side[:, to[0]] = cross[here, :].astype(jnp.float32).T.astype(jnp.bfloat16)

    given = [left[:, 0:BLOCK] for left in lefts]
    solved = fast_dot(beside(given * 3), first_side[...])
    solved_rows[:, 0:order] = solved
    first_rounded = solved.astype(jnp.bfloat16)
    given = jnp.concatenate([left[:, BLOCK : 2 * BLOCK] for left in lefts], axis=1)
    left_over = given.astype(jnp.float32) - fast_dot(first_rounded, cross_side[...])
    high, middle, low = split_three(left_over)
    solved = (
        fast_dot(beside([high] * 3), second_side[...])
        + fast_dot(beside([middle] * 2), second_side[0 : 2 * order, :])
        + fast_dot(low, second_side[0:order, :])
    )
    solved_rows[:, order:] = solved
    rounded[:, 0:order] = first_rounded
    rounded[:, order:] = solved.astype(jnp.bfloat16)
    own[:, 0:BLOCK] = solved_rows[:, pl.ds(own_col, BLOCK)]
    own[:, BLOCK:] = solved_rows[:, pl.ds(order + own_col, BLOCK)]


def solve_rows(place, lefts, first_inverse, second_inverse, cross):
    count = lefts[0].shape[0]
    on_vmem = pl.BlockSpec(memory_space=pltpu.VMEM)
    return pl.pallas_call(
        rows_kernel,
        grid=(1,),
        in_specs=[pl.BlockSpec(memory_space=pltpu.SMEM)] + [on_vmem] * (len(lefts) + 3),
        out_shape=[
            jax.ShapeDtypeStruct((count, 2 * P_SIZE), jnp.bfloat16),
            jax.ShapeDtypeStruct((count, 2 * BLOCK), jnp.float32),
        ],
        scratch_shapes=[
            pltpu.VMEM((3 * P_SIZE, P_SIZE), jnp.bfloat16),
            pltpu.VMEM((P_SIZE, P_SIZE), jnp.bfloat16),
            pltpu.VMEM((3 * P_SIZE, P_SIZE), jnp.bfloat16),
            pltpu.VMEM((count, 2 * P_SIZE), jnp.float32),
        ],
        compiler_params=pltpu.CompilerParams(vmem_limit_bytes=24 * 2**20),
        cost_estimate=pl.CostEstimate(
            flops=12 * count * P_SIZE**2, bytes_accessed=10 * 2**20, transcendentals=0
        ),
    )(place, *lefts, first_inverse, second_inverse, cross)


def lower_dot(side, parts):
    order = side.shape[0]
    half = order // 2
    corner = beside([side[0:half, k * order : k * order + half] for k in range(len(parts))])
    upper = fast_dot(corner, jnp.concatenate([part[0:half] for part in parts]))
    lower = fast_dot(side[half:order, 0 : len(parts) * order], jnp.concatenate(parts))
    return jnp.concatenate([upper, lower])


def cols_kernel(chips, place, tiles, *refs):
    evens, odds = refs[:chips], refs[chips]
    first_own, first_side, second_own, second_side, cross, own_cross = refs[chips + 1 : chips + 7]
    rounded, own, result = refs[chips + 7 : chips + 10]
    given_cols, solved_cols, spread_rows, held, gone = refs[chips + 10 :]
    tile_rows = own_cross.shape[0]
    order = P_SIZE
    group = 4
    count = given_cols.shape[1]
    blank = jnp.zeros((tile_rows, BLOCK), jnp.float32)
    leaving = []

    def send(begin, end):
        for t in range(NT):
            here = (t, pl.ds(begin, end - begin))
            copy = pltpu.make_async_copy(held.at[here], result.at[here], gone.at[begin // 2, t])
            copy.start()
            leaving.append(copy)

    held[0, 0] = first_own[...]
    held[0, 1] = blank
    held[1, 0] = own_cross[...]
    held[1, 1] = second_own[...]
    for t in range(2, NT):
        rows = slice((t - 2) * tile_rows, (t - 1) * tile_rows)
        held[t, 0] = own[rows, 0:BLOCK]
        held[t, 1] = own[rows, BLOCK:]
    send(0, 2)
    for chip in range(chips):
        for core in range(2):
            source = odds.at[chip] if core else evens[chip]
            first = pl.multiple_of((place[0] ^ (2 * chip + core)) * tile_rows, tile_rows)
            for t in range(2):
                given_cols[pl.ds(t * order + first, tile_rows), :] = source[
                    t * tile_rows : (t + 1) * tile_rows, :
                ]
    for t in range(2, NT):
        natural_tile(tiles[t], spread_rows.at[t - 2], tile_rows)
    width = 1024
    for first_col in range(0, count, width):
        last_col = min(first_col + width, count)
        here = slice(first_col, last_col)
        given = given_cols[0:order, here]
        first = lower_dot(first_side, [given] * 3).astype(jnp.bfloat16)
        solved_cols[0:order, here] = first
        left_over = given_cols[order:, here].astype(jnp.float32) - fast_dot(cross[...], first)
        high, middle, low = split_three(left_over)
        second = (
            lower_dot(second_side, [high] * 3)
            + lower_dot(second_side, [middle] * 2)
            + lower_dot(second_side, [low])
        )
        solved_cols[order:, here] = second.astype(jnp.bfloat16)
        for begin in range(first_col, last_col, group * BLOCK):
            end = min(begin + group * BLOCK, last_col)
            product = fast_dot(rounded[...], solved_cols[:, begin:end])
            for column in range(begin, end, BLOCK):
                s = column // BLOCK + 2
                held[0, s] = blank
                held[1, s] = blank
                for t in range(2, NT):
                    rows = slice((t - 2) * tile_rows, (t - 1) * tile_rows)
                    held[t, s] = (
                        spread_rows[t - 2, pl.ds(s, tile_rows, stride=NT), :]
                        - product[rows, column - begin : column - begin + BLOCK]
                    )
            send(begin // BLOCK + 2, end // BLOCK + 2)
    for copy in leaving:
        copy.wait()


def solve_cols(place, tiles, evens, odds, corners, rounded, own, tile_rows):
    chips = len(evens)
    on_vmem = pl.BlockSpec(memory_space=pltpu.VMEM)
    shape = (NT, NT, tile_rows, BLOCK)
    solved = pltpu.VMEM((2 * P_SIZE, (NT - 2) * BLOCK), jnp.bfloat16)
    return pl.pallas_call(
        functools.partial(cols_kernel, chips),
        in_specs=[pl.BlockSpec(memory_space=pltpu.SMEM)] + [on_vmem] * (chips + len(corners) + 4),
        out_specs=pl.BlockSpec(memory_space=pl.ANY),
        out_shape=jax.ShapeDtypeStruct(shape, jnp.float32),
        scratch_shapes=[
            solved,
            solved,
            pltpu.VMEM((NT - 2, NT * tile_rows, BLOCK), jnp.float32),
            pltpu.VMEM(shape, jnp.float32),
            pltpu.SemaphoreType.DMA((NT // 2, NT)),
        ],
        compiler_params=pltpu.CompilerParams(vmem_limit_bytes=44 * 2**20),
        cost_estimate=pl.CostEstimate(
            flops=10 * 10**9, bytes_accessed=24 * 2**20, transcendentals=0
        ),
    )(place, tiles, *evens, odds, *corners, rounded, own)


def swap(value, axis, offset):
    count = lax.axis_size(axis)
    return lax.ppermute(value, axis, [(i, i ^ offset) for i in range(count)])


def per_device(kernel):
    row_count = lax.axis_size("row")
    col_count = lax.axis_size("col")
    tile_rows = P_SIZE // row_count
    if P_SIZE != col_count * BLOCK or tile_rows % STEP:
        return per_device_general(kernel)
    place = jnp.stack([lax.axis_index("row"), lax.axis_index("col")]).astype(jnp.int32)
    tiles = kernel.reshape(NT, NT, tile_rows * BLOCK)
    corner, top = take_top(tiles[0:2], tile_rows)
    left = take_left(tiles, tile_rows)
    chips = range(2, row_count, 2)
    over_cols = jnp.stack([corner] + [swap(corner, "col", d) for d in range(1, col_count)])
    over_cols, left = lax.optimization_barrier((over_cols, left))
    first = over_cols[:, 0:1]
    near = jnp.stack([first] + [swap(first, "row", d) for d in chips])
    lefts = {0: left}
    for d in range(1, col_count):
        if d != 2:
            lefts[d] = swap(left, "col", d)
    near, other = lax.optimization_barrier((near, over_cols[:, 1:]))
    far = swap(near, "row", 1)
    other_near = [other] + [swap(other, "row", d) for d in chips]
    tile = jax.ShapeDtypeStruct((tile_rows, BLOCK), jnp.float32)
    square = jax.ShapeDtypeStruct((P_SIZE, P_SIZE), jnp.float32)
    first_own, first_side, first_inverse = factor_call(
        first_kernel,
        place,
        (near, far),
        (),
        [tile, jax.ShapeDtypeStruct((P_SIZE, 3 * P_SIZE), jnp.bfloat16), square],
        40 * 10**9,
    )
    others = [lefts[d] for d in sorted(lefts) if d]
    *other_near, top, left, first_side = lax.optimization_barrier(
        (*other_near, top, left, first_side, *others)
    )[: len(other_near) + 3]
    other_near = jnp.stack(other_near)
    other_far = swap(other_near, "row", 1)
    if col_count > 2:
        lefts[2] = swap(left, "col", 2)
    lefts = [lefts[d] for d in range(col_count)]
    evens = [top] + [swap(top, "row", d) for d in chips]
    second_own, second_side, second_inverse, cross, own_cross = factor_call(
        second_kernel,
        place,
        (other_near, other_far),
        (first_side,),
        [
            tile,
            jax.ShapeDtypeStruct((P_SIZE, 3 * P_SIZE), jnp.bfloat16),
            square,
            jax.ShapeDtypeStruct((P_SIZE, P_SIZE), jnp.bfloat16),
            tile,
        ],
        40 * 10**9,
    )
    *evens, second_side, lefts[2 % col_count] = lax.optimization_barrier(
        (*evens, second_side, lefts[2 % col_count])
    )
    odds = swap(jnp.stack(evens), "row", 1)
    rounded, own = solve_rows(place, lefts, first_inverse, second_inverse, cross)
    corners = (first_own, first_side, second_own, second_side, cross, own_cross)
    result = solve_cols(place, tiles, evens, odds, corners, rounded, own, tile_rows)
    return result.reshape(kernel.shape)


def solution(mesh):
    placed = P(None, "row", None, "col", None)
    return jax.shard_map(
        per_device, mesh=mesh, in_specs=(placed,), out_specs=placed, check_vma=False
    )
```
